32 devices in a mesh: groups: 2 (over x), frames: 16 (over z, y, core).
Axes of the slice: x: 2, y: 2, z: 4, core: 2. Of those that a mesh axis runs over, the one named last changes fastest.
Arguments:
- latents: bfloat16 [4, 64, 128, 320], P('groups', 'frames'), parts along dimension 0, may hold values from -6 to 6
- in_weight: bfloat16 [3, 3, 320, 320], replicated, may hold values from -0.109375 to 0.109375
- time_weight: bfloat16 [3, 320, 320], replicated, may hold values from -0.1875 to 0.1875
- mid_weight: bfloat16 [3, 3, 320, 640], replicated, may hold values from -0.109375 to 0.109375
- up_weight: bfloat16 [3, 3, 960, 320], replicated, may hold values from -0.0625 to 0.0625
Outputs:
- mixed: bfloat16 [4, 64, 128, 320], P('groups', 'frames'), parts along dimension 0
The draws below stay inside these ranges and needn't reach their ends.
There are 2 independent parts, one for each index of `groups`. The reference program is written for one: setup_inputs(seed, part) draws one part's arguments, and reference() takes and returns one part's arrays. A program takes and returns all parts, laid end to end along the dimension named above; an argument that names none is the same for every part. Nothing has to cross between parts.
All inputs are finite; a program needn't handle non-finite values.
Results may differ from the reference program's by a relative error of at most 0.0045.
Values may be sent and summed in bfloat16 or wider, within the bound.
No kernel may reach another device: no remote copies, remote signals or barrier semaphores. Data moves between devices by JAX's collectives and lax.ppermute only.
A program may use at most 64 MiB of HBM per device.

```python
import jax
import jax.numpy as jnp
from jax import lax

C = 320
CM = 640
W = 128
FRAMES = 4
CLIPS = 2
ROWS = 64


def steps_of(own_key, extent, cuts, smallest, largest):
    def one(axis_at, parts):
        steps = jax.random.uniform(jax.random.fold_in(jax.random.fold_in(own_key, 6), axis_at), (parts,), jnp.float32, smallest / len(cuts), largest / len(cuts))
        return jnp.repeat(jnp.exp(steps), extent[axis_at] // parts).reshape((-1,) + (1,) * (len(extent) - axis_at - 1))

    level = one(*cuts[0])
    for cut in cuts[1:]:
        level = level * one(*cut)
    return level


def scatter_about(key, dims, width, bound, shards=(), kind=jnp.bfloat16):
    level = steps_of(key, dims, shards, -0.22, 0.18) if shards else 1.0
    entries = jax.random.normal(key, dims, jnp.float32) * width * level
    return jnp.minimum(jnp.maximum(entries, -bound), bound).astype(kind)


def setup_inputs(seed: int = 0, part: int = 0) -> dict:
    key_list = jax.random.split(jax.random.key(seed), 6)
    part_keys = jax.random.split(jax.random.fold_in(key_list[5], part), 6)
    return {
        "latents": scatter_about(part_keys[0], (CLIPS, ROWS, W, C), 1.0, 6.0, ((1, 16),)),
        "in_weight": scatter_about(key_list[1], (3, 3, C, C), (9 * C) ** -0.5, 0.109375),
        "time_weight": scatter_about(key_list[2], (3, C, C), (3 * C) ** -0.5, 0.1875),
        "mid_weight": scatter_about(key_list[3], (3, 3, C, CM), (9 * C) ** -0.5, 0.109375),
        "up_weight": scatter_about(key_list[4], (3, 3, C + CM, C), (9 * (C + CM)) ** -0.5, 0.0625),
    }


def convolve(field, weight):
    return lax.conv_general_dilated(field.astype(jnp.float32), weight.astype(jnp.float32), (1, 1), ((1, 1), (1, 1)), dimension_numbers=("NHWC", "HWIO", "NHWC"), precision=lax.Precision.HIGHEST)


def reference(latents, in_weight, time_weight, mid_weight, up_weight):
    clip_count = latents.shape[0]
    height = latents.shape[1] // FRAMES
    columns = latents.shape[2]
    channels = latents.shape[3]
    offset = height // 2
    ordered = jnp.roll(latents, offset, axis=1)
    frames_all = ordered.reshape(clip_count * FRAMES, height, columns, channels)
    first = jax.nn.silu(convolve(frames_all, in_weight)).astype(jnp.bfloat16)
    series = first.reshape(clip_count, FRAMES, height * columns, channels).astype(jnp.float32)
    padded = jnp.pad(series, ((0, 0), (1, 1), (0, 0), (0, 0)))
    stacked = jnp.concatenate([padded[:, :-2], series, padded[:, 2:]], axis=-1)
    merged = time_weight.astype(jnp.float32).reshape(3 * channels, channels)
    temporal = jnp.einsum("abpk,kc->abpc", stacked, merged, precision=lax.Precision.HIGHEST)
    skip = (series + temporal).astype(jnp.bfloat16).reshape(clip_count * FRAMES, height, columns, channels)
    pooled = skip.astype(jnp.float32).reshape(clip_count * FRAMES, height // 2, 2, columns // 2, 2, channels).mean(axis=(2, 4)).astype(jnp.bfloat16)
    middle = jax.nn.silu(convolve(pooled, mid_weight)).astype(jnp.bfloat16)
    upper = jnp.repeat(jnp.repeat(middle, 2, axis=1), 2, axis=2)
    joined = jnp.concatenate([skip, upper], axis=-1)
    mixed = (frames_all.astype(jnp.float32) + convolve(joined, up_weight)).astype(jnp.bfloat16)
    return jnp.roll(mixed.reshape(latents.shape), -offset, axis=1)
```

```python
import jax
import jax.numpy as jnp
from jax import lax
from jax.experimental import pallas as pl
from jax.experimental.pallas import tpu as pltpu
from jax.sharding import PartitionSpec as P


FRAMES = 4
BF16 = jnp.bfloat16
F32 = jnp.float32
LIMIT = 32 * 1024 * 1024


def one_hot(source):
    width = source.shape[1]
    rows = lax.broadcasted_iota(jnp.int32, (source_rows(source), width), 0)
    return (rows == source).astype(BF16)


def source_rows(source):
    return source.shape[1] if source.shape[0] == 1 else source.shape[0]


def lanes(width):
    return lax.broadcasted_iota(jnp.int32, (1, width), 1)


def picks(sources):
    return jnp.concatenate([one_hot(source) for source in sources], axis=1)


def sort_picks(width):
    lane = lanes(width)
    column = jnp.where(lane < width // 2, 2 * lane, 2 * lane - width + 1)
    return picks([column - 1, column, column + 1])


def sorted_shift_picks(width):
    half = width // 2
    lane = lanes(width)
    left = jnp.where(lane < half, jnp.where(lane == 0, -1, lane + half - 1), lane - half)
    right = jnp.where(lane < half, lane + half, jnp.where(lane == width - 1, -1, lane - half + 1))
    return picks([left, right])


def pair_shift_picks(width):
    half = width // 2
    lane = lanes(width)
    left = jnp.where(lane % half == 0, -1, lane - 1)
    right = jnp.where(lane % half == half - 1, -1, lane + 1)
    return picks([left, right])


def unsort_pick(width):
    lane = lanes(width)
    return one_hot(jnp.where(lane % 2 == 0, lane // 2, width // 2 + lane // 2))


def dot(left, right):
    return jnp.dot(left, right, preferred_element_type=F32)


def silu(value):
    return value / (1.0 + jnp.exp(-value))


def fill_sorted(field, place, latent, row, pick, clips):
    channels, width = latent(0).shape
    for clip in range(clips):
        moved = dot(latent(clip), pick).astype(BF16)
        for tap in range(3):
            start = (row * 3 + tap) * channels
            field[start : start + channels, clip * width : (clip + 1) * width] = moved[
                :, tap * width : (tap + 1) * width
            ]


def inner_kernel(latent_ref, weight_ref, first_ref, turned_ref, field_ref):
    clips, rows, channels, width = latent_ref.shape
    pick = sort_picks(width)
    for row in range(rows):
        fill_sorted(field_ref, None, lambda clip: latent_ref[clip, row], row, pick, clips)
    turned_ref[...] = weight_ref[...].T
    depth = 3 * channels
    for row in range(rows - 2):
        total = dot(turned_ref[...], field_ref[row * depth : (row + 3) * depth, :])
        first_ref[row] = silu(total).astype(BF16)


def outer_kernel(low_ref, high_ref, turned_ref, field_ref, first_ref, rim_ref):
    clips, _, channels, width = low_ref.shape
    rows = field_ref.shape[0] // (3 * channels)
    depth = 3 * channels
    pick = sort_picks(width)
    fill_sorted(rim_ref, None, lambda clip: low_ref[clip, 0], 0, pick, clips)
    fill_sorted(rim_ref, None, lambda clip: high_ref[clip, 0], 1, pick, clips)
    top = dot(turned_ref[:, :depth], rim_ref[:depth, :])
    top += dot(turned_ref[:, depth:], field_ref[: 2 * depth, :])
    first_ref[0] = silu(top).astype(BF16)
    bottom = dot(turned_ref[:, : 2 * depth], field_ref[(rows - 2) * depth :, :])
    bottom += dot(turned_ref[:, 2 * depth :], rim_ref[depth:, :])
    first_ref[1] = silu(bottom).astype(BF16)


def weights_kernel(time_ref, mid_ref, up_ref, time_out, mid_out, skip_out, phase_out):
    channels = up_ref.shape[2]
    time_out[...] = time_ref[...].T
    mid_out[...] = mid_ref[...].T
    skip_out[...] = jnp.concatenate(
        [up_ref[dr, dc, :, :channels] for dr in range(3) for dc in range(3)], axis=1
    )
    inner = up_ref.shape[3] - channels
    taps = [[up_ref[dr, dc, :, channels:].astype(F32) for dc in range(3)] for dr in range(3)]
    groups = ((lambda t: t[0], lambda t: t[1] + t[2]), (lambda t: t[0] + t[1], lambda t: t[2]))
    for row_phase in range(2):
        for row_tap in range(2):
            merged = [groups[row_phase][row_tap]([taps[dr][dc] for dr in range(3)]) for dc in range(3)]
            for column_phase in range(2):
                for column_tap in range(2):
                    value = groups[column_phase][column_tap](merged)
                    start = (2 * row_tap + column_tap) * inner
                    phase_out[2 * row_phase + column_phase, :, start : start + inner] = value.astype(
                        BF16
                    )


def skip_kernel(
    inner_ref, outer_ref, inner_before, outer_before, inner_after, outer_after, weight_ref,
    skip_ref, previous_ref, next_ref,
):
    rows = skip_ref.shape[0]
    wide = skip_ref.shape[2]
    half = wide // 4
    lane = lax.broadcasted_iota(jnp.int32, (1, wide), 1)
    lower = (lane // half) % 2 == 0
    sums = []
    for row in range(rows):
        edge = row in (0, rows - 1)
        at = (0 if row == 0 else 1) if edge else row - 1
        before, own, after = (
            (outer_before, outer_ref, outer_after) if edge else (inner_before, inner_ref, inner_after)
        )
        centre = own[at]
        stacked = jnp.concatenate([before[at], centre, after[at]], axis=0)
        skip = (centre.astype(F32) + dot(weight_ref[...], stacked)).astype(BF16)
        skip_ref[row] = skip
        sums.append(skip.astype(F32))
        if row == 0:
            previous_ref[0] = skip
        if row == rows - 1:
            next_ref[0] = skip
    parts = []
    for pooled_row in range(rows // 2):
        both = sums[2 * pooled_row] + sums[2 * pooled_row + 1]
        swapped = jnp.where(
            lower, jnp.roll(both, -half, axis=1), jnp.roll(both, half, axis=1)
        )
        parts.append((both + swapped) * 0.25)
    pooled = jnp.where(lower, parts[0], parts[1]).astype(BF16)
    previous_ref[1] = pooled
    next_ref[1] = pooled


def half_swap(value, lower, half):
    return jnp.where(lower, jnp.roll(value, -half, axis=1), jnp.roll(value, half, axis=1))


def joined_pair(left, right, lower, half):
    mixed = jnp.where(lower, right.astype(F32), left.astype(F32))
    return half_swap(mixed, lower, half).astype(BF16)


def last_kernel(
    flag_ref, skip_ref, own_ref, low_ref, high_ref, mid_ref, skip_weight, phase_weight, latent_ref,
    out_ref, field, pooled_field, middle_field,
):
    rows, channels, wide = skip_ref.shape
    clips = latent_ref.shape[0]
    width = wide // clips
    half = width // 2
    inner = mid_ref.shape[0]
    depth = 3 * channels
    lane = lax.broadcasted_iota(jnp.int32, (1, wide), 1)
    lower = (lane // half) % 2 == 0

    pair_pick = pair_shift_picks(width)
    low_pair, own_pair, high_pair = low_ref[1], own_ref[1], high_ref[1]
    pairs = [
        low_pair,
        joined_pair(low_pair, own_pair, lower, half),
        own_pair,
        joined_pair(own_pair, high_pair, lower, half),
        high_pair,
    ]

    def store_shifted(target, base, value, size, pick):
        target[base + size : base + 2 * size, :] = value
        for clip in range(clips):
            span = slice(clip * width, (clip + 1) * width)
            moved = dot(value[:, span], pick).astype(BF16)
            target[base : base + size, span] = moved[:, :width]
            target[base + 2 * size : base + 3 * size, span] = moved[:, width:]

    for at, pair in enumerate(pairs):
        store_shifted(pooled_field, at * depth, pair, channels, pair_pick)
    keep_low = jnp.logical_or(flag_ref[0] == 0, jnp.logical_not(lower))
    keep_high = jnp.logical_or(flag_ref[1] == 0, lower)
    above = silu(dot(mid_ref[...], pooled_field[: 3 * depth, :]))
    above = jnp.where(keep_low, above, 0.0)
    below = silu(dot(mid_ref[...], pooled_field[2 * depth :, :]))
    below = jnp.where(keep_high, below, 0.0)
    centre = half_swap(jnp.where(lower, below, above), lower, half)
    for at, value in enumerate((above, centre, below)):
        store_shifted(middle_field, at * 3 * inner, value.astype(BF16), inner, pair_pick)

    shift_pick = sorted_shift_picks(width)
    for row in range(rows + 2):
        value = low_ref[0] if row == 0 else high_ref[0] if row == rows + 1 else skip_ref[row - 1]
        store_shifted(field, row * depth, value, channels, shift_pick)

    sort_pick = sort_picks(width)[:, width : 2 * width]
    unsort = unsort_pick(width)
    for row_phase in range(2):
        phases = []
        for column_phase in range(2):
            weight = phase_weight[2 * row_phase + column_phase]
            total = None
            for tap in range(2):
                start = (row_phase + tap) * 3 * inner + column_phase * inner
                part = dot(
                    weight[:, tap * 2 * inner : (tap + 1) * 2 * inner],
                    middle_field[start : start + 2 * inner, :],
                )
                total = part if total is None else total + part
            phases.append(total)
        uppers = (
            jnp.where(lower, phases[0], jnp.roll(phases[1], half, axis=1)),
            jnp.where(lower, jnp.roll(phases[0], -half, axis=1), phases[1]),
        )
        for at in range(rows // 2):
            row = 2 * at + row_phase
            total = uppers[at] + dot(skip_weight[...], field[row * depth : (row + 3) * depth, :])
            for clip in range(clips):
                span = slice(clip * width, (clip + 1) * width)
                latent = dot(latent_ref[clip, row], sort_pick)
                mixed = (latent + total[:, span]).astype(BF16)
                out_ref[clip, row] = dot(mixed, unsort).astype(BF16)


def call(kernel, name, outputs, scratch=(), flops=0, kept=True, inputs=None):
    shapes = [
        pltpu.VMEM(shape, dtype) if kept else jax.ShapeDtypeStruct(shape, dtype)
        for shape, dtype in outputs
    ]
    specs = {} if inputs is None else {"in_specs": inputs}
    return pl.pallas_call(
        kernel,
        out_shape=shapes,
        scratch_shapes=list(scratch),
        compiler_params=pltpu.CompilerParams(vmem_limit_bytes=LIMIT),
        cost_estimate=pl.CostEstimate(flops=flops, bytes_accessed=1 << 20, transcendentals=0),
        name=name,
        **specs,
    )


def chain(axis, step, keep):
    count = lax.axis_size(axis)
    return [
        (source, (source + step) % count) for source in range(count) if keep(source)
    ]


def body(latents, in_weight, time_weight, mid_weight, up_weight):
    device_count = lax.axis_size("frames")
    bands = device_count // FRAMES
    offset = bands // 2
    band_of = lambda index: (index + offset) % bands
    frame_of = lambda index: (index + offset) // bands % FRAMES
    band = band_of(lax.axis_index("frames"))
    down = chain("frames", 1, lambda i: band_of(i) != bands - 1)
    up = chain("frames", -1, lambda i: band_of(i) != 0)
    later = chain("frames", bands, lambda i: frame_of(i) != FRAMES - 1)
    earlier = chain("frames", -bands, lambda i: frame_of(i) != 0)

    clips, rows, width, channels = latents.shape
    inner = mid_weight.shape[3]
    wide = clips * width
    depth = 3 * channels
    turned = jnp.swapaxes(latents, 2, 3)
    low = lax.ppermute(turned[:, rows - 1 :], "frames", down)
    high = lax.ppermute(turned[:, :1], "frames", up)

    first_inner, in_turned, field = call(
        inner_kernel,
        "first_inner",
        [
            ((rows - 2, channels, wide), BF16),
            ((channels, 3 * depth), BF16),
            ((rows * depth, wide), BF16),
        ],
        flops=2 * (rows - 2) * wide * channels * 3 * depth,
    )(turned, in_weight.reshape(3 * depth, channels))
    inner_before = lax.ppermute(first_inner, "frames", later)
    inner_after = lax.ppermute(first_inner, "frames", earlier)

    (first_outer,) = call(
        outer_kernel,
        "first_outer",
        [((2, channels, wide), BF16)],
        [pltpu.VMEM((2 * depth, wide), BF16)],
        flops=2 * 2 * wide * channels * 3 * depth,
    )(low, high, in_turned, field)
    outer_before = lax.ppermute(first_outer, "frames", later)
    outer_after = lax.ppermute(first_outer, "frames", earlier)

    time_rows, mid_rows, up_rows, first_outer = lax.optimization_barrier(
        (
            time_weight.reshape(depth, channels),
            mid_weight.reshape(3 * depth, inner),
            jnp.swapaxes(up_weight, 2, 3),
            first_outer,
        )
    )
    time_turned, mid_turned, skip_weight, phase_weight = call(
        weights_kernel,
        "weights",
        [
            ((channels, depth), BF16),
            ((inner, 3 * depth), BF16),
            ((channels, 3 * depth), BF16),
            ((4, channels, 4 * inner), BF16),
        ],
        flops=10**10,
    )(time_rows, mid_rows, up_rows)

    skip, to_previous, to_next = call(
        skip_kernel,
        "skip",
        [
            ((rows, channels, wide), BF16),
            ((2, channels, wide), BF16),
            ((2, channels, wide), BF16),
        ],
        flops=2 * rows * wide * depth * channels,
    )(first_inner, first_outer, inner_before, outer_before, inner_after, outer_after, time_turned)
    from_previous = lax.ppermute(to_next, "frames", down)
    from_next = lax.ppermute(to_previous, "frames", up)

    flags = jnp.stack([band == 0, band == bands - 1]).astype(jnp.int32)
    whole = pl.BlockSpec(memory_space=pltpu.VMEM)
    (mixed,) = call(
        last_kernel,
        "last",
        [(turned.shape, BF16)],
        [
            pltpu.VMEM(((rows + 2) * depth, wide), BF16),
            pltpu.VMEM((5 * depth, wide), BF16),
            pltpu.VMEM((9 * inner, wide), BF16),
        ],
        flops=2 * rows * wide * channels * (3 * depth + 4 * inner),
        kept=False,
        inputs=[pl.BlockSpec(memory_space=pltpu.SMEM)] + [whole] * 8,
    )(
        flags, skip, to_previous, from_previous, from_next, mid_turned, skip_weight, phase_weight,
        turned,
    )
    return jnp.swapaxes(mixed, 2, 3)


def solution(mesh):
    in_specs = (P("groups", "frames", None, None), P(), P(), P(), P())
    out_specs = P("groups", "frames", None, None)
    return jax.shard_map(body, mesh=mesh, in_specs=in_specs, out_specs=out_specs, check_vma=False)
```

```python
import jax
import jax.numpy as jnp
from jax import lax
from jax.experimental import pallas as pl
from jax.experimental.pallas import tpu as pltpu
from jax.sharding import PartitionSpec as P


FRAMES = 4
BF16 = jnp.bfloat16
F32 = jnp.float32
MIB = 1024 * 1024


def dot(left, right):
    return jnp.dot(left, right, preferred_element_type=F32)


def silu(value):
    return value / (1.0 + jnp.exp(-value))


def sort_pick(width, clips):
    wide, half = width * clips, width // 2
    source = lax.broadcasted_iota(jnp.int32, (wide, wide), 0)
    lane = lax.broadcasted_iota(jnp.int32, (wide, wide), 1)
    parity, clip, j = lane // (wide // 2), lane // half % clips, lane % half
    return (source == clip * width + 2 * j + parity).astype(BF16)


def unsort_pick(width, clips):
    wide, half = width * clips, width // 2
    source = lax.broadcasted_iota(jnp.int32, (wide, wide), 0)
    lane = lax.broadcasted_iota(jnp.int32, (wide, wide), 1)
    clip, column = lane // width, lane % width
    return (source == column % 2 * (wide // 2) + clip * half + column // 2).astype(BF16)


def from_left(value, half):
    lane = lax.broadcasted_iota(jnp.int32, (1, value.shape[1]), 1)
    return jnp.where(lane % half == 0, 0.0, pltpu.roll(value, 1, 1))


def from_right(value, half):
    width = value.shape[1]
    lane = lax.broadcasted_iota(jnp.int32, (1, width), 1)
    return jnp.where(lane % half == half - 1, 0.0, pltpu.roll(value, width - 1, 1))


def store_taps(field, base, even, odd, half):
    channels, lanes = even.shape
    e, o = even.astype(BF16), odd.astype(BF16)
    blocks = ((from_left(odd, half).astype(BF16), e), (e, o), (o, from_right(even, half).astype(BF16)))
    for tap, pair in enumerate(blocks):
        rows = slice(base + tap * channels, base + (tap + 1) * channels)
        field[rows, :lanes] = pair[0]
        field[rows, lanes:] = pair[1]


def store_row_taps(field, base, lane_base, value, half):
    channels, lanes = value.shape
    blocks = (from_left(value, half).astype(BF16), value.astype(BF16), from_right(value, half).astype(BF16))
    for tap, block in enumerate(blocks):
        field[base + tap * channels : base + (tap + 1) * channels, lane_base : lane_base + lanes] = block


def first_inner_kernel(
    latent_hbm, weight_hbm, first_ref, turned_ref, field_ref, low_ref, high_ref,
    latent, weight, latent_sem, weight_sem,
):
    clips, rows, channels, width = latent.shape
    taps = weight.shape[0]
    wide = clips * width
    get_latent = pltpu.make_async_copy(latent_hbm, latent, latent_sem)
    get_latent.start()
    cuts = list(range(0, taps, 1024)) + [taps]
    gets = [
        pltpu.make_async_copy(weight_hbm.at[a:b], weight.at[a:b], weight_sem.at[n])
        for n, (a, b) in enumerate(zip(cuts, cuts[1:]))
    ]
    for get in gets:
        get.start()
    pick = sort_pick(width, clips)
    get_latent.wait()
    low_ref[...] = latent[:, rows - 1]
    high_ref[...] = latent[:, 0]
    depth = 3 * channels
    for row in range(rows):
        natural = jnp.concatenate([latent[clip, row] for clip in range(clips)], axis=1)
        value = dot(natural, pick)
        store_taps(field_ref, row * depth, value[:, : wide // 2], value[:, wide // 2 :], width // 2)
    for get, a, b in zip(gets, cuts, cuts[1:]):
        get.wait()
        turned_ref[:, a:b] = weight[a:b, :].T
    for row in range(rows - 2):
        total = dot(turned_ref[...], field_ref[row * depth : (row + 3) * depth, :])
        first_ref[row] = silu(total).astype(BF16)


def first_outer_kernel(low_ref, high_ref, turned_ref, field_ref, first_ref, rim):
    clips, channels, width = low_ref.shape
    depth = 3 * channels
    rows = field_ref.shape[0] // depth
    wide = clips * width
    pick = sort_pick(width, clips)
    for at, ref in enumerate((low_ref, high_ref)):
        natural = jnp.concatenate([ref[clip] for clip in range(clips)], axis=1)
        value = dot(natural, pick)
        store_taps(rim, at * depth, value[:, : wide // 2], value[:, wide // 2 :], width // 2)
    top = dot(turned_ref[:, depth:], field_ref[: 2 * depth, :])
    top += dot(turned_ref[:, :depth], rim[:depth, :])
    first_ref[0] = silu(top).astype(BF16)
    bottom = dot(turned_ref[:, : 2 * depth], field_ref[(rows - 2) * depth :, :])
    bottom += dot(turned_ref[:, 2 * depth :], rim[depth:, :])
    first_ref[1] = silu(bottom).astype(BF16)


def weights_kernel(
    time_hbm, mid_hbm, up_hbm, time_out, mid_out, skip_out, phase_out,
    time_rows, mid_rows, up_rows, sems,
):
    taps, inner = mid_rows.shape
    channels = up_rows.shape[2]
    cuts = list(range(0, taps, 1024)) + [taps]
    pieces = [(time_hbm, time_rows)]
    pieces += [(mid_hbm.at[a:b], mid_rows.at[a:b]) for a, b in zip(cuts, cuts[1:])]
    pieces += [(up_hbm, up_rows)]
    gets = [
        pltpu.make_async_copy(source, target, sems.at[n])
        for n, (source, target) in enumerate(pieces)
    ]
    for get in gets:
        get.start()
    gets[0].wait()
    time_out[...] = time_rows[...].T
    for get, a, b in zip(gets[1:-1], cuts, cuts[1:]):
        get.wait()
        mid_out[:, a:b] = mid_rows[a:b, :].T
    gets[-1].wait()
    skip_out[...] = jnp.concatenate(
        [up_rows[dr, dc, :, :channels] for dr in range(3) for dc in range(3)], axis=1
    )
    taps = [[up_rows[dr, dc, :, channels:].astype(F32) for dc in range(3)] for dr in range(3)]
    groups = ((lambda t: t[0], lambda t: t[1] + t[2]), (lambda t: t[0] + t[1], lambda t: t[2]))
    for row_phase in range(2):
        for row_tap in range(2):
            merged = [groups[row_phase][row_tap]([taps[dr][dc] for dr in range(3)]) for dc in range(3)]
            for column_phase in range(2):
                for column_tap in range(2):
                    value = groups[column_phase][column_tap](merged)
                    start = (2 * row_tap + column_tap) * inner
                    phase_out[2 * row_phase + column_phase, :, start : start + inner] = value.astype(
                        BF16
                    )


def skip_kernel(
    flag_ref, inner_ref, outer_ref, inner_before, outer_before, inner_after, outer_after, relayed,
    weight_ref, skip_ref, previous_ref, next_ref,
):
    rows, _, wide = skip_ref.shape
    lanes = wide // 2
    for pooled_row in range(rows // 2):
        sums = None
        for row in (2 * pooled_row, 2 * pooled_row + 1):
            edge = row in (0, rows - 1)
            at = (0 if row == 0 else 1) if edge else row - 1
            before, own, after = (
                (outer_before, outer_ref, outer_after)
                if edge
                else (inner_before, inner_ref, inner_after)
            )
            centre, early, late = own[at], before[at], after[at]
            if not edge:
                early = jnp.where(flag_ref[2] != 0, relayed[at], early)
                late = jnp.where(flag_ref[3] != 0, relayed[at], late)
            stacked = jnp.concatenate([early, centre, late], axis=0)
            skip = (centre.astype(F32) + dot(weight_ref[...], stacked)).astype(BF16)
            skip_ref[row] = skip
            if row == 0:
                previous_ref[0] = skip
            if row == rows - 1:
                next_ref[0] = skip
            skip = skip.astype(F32)
            sums = skip if sums is None else sums + skip
        pooled = ((sums[:, :lanes] + sums[:, lanes:]) * 0.25).astype(BF16)
        span = slice(pooled_row * lanes, (pooled_row + 1) * lanes)
        previous_ref[1, :, span] = pooled
        next_ref[1, :, span] = pooled


def own_kernel(skip_ref, pair_ref, mid_ref, skip_weight, mixed_ref, middle_ref, field, pooled, *, half):
    rows, channels, wide = skip_ref.shape
    lanes = wide // 2
    depth = 3 * channels
    for at in range(2):
        row = pair_ref[1, :, at * lanes : (at + 1) * lanes].astype(F32)
        store_row_taps(pooled, 0, at * lanes, row, half)
    for row in range(rows):
        value = skip_ref[row].astype(F32)
        store_taps(field, row * depth, value[:, :lanes], value[:, lanes:], half)
    parts = [dot(mid_ref[:, dr * depth : (dr + 1) * depth], pooled[...]) for dr in range(3)]
    middle_ref[:, :lanes] = parts[2][:, :lanes]
    middle_ref[:, lanes : 2 * lanes] = parts[2][:, lanes:] + parts[1][:, :lanes]
    middle_ref[:, 2 * lanes : 3 * lanes] = parts[1][:, lanes:] + parts[0][:, :lanes]
    middle_ref[:, 3 * lanes :] = parts[0][:, lanes:]
    for row in range(rows):
        first, last = max(row - 1, 0), min(row + 2, rows)
        mixed_ref[row] = dot(
            skip_weight[:, (first - row + 1) * depth : (last - row + 1) * depth],
            field[first * depth : last * depth, :],
        )


def last_kernel(
    flag_ref, mixed_ref, middle_ref, low_ref, high_ref, mid_ref, skip_weight, phase_weight, field_ref,
    out_ref, low_field, high_field, cross_field, rims, middle_field,
):
    rows, channels, wide = mixed_ref.shape
    clips, _, _, width = out_ref.shape
    half, lanes = width // 2, wide // 2
    inner = mid_ref.shape[0]
    depth = 3 * channels

    for target, ref, inward in ((low_field, low_ref, 1), (high_field, high_ref, 0)):
        for at in range(2):
            row = ref[1, :, at * lanes : (at + 1) * lanes].astype(F32)
            store_row_taps(target, 0, at * lanes, row, half)
        cross_field[:, (1 - inward) * lanes : (2 - inward) * lanes] = target[
            :, inward * lanes : (inward + 1) * lanes
        ]
    above = dot(mid_ref[:, :depth], low_field[...])
    cross = dot(mid_ref[:, depth : 2 * depth], cross_field[...])
    below = dot(mid_ref[:, 2 * depth :], high_field[...])
    middles = [
        middle_ref[:, :lanes] + above[:, :lanes] + cross[:, :lanes],
        middle_ref[:, lanes : 2 * lanes] + above[:, lanes:],
        middle_ref[:, 2 * lanes : 3 * lanes] + below[:, :lanes],
        middle_ref[:, 3 * lanes :] + below[:, lanes:] + cross[:, lanes:],
    ]
    kept = (flag_ref[0] == 0, None, None, flag_ref[1] == 0)
    for at, (value, keep) in enumerate(zip(middles, kept)):
        value = silu(value)
        if keep is not None:
            value = jnp.where(keep, value, 0.0)
        store_row_taps(middle_field, at * 3 * inner, 0, value.astype(BF16).astype(F32), half)

    for at, ref in enumerate((low_ref, high_ref)):
        value = ref[0].astype(F32)
        store_taps(rims, at * depth, value[:, :lanes], value[:, lanes:], half)
    from_rim = {
        0: dot(skip_weight[:, :depth], rims[:depth, :]),
        rows - 1: dot(skip_weight[:, 2 * depth :], rims[depth:, :]),
    }
    unsort = unsort_pick(width, clips)
    block = 3 * inner
    for row_phase in range(2):
        phases = []
        for column_phase in range(2):
            total = None
            for tap in range(2):
                sides = [
                    middle_field[
                        (row_phase + tap + at) * block
                        + column_phase * inner : (row_phase + tap + at) * block
                        + (column_phase + 2) * inner,
                        :,
                    ]
                    for at in range(rows // 2)
                ]
                part = dot(
                    phase_weight[
                        2 * row_phase + column_phase, :, tap * 2 * inner : (tap + 1) * 2 * inner
                    ],
                    jnp.concatenate(sides, axis=1),
                )
                total = part if total is None else total + part
            phases.append(total)
        for at in range(rows // 2):
            row = 2 * at + row_phase
            latent = field_ref[row * depth + channels : row * depth + 2 * channels, :].astype(F32)
            upper = jnp.concatenate([phase[:, at * lanes : (at + 1) * lanes] for phase in phases], axis=1)
            total = latent + mixed_ref[row] + upper
            if row in from_rim:
                total += from_rim[row]
            natural = dot(total.astype(BF16), unsort).astype(BF16)
            for clip in range(clips):
                out_ref[clip, row] = natural[:, clip * width : (clip + 1) * width]


def call(kernel, name, outputs, limit, scratch=(), flops=0, kept=True, inputs=None):
    shapes = [
        pltpu.VMEM(shape, dtype) if kept else jax.ShapeDtypeStruct(shape, dtype)
        for shape, dtype in outputs
    ]
    specs = {} if inputs is None else {"in_specs": inputs}
    return pl.pallas_call(
        kernel,
        out_shape=shapes,
        scratch_shapes=list(scratch),
        compiler_params=pltpu.CompilerParams(vmem_limit_bytes=limit * MIB),
        cost_estimate=pl.CostEstimate(flops=flops, bytes_accessed=1 << 20, transcendentals=0),
        name=name,
        **specs,
    )


def in_hbm(value):
    return pltpu.with_memory_space_constraint(value, pltpu.HBM)


def in_vmem(*values):
    return [pltpu.with_memory_space_constraint(value, pltpu.VMEM) for value in values]


def body(latents, in_weight, time_weight, mid_weight, up_weight):
    device_count = lax.axis_size("frames")
    bands = device_count // FRAMES
    offset = bands // 2
    band_of = lambda index: (index + offset) % bands
    frame_of = lambda index: (index + offset) // bands % FRAMES
    chain = lambda step, keep: [
        (i, (i + step) % device_count) for i in range(device_count) if keep(i)
    ]
    band = band_of(lax.axis_index("frames"))
    down = chain(1, lambda i: band_of(i) != bands - 1)
    up = chain(-1, lambda i: band_of(i) != 0)
    later = chain(bands, lambda i: frame_of(i) != FRAMES - 1)
    earlier = chain(-bands, lambda i: frame_of(i) != 0)
    near = lambda pairs: [(i, j) for i, j in pairs if abs(i - j) == bands]
    far = [(i, j) for i, j in later + earlier if abs(i - j) != bands]
    hops = [(i, i - offset) for i, _ in far]
    relays = [(i - offset, j) for i, j in far]
    index = lax.axis_index("frames")
    flags = jnp.stack(
        [
            band == 0,
            band == bands - 1,
            jnp.logical_and(index >= offset, index < bands),
            index >= device_count - offset,
        ]
    ).astype(jnp.int32)

    clips, rows, width, channels = latents.shape
    inner = mid_weight.shape[3]
    wide = clips * width
    depth = 3 * channels
    anywhere = pl.BlockSpec(memory_space=pl.ANY)
    whole = pl.BlockSpec(memory_space=pltpu.VMEM)
    scalars = pl.BlockSpec(memory_space=pltpu.SMEM)
    turned = jnp.swapaxes(latents, 2, 3)

    first_inner, in_turned, field, low_rim, high_rim = call(
        first_inner_kernel,
        "first_inner",
        [
            ((rows - 2, channels, wide), BF16),
            ((channels, 3 * depth), BF16),
            ((rows * depth, wide), BF16),
            ((clips, channels, width), BF16),
            ((clips, channels, width), BF16),
        ],
        12,
        [
            pltpu.VMEM(turned.shape, BF16),
            pltpu.VMEM((3 * depth, channels), BF16),
            pltpu.SemaphoreType.DMA(()),
            pltpu.SemaphoreType.DMA((-(-3 * depth // 1024),)),
        ],
        flops=2 * (rows - 2) * wide * channels * 3 * depth,
        inputs=[anywhere, anywhere],
    )(in_hbm(turned), in_hbm(in_weight.reshape(3 * depth, channels)))
    hopped = lax.ppermute(first_inner, "frames", hops)
    inner_before = lax.ppermute(first_inner, "frames", near(later))
    inner_after = lax.ppermute(first_inner, "frames", near(earlier))
    relayed = lax.ppermute(hopped, "frames", relays)
    low = lax.ppermute(low_rim, "frames", down)
    high = lax.ppermute(high_rim, "frames", up)

    (first_outer,) = call(
        first_outer_kernel,
        "first_outer",
        [((2, channels, wide), BF16)],
        8,
        [pltpu.VMEM((2 * depth, wide), BF16)],
        flops=2 * 2 * wide * channels * 3 * depth,
        inputs=[whole] * 4,
    )(*in_vmem(low, high, in_turned, field))
    outer_before = lax.ppermute(first_outer, "frames", later)
    outer_after = lax.ppermute(first_outer, "frames", earlier)

    time_rows, mid_rows, up_rows, first_outer, _ = lax.optimization_barrier(
        (
            time_weight.reshape(depth, channels),
            mid_weight.reshape(3 * depth, inner),
            jnp.swapaxes(up_weight, 2, 3),
            first_outer,
            hopped,
        )
    )
    time_turned, mid_turned, skip_weight, phase_weight = call(
        weights_kernel,
        "weights",
        [
            ((channels, depth), BF16),
            ((inner, 3 * depth), BF16),
            ((channels, 3 * depth), BF16),
            ((4, channels, 4 * inner), BF16),
        ],
        20,
        [
            pltpu.VMEM(time_rows.shape, BF16),
            pltpu.VMEM(mid_rows.shape, BF16),
            pltpu.VMEM(up_rows.shape, BF16),
            pltpu.SemaphoreType.DMA((2 + -(-3 * depth // 1024),)),
        ],
        flops=2 * 10**9,
        inputs=[anywhere] * 3,
    )(in_hbm(time_rows), in_hbm(mid_rows), in_hbm(up_rows))

    skip, to_previous, to_next = call(
        skip_kernel,
        "skip",
        [
            ((rows, channels, wide), BF16),
            ((2, channels, wide), BF16),
            ((2, channels, wide), BF16),
        ],
        8,
        flops=2 * rows * wide * depth * channels,
        inputs=[scalars] + [whole] * 8,
    )(
        flags,
        *in_vmem(
            first_inner,
            first_outer,
            inner_before,
            outer_before,
            inner_after,
            outer_after,
            relayed,
            time_turned,
        ),
    )
    from_previous = lax.ppermute(to_next, "frames", down)
    from_next = lax.ppermute(to_previous, "frames", up)

    mixed, middle = call(
        lambda *refs: own_kernel(*refs, half=width // 2),
        "own_rows",
        [((rows, channels, wide), F32), ((inner, 2 * wide), F32)],
        16,
        [pltpu.VMEM((rows * depth, wide), BF16), pltpu.VMEM((depth, wide), BF16)],
        flops=2 * wide * depth * (3 * inner + (3 * rows - 2) * channels),
        inputs=[whole] * 4,
    )(*in_vmem(skip, to_previous, mid_turned, skip_weight))

    (out,) = call(
        last_kernel,
        "last",
        [(turned.shape, BF16)],
        20,
        [
            pltpu.VMEM((depth, wide), BF16),
            pltpu.VMEM((depth, wide), BF16),
            pltpu.VMEM((depth, wide), BF16),
            pltpu.VMEM((2 * depth, wide), BF16),
            pltpu.VMEM((4 * 3 * inner, wide // 2), BF16),
        ],
        flops=2 * wide * (3 * depth * inner + 2 * depth * channels + rows * 4 * inner * channels),
        kept=False,
        inputs=[scalars] + [whole] * 8,
    )(
        flags,
        *in_vmem(
            mixed, middle, from_previous, from_next, mid_turned, skip_weight, phase_weight, field
        ),
    )
    return jnp.swapaxes(out, 2, 3)


def solution(mesh):
    in_specs = (P("groups", "frames", None, None), P(), P(), P(), P())
    out_specs = P("groups", "frames", None, None)
    return jax.shard_map(body, mesh=mesh, in_specs=in_specs, out_specs=out_specs, check_vma=False)
```

```python
import jax
import jax.numpy as jnp
from jax import lax
from jax.experimental import pallas as pl
from jax.experimental.pallas import tpu as pltpu
from jax.sharding import PartitionSpec as P


FRAMES = 4
BF16 = jnp.bfloat16
F32 = jnp.float32
MIB = 1024 * 1024


def dot(left, right):
    return jnp.dot(left, right, preferred_element_type=F32)


def silu(value):
    return value / (1.0 + jnp.exp(-value))


def sort_pick(width, clips):
    wide, half = width * clips, width // 2
    source = lax.broadcasted_iota(jnp.int32, (wide, wide), 0)
    lane = lax.broadcasted_iota(jnp.int32, (wide, wide), 1)
    parity, clip, j = lane // (wide // 2), lane // half % clips, lane % half
    return (source == clip * width + 2 * j + parity).astype(BF16)


def unsort_pick(width, clips):
    wide, half = width * clips, width // 2
    source = lax.broadcasted_iota(jnp.int32, (wide, wide), 0)
    lane = lax.broadcasted_iota(jnp.int32, (wide, wide), 1)
    clip, column = lane // width, lane % width
    return (source == column % 2 * (wide // 2) + clip * half + column // 2).astype(BF16)


def from_left(value, half):
    lane = lax.broadcasted_iota(jnp.int32, (1, value.shape[1]), 1)
    return jnp.where(lane % half == 0, 0.0, pltpu.roll(value, 1, 1))


def from_right(value, half):
    width = value.shape[1]
    lane = lax.broadcasted_iota(jnp.int32, (1, width), 1)
    return jnp.where(lane % half == half - 1, 0.0, pltpu.roll(value, width - 1, 1))


def store_taps(field, base, even, odd, half):
    channels, lanes = even.shape
    e, o = even.astype(BF16), odd.astype(BF16)
    blocks = ((from_left(odd, half).astype(BF16), e), (e, o), (o, from_right(even, half).astype(BF16)))
    for tap, pair in enumerate(blocks):
        rows = slice(base + tap * channels, base + (tap + 1) * channels)
        field[rows, :lanes] = pair[0]
        field[rows, lanes:] = pair[1]


def store_row_taps(field, base, lane_base, value, half):
    channels, lanes = value.shape
    blocks = (from_left(value, half).astype(BF16), value.astype(BF16), from_right(value, half).astype(BF16))
    for tap, block in enumerate(blocks):
        field[base + tap * channels : base + (tap + 1) * channels, lane_base : lane_base + lanes] = block


def rims_kernel(flag_ref, latent_hbm, inside_ref, across_ref, sems):
    last = latent_hbm.shape[1] - 1
    odd = flag_ref[2]
    gets = [
        pltpu.make_async_copy(latent_hbm.at[:, row], ref, sems.at[at])
        for at, (row, ref) in enumerate(((last * (1 - odd), inside_ref), (last * odd, across_ref)))
    ]
    for get in gets:
        get.start()
    for get in gets:
        get.wait()


def prepare_kernel(
    latent_hbm, weight_hbm, turned_ref, field_ref, latent, weight, latent_sem, weight_sem
):
    clips, rows, channels, width = latent.shape
    taps = weight.shape[0]
    get_latent = pltpu.make_async_copy(latent_hbm, latent, latent_sem)
    get_latent.start()
    cuts = list(range(0, taps, 1024)) + [taps]
    gets = [
        pltpu.make_async_copy(weight_hbm.at[a:b], weight.at[a:b], weight_sem.at[n])
        for n, (a, b) in enumerate(zip(cuts, cuts[1:]))
    ]
    for get in gets:
        get.start()
    pick = sort_pick(width, clips)
    get_latent.wait()
    for row in range(rows):
        value = dot(jnp.concatenate([latent[clip, row] for clip in range(clips)], axis=1), pick)
        lanes = value.shape[1] // 2
        store_taps(field_ref, row * 3 * channels, value[:, :lanes], value[:, lanes:], width // 2)
    for get, a, b in zip(gets, cuts, cuts[1:]):
        get.wait()
        turned_ref[:, a:b] = weight[a:b, :].T


def first_own_kernel(turned_ref, field_ref, first_ref, partial_ref):
    rows, channels, _ = first_ref.shape
    depth = 3 * channels
    for row in range(rows):
        start, stop = max(row - 1, 0), min(row + 2, rows)
        total = dot(
            turned_ref[:, (start - row + 1) * depth : (stop - row + 1) * depth],
            field_ref[start * depth : stop * depth, :],
        )
        if row == 0:
            partial_ref[0] = total
        elif row == rows - 1:
            partial_ref[1] = total
        else:
            first_ref[row] = silu(total).astype(BF16)


def first_rest_kernel(
    flag_ref, inside_ref, across_ref, turned_ref, partial_ref, own_ref, first_ref, rim
):
    clips, channels, width = inside_ref.shape
    depth = 3 * channels
    rows = first_ref.shape[0]
    pick = sort_pick(width, clips)
    odd = flag_ref[2] != 0
    for at in range(2):
        one, other = (inside_ref, across_ref) if at == 0 else (across_ref, inside_ref)
        blocks = [jnp.where(odd, one[clip], other[clip]) for clip in range(clips)]
        value = dot(jnp.concatenate(blocks, axis=1), pick)
        lanes = value.shape[1] // 2
        store_taps(rim, at * depth, value[:, :lanes], value[:, lanes:], width // 2)
    top = partial_ref[0] + dot(turned_ref[:, :depth], rim[:depth, :])
    first_ref[0] = silu(top).astype(BF16)
    bottom = partial_ref[1] + dot(turned_ref[:, 2 * depth :], rim[depth:, :])
    first_ref[rows - 1] = silu(bottom).astype(BF16)


def weights_kernel(
    time_hbm, mid_hbm, up_hbm, time_out, mid_out, skip_out, phase_out,
    time_rows, mid_rows, up_rows, sems,
):
    taps, inner = mid_rows.shape
    channels = up_rows.shape[2]
    cuts = list(range(0, taps, 1024)) + [taps]
    pieces = [(time_hbm, time_rows)]
    pieces += [(mid_hbm.at[a:b], mid_rows.at[a:b]) for a, b in zip(cuts, cuts[1:])]
    pieces += [(up_hbm, up_rows)]
    gets = [
        pltpu.make_async_copy(source, target, sems.at[n])
        for n, (source, target) in enumerate(pieces)
    ]
    for get in gets:
        get.start()
    gets[0].wait()
    time_out[...] = time_rows[...].T
    for get, a, b in zip(gets[1:-1], cuts, cuts[1:]):
        get.wait()
        mid_out[:, a:b] = mid_rows[a:b, :].T
    gets[-1].wait()
    skip_out[...] = jnp.concatenate(
        [up_rows[dr, dc, :, :channels] for dr in range(3) for dc in range(3)], axis=1
    )
    taps = [[up_rows[dr, dc, :, channels:].astype(F32) for dc in range(3)] for dr in range(3)]
    groups = ((lambda t: t[0], lambda t: t[1] + t[2]), (lambda t: t[0] + t[1], lambda t: t[2]))
    for row_phase in range(2):
        for row_tap in range(2):
            merged = [groups[row_phase][row_tap]([taps[dr][dc] for dr in range(3)]) for dc in range(3)]
            for column_phase in range(2):
                for column_tap in range(2):
                    value = groups[column_phase][column_tap](merged)
                    start = (2 * row_tap + column_tap) * inner
                    phase_out[2 * row_phase + column_phase, :, start : start + inner] = value.astype(
                        BF16
                    )


def skip_kernel(
    flag_ref, first_ref, outer_ref, middle_ref, relayed_ref, weight_ref,
    skip_ref, inside_ref, across_ref,
):
    rows, _, wide = skip_ref.shape
    lanes = wide // 2
    odd_band, odd_frame = flag_ref[2] != 0, flag_ref[3] != 0
    skips = []
    for row in range(rows):
        centre, middle = first_ref[row], middle_ref[row]
        outer = jnp.where(flag_ref[4] != 0, relayed_ref[row], outer_ref[row])
        before = jnp.where(odd_frame, outer, middle)
        after = jnp.where(odd_frame, middle, outer)
        stacked = jnp.concatenate([before, centre, after], axis=0)
        skip = (centre.astype(F32) + dot(weight_ref[...], stacked)).astype(BF16)
        skip_ref[row] = skip
        skips.append(skip)
    inside_ref[0] = jnp.where(odd_band, skips[0], skips[-1])
    across_ref[0] = jnp.where(odd_band, skips[-1], skips[0])
    for pooled_row in range(rows // 2):
        sums = skips[2 * pooled_row].astype(F32) + skips[2 * pooled_row + 1].astype(F32)
        pooled = ((sums[:, :lanes] + sums[:, lanes:]) * 0.25).astype(BF16)
        span = slice(pooled_row * lanes, (pooled_row + 1) * lanes)
        inside_ref[1, :, span] = pooled
        across_ref[1, :, span] = pooled


def own_kernel(skip_ref, pair_ref, mid_ref, skip_weight, mixed_ref, middle_ref, field, pooled, *, half):
    rows, channels, wide = skip_ref.shape
    lanes = wide // 2
    depth = 3 * channels
    for at in range(2):
        row = pair_ref[1, :, at * lanes : (at + 1) * lanes].astype(F32)
        store_row_taps(pooled, 0, at * lanes, row, half)
    for row in range(rows):
        value = skip_ref[row].astype(F32)
        store_taps(field, row * depth, value[:, :lanes], value[:, lanes:], half)
    parts = [dot(mid_ref[:, dr * depth : (dr + 1) * depth], pooled[...]) for dr in range(3)]
    middle_ref[:, :lanes] = parts[2][:, :lanes]
    middle_ref[:, lanes : 2 * lanes] = parts[2][:, lanes:] + parts[1][:, :lanes]
    middle_ref[:, 2 * lanes : 3 * lanes] = parts[1][:, lanes:] + parts[0][:, :lanes]
    middle_ref[:, 3 * lanes :] = parts[0][:, lanes:]
    for row in range(rows):
        first, last = max(row - 1, 0), min(row + 2, rows)
        mixed_ref[row] = dot(
            skip_weight[:, (first - row + 1) * depth : (last - row + 1) * depth],
            field[first * depth : last * depth, :],
        )


def last_kernel(
    flag_ref, mixed_ref, middle_ref, inside_ref, across_ref, mid_ref, skip_weight, phase_weight, field_ref,
    out_ref, low_field, high_field, cross_field, rims, middle_field,
):
    rows, channels, wide = mixed_ref.shape
    clips, _, _, width = out_ref.shape
    half, lanes = width // 2, wide // 2
    inner = mid_ref.shape[0]
    depth = 3 * channels

    odd = flag_ref[2] != 0
    lows = [jnp.where(odd, inside_ref[at], across_ref[at]) for at in range(2)]
    highs = [jnp.where(odd, across_ref[at], inside_ref[at]) for at in range(2)]
    for target, pair, inward in ((low_field, lows[1], 1), (high_field, highs[1], 0)):
        for at in range(2):
            row = pair[:, at * lanes : (at + 1) * lanes].astype(F32)
            store_row_taps(target, 0, at * lanes, row, half)
        cross_field[:, (1 - inward) * lanes : (2 - inward) * lanes] = target[
            :, inward * lanes : (inward + 1) * lanes
        ]
    above = dot(mid_ref[:, :depth], low_field[...])
    cross = dot(mid_ref[:, depth : 2 * depth], cross_field[...])
    below = dot(mid_ref[:, 2 * depth :], high_field[...])
    middles = [
        middle_ref[:, :lanes] + above[:, :lanes] + cross[:, :lanes],
        middle_ref[:, lanes : 2 * lanes] + above[:, lanes:],
        middle_ref[:, 2 * lanes : 3 * lanes] + below[:, :lanes],
        middle_ref[:, 3 * lanes :] + below[:, lanes:] + cross[:, lanes:],
    ]
    kept = (flag_ref[0] == 0, None, None, flag_ref[1] == 0)
    for at, (value, keep) in enumerate(zip(middles, kept)):
        value = silu(value)
        if keep is not None:
            value = jnp.where(keep, value, 0.0)
        store_row_taps(middle_field, at * 3 * inner, 0, value.astype(BF16).astype(F32), half)

    for at, row in enumerate((lows[0], highs[0])):
        value = row.astype(F32)
        store_taps(rims, at * depth, value[:, :lanes], value[:, lanes:], half)
    from_rim = {
        0: dot(skip_weight[:, :depth], rims[:depth, :]),
        rows - 1: dot(skip_weight[:, 2 * depth :], rims[depth:, :]),
    }
    unsort = unsort_pick(width, clips)
    block = 3 * inner
    for row_phase in range(2):
        phases = []
        for column_phase in range(2):
            total = None
            for tap in range(2):
                sides = [
                    middle_field[
                        (row_phase + tap + at) * block
                        + column_phase * inner : (row_phase + tap + at) * block
                        + (column_phase + 2) * inner,
                        :,
                    ]
                    for at in range(rows // 2)
                ]
                part = dot(
                    phase_weight[
                        2 * row_phase + column_phase, :, tap * 2 * inner : (tap + 1) * 2 * inner
                    ],
                    jnp.concatenate(sides, axis=1),
                )
                total = part if total is None else total + part
            phases.append(total)
        for at in range(rows // 2):
            row = 2 * at + row_phase
            latent = field_ref[row * depth + channels : row * depth + 2 * channels, :].astype(F32)
            upper = jnp.concatenate([phase[:, at * lanes : (at + 1) * lanes] for phase in phases], axis=1)
            total = latent + mixed_ref[row] + upper
            if row in from_rim:
                total += from_rim[row]
            natural = dot(total.astype(BF16), unsort).astype(BF16)
            for clip in range(clips):
                out_ref[clip, row] = natural[:, clip * width : (clip + 1) * width]


def call(kernel, name, outputs, limit, scratch=(), flops=0, kept=True, inputs=None, aliases=None):
    shapes = [
        pltpu.VMEM(shape, dtype) if kept else jax.ShapeDtypeStruct(shape, dtype)
        for shape, dtype in outputs
    ]
    specs = {} if inputs is None else {"in_specs": inputs}
    return pl.pallas_call(
        kernel,
        out_shape=shapes,
        scratch_shapes=list(scratch),
        compiler_params=pltpu.CompilerParams(vmem_limit_bytes=limit * MIB),
        cost_estimate=pl.CostEstimate(flops=flops, bytes_accessed=1 << 20, transcendentals=0),
        name=name,
        input_output_aliases=aliases or {},
        **specs,
    )


def in_hbm(value):
    return pltpu.with_memory_space_constraint(value, pltpu.HBM)


def in_vmem(*values):
    return [pltpu.with_memory_space_constraint(value, pltpu.VMEM) for value in values]


def body(latents, in_weight, time_weight, mid_weight, up_weight):
    device_count = lax.axis_size("frames")
    bands = device_count // FRAMES
    offset = bands // 2
    band_of = lambda index: (index + offset) % bands
    frame_of = lambda index: (index + offset) // bands % FRAMES
    swap = lambda step, group, lowest: [
        pair
        for i in range(device_count)
        if group(i) % 2 == lowest and group(i) + 1 < (FRAMES if step == bands else bands)
        for j in [(i + step) % device_count]
        for pair in ((i, j), (j, i))
    ]
    inside, across = swap(1, band_of, 0), swap(1, band_of, 1)
    outer_frames, middle_frames = swap(bands, frame_of, 0), swap(bands, frame_of, 1)
    relayed_pairs = [(i, j) for i, j in outer_frames if abs(i - j) != bands and band_of(i) % 2 == 0]
    hops = [(i, i - offset + 1) for i, _ in relayed_pairs]
    relays = [(i - offset + 1, j) for i, j in relayed_pairs]
    outer_frames = [pair for pair in outer_frames if pair not in relayed_pairs]
    index = lax.axis_index("frames")
    band, frame = band_of(index), frame_of(index)
    is_relayed = jnp.logical_and(jnp.logical_and(frame < 2, band < offset), band % 2 == 0)
    flags = jnp.stack([band == 0, band == bands - 1, band % 2, frame % 2, is_relayed]).astype(jnp.int32)

    clips, rows, width, channels = latents.shape
    inner = mid_weight.shape[3]
    wide = clips * width
    depth = 3 * channels
    anywhere = pl.BlockSpec(memory_space=pl.ANY)
    whole = pl.BlockSpec(memory_space=pltpu.VMEM)
    scalars = pl.BlockSpec(memory_space=pltpu.SMEM)
    turned = jnp.swapaxes(latents, 2, 3)

    inside_rim, across_rim = call(
        rims_kernel,
        "rims",
        [((clips, channels, width), BF16)] * 2,
        1,
        [pltpu.SemaphoreType.DMA((2,))],
        inputs=[scalars, anywhere],
    )(flags, in_hbm(turned))
    inside_row = lax.ppermute(inside_rim, "frames", inside)
    across_row = lax.ppermute(across_rim, "frames", across)
    in_turned, field = call(
        prepare_kernel,
        "prepare",
        [((channels, 3 * depth), BF16), ((rows * depth, wide), BF16)],
        8,
        [
            pltpu.VMEM(turned.shape, BF16),
            pltpu.VMEM((3 * depth, channels), BF16),
            pltpu.SemaphoreType.DMA(()),
            pltpu.SemaphoreType.DMA((-(-3 * depth // 1024),)),
        ],
        flops=2 * rows * wide * channels * wide,
        inputs=[anywhere, anywhere],
    )(in_hbm(turned), in_hbm(in_weight.reshape(3 * depth, channels)))
    first_own, partial = call(
        first_own_kernel,
        "first_own",
        [((rows, channels, wide), BF16), ((2, channels, wide), F32)],
        8,
        flops=2 * wide * channels * depth * (3 * rows - 2),
        inputs=[whole] * 2,
    )(*in_vmem(in_turned, field))
    (first,) = call(
        first_rest_kernel,
        "first_rest",
        [((rows, channels, wide), BF16)],
        8,
        [pltpu.VMEM((2 * depth, wide), BF16)],
        flops=2 * 2 * wide * channels * depth,
        inputs=[scalars] + [whole] * 5,
        aliases={5: 0},
    )(flags, *in_vmem(inside_row, across_row, in_turned, partial, first_own))
    hopped = lax.ppermute(first, "frames", hops)
    outer = lax.ppermute(first, "frames", outer_frames)
    middle = lax.ppermute(first, "frames", middle_frames)

    time_rows, mid_rows, up_rows, first = lax.optimization_barrier(
        (
            time_weight.reshape(depth, channels),
            mid_weight.reshape(3 * depth, inner),
            jnp.swapaxes(up_weight, 2, 3),
            first,
        )
    )
    time_turned, mid_turned, skip_weight, phase_weight = call(
        weights_kernel,
        "weights",
        [
            ((channels, depth), BF16),
            ((inner, 3 * depth), BF16),
            ((channels, 3 * depth), BF16),
            ((4, channels, 4 * inner), BF16),
        ],
        20,
        [
            pltpu.VMEM(time_rows.shape, BF16),
            pltpu.VMEM(mid_rows.shape, BF16),
            pltpu.VMEM(up_rows.shape, BF16),
            pltpu.SemaphoreType.DMA((2 + -(-3 * depth // 1024),)),
        ],
        flops=2 * 10**9,
        inputs=[anywhere] * 3,
    )(in_hbm(time_rows), in_hbm(mid_rows), in_hbm(up_rows))

    hopped, time_turned = lax.optimization_barrier((hopped, time_turned))
    relayed = lax.ppermute(hopped, "frames", relays)
    skip, inside_rows, across_rows = call(
        skip_kernel,
        "skip",
        [
            ((rows, channels, wide), BF16),
            ((2, channels, wide), BF16),
            ((2, channels, wide), BF16),
        ],
        8,
        flops=2 * rows * wide * depth * channels,
        inputs=[scalars] + [whole] * 5,
    )(flags, *in_vmem(first, outer, middle, relayed, time_turned))
    from_across = lax.ppermute(across_rows, "frames", across)
    from_inside = lax.ppermute(inside_rows, "frames", inside)

    mixed, middle = call(
        lambda *refs: own_kernel(*refs, half=width // 2),
        "own_rows",
        [((rows, channels, wide), F32), ((inner, 2 * wide), F32)],
        16,
        [pltpu.VMEM((rows * depth, wide), BF16), pltpu.VMEM((depth, wide), BF16)],
        flops=2 * wide * depth * (3 * inner + (3 * rows - 2) * channels),
        inputs=[whole] * 4,
    )(*in_vmem(skip, inside_rows, mid_turned, skip_weight))

    (out,) = call(
        last_kernel,
        "last",
        [(turned.shape, BF16)],
        20,
        [
            pltpu.VMEM((depth, wide), BF16),
            pltpu.VMEM((depth, wide), BF16),
            pltpu.VMEM((depth, wide), BF16),
            pltpu.VMEM((2 * depth, wide), BF16),
            pltpu.VMEM((4 * 3 * inner, wide // 2), BF16),
        ],
        flops=2 * wide * (3 * depth * inner + 2 * depth * channels + rows * 4 * inner * channels),
        kept=False,
        inputs=[scalars] + [whole] * 8,
    )(
        flags,
        *in_vmem(
            mixed, middle, from_inside, from_across, mid_turned, skip_weight, phase_weight, field
        ),
    )
    return jnp.swapaxes(out, 2, 3)


def solution(mesh):
    in_specs = (P("groups", "frames", None, None), P(), P(), P(), P())
    out_specs = P("groups", "frames", None, None)
    return jax.shard_map(body, mesh=mesh, in_specs=in_specs, out_specs=out_specs, check_vma=False)
```

```python
import jax
import jax.numpy as jnp
from jax import lax
from jax.experimental import pallas as pl
from jax.experimental.pallas import tpu as pltpu
from jax.sharding import PartitionSpec as P


FRAMES = 4
BF16 = jnp.bfloat16
F32 = jnp.float32
MIB = 1024 * 1024


def dot(left, right):
    return jnp.dot(left, right, preferred_element_type=F32)


def silu(value):
    return value / (1.0 + jnp.exp(-value))


def sort_pick(width, clips):
    wide, half = width * clips, width // 2
    source = lax.broadcasted_iota(jnp.int32, (wide, wide), 0)
    lane = lax.broadcasted_iota(jnp.int32, (wide, wide), 1)
    parity, clip, j = lane // (wide // 2), lane // half % clips, lane % half
    return (source == clip * width + 2 * j + parity).astype(BF16)


def unsort_pick(width, clips):
    wide, half = width * clips, width // 2
    source = lax.broadcasted_iota(jnp.int32, (wide, wide), 0)
    lane = lax.broadcasted_iota(jnp.int32, (wide, wide), 1)
    clip, column = lane // width, lane % width
    return (source == column % 2 * (wide // 2) + clip * half + column // 2).astype(BF16)


def from_left(value, half):
    lane = lax.broadcasted_iota(jnp.int32, (1, value.shape[1]), 1)
    return jnp.where(lane % half == 0, 0.0, pltpu.roll(value, 1, 1))


def from_right(value, half):
    width = value.shape[1]
    lane = lax.broadcasted_iota(jnp.int32, (1, width), 1)
    return jnp.where(lane % half == half - 1, 0.0, pltpu.roll(value, width - 1, 1))


def store_taps(field, base, even, odd, half):
    channels, lanes = even.shape
    e, o = even.astype(BF16), odd.astype(BF16)
    blocks = ((from_left(odd, half).astype(BF16), e), (e, o), (o, from_right(even, half).astype(BF16)))
    for tap, pair in enumerate(blocks):
        rows = slice(base + tap * channels, base + (tap + 1) * channels)
        field[rows, :lanes] = pair[0]
        field[rows, lanes:] = pair[1]


def store_row_taps(field, base, lane_base, value, half):
    channels, lanes = value.shape
    blocks = (from_left(value, half).astype(BF16), value.astype(BF16), from_right(value, half).astype(BF16))
    for tap, block in enumerate(blocks):
        field[base + tap * channels : base + (tap + 1) * channels, lane_base : lane_base + lanes] = block


def fetch_kernel(
    flag_ref, latent_hbm, weight_hbm, inside_ref, across_ref, latent_ref, weight_ref, sems
):
    last = latent_hbm.shape[1] - 1
    odd = flag_ref[2]
    pieces = [
        (latent_hbm.at[:, last * odd], across_ref),
        (latent_hbm.at[:, last * (1 - odd)], inside_ref),
        (latent_hbm, latent_ref),
        (weight_hbm, weight_ref),
    ]
    gets = [
        pltpu.make_async_copy(source, target, sems.at[n])
        for n, (source, target) in enumerate(pieces)
    ]
    for get in gets:
        get.start()
    for get in gets:
        get.wait()


def prepare_kernel(latent_ref, weight_ref, turned_ref, field_ref):
    clips, rows, channels, width = latent_ref.shape
    pick = sort_pick(width, clips)
    for row in range(rows):
        value = dot(jnp.concatenate([latent_ref[clip, row] for clip in range(clips)], axis=1), pick)
        lanes = value.shape[1] // 2
        store_taps(field_ref, row * 3 * channels, value[:, :lanes], value[:, lanes:], width // 2)
    turned_ref[...] = weight_ref[...].T


def first_kernel(flag_ref, inside_ref, across_ref, turned_ref, field_ref, first_ref, rim):
    clips, channels, width = inside_ref.shape
    depth = 3 * channels
    rows = first_ref.shape[0]
    pick = sort_pick(width, clips)
    odd = flag_ref[2] != 0
    for at in range(2):
        one, other = (inside_ref, across_ref) if at == 0 else (across_ref, inside_ref)
        blocks = [jnp.where(odd, one[clip], other[clip]) for clip in range(clips)]
        value = dot(jnp.concatenate(blocks, axis=1), pick)
        lanes = value.shape[1] // 2
        store_taps(rim, at * depth, value[:, :lanes], value[:, lanes:], width // 2)
    for row in list(range(1, rows - 1)) + [0, rows - 1]:
        start, stop = max(row - 1, 0), min(row + 2, rows)
        total = dot(
            turned_ref[:, (start - row + 1) * depth : (stop - row + 1) * depth],
            field_ref[start * depth : stop * depth, :],
        )
        if row == 0:
            total += dot(turned_ref[:, :depth], rim[:depth, :])
        if row == rows - 1:
            total += dot(turned_ref[:, 2 * depth :], rim[depth:, :])
        first_ref[row] = silu(total).astype(BF16)


def weights_kernel(
    time_hbm, mid_hbm, up_hbm, time_out, mid_out, skip_out, phase_out,
    time_rows, mid_rows, up_rows, sems,
):
    taps, inner = mid_rows.shape
    channels = up_rows.shape[2]
    cuts = list(range(0, taps, 1024)) + [taps]
    pieces = [(time_hbm, time_rows)]
    pieces += [(mid_hbm.at[a:b], mid_rows.at[a:b]) for a, b in zip(cuts, cuts[1:])]
    pieces += [(up_hbm, up_rows)]
    gets = [
        pltpu.make_async_copy(source, target, sems.at[n])
        for n, (source, target) in enumerate(pieces)
    ]
    for get in gets:
        get.start()
    gets[0].wait()
    time_out[...] = time_rows[...].T
    for get, a, b in zip(gets[1:-1], cuts, cuts[1:]):
        get.wait()
        mid_out[:, a:b] = mid_rows[a:b, :].T
    gets[-1].wait()
    skip_out[...] = jnp.concatenate(
        [up_rows[dr, dc, :, :channels] for dr in range(3) for dc in range(3)], axis=1
    )
    taps = [[up_rows[dr, dc, :, channels:].astype(F32) for dc in range(3)] for dr in range(3)]
    groups = ((lambda t: t[0], lambda t: t[1] + t[2]), (lambda t: t[0] + t[1], lambda t: t[2]))
    for row_phase in range(2):
        for row_tap in range(2):
            merged = [groups[row_phase][row_tap]([taps[dr][dc] for dr in range(3)]) for dc in range(3)]
            for column_phase in range(2):
                for column_tap in range(2):
                    value = groups[column_phase][column_tap](merged)
                    start = (2 * row_tap + column_tap) * inner
                    phase_out[2 * row_phase + column_phase, :, start : start + inner] = value.astype(
                        BF16
                    )


def skip_kernel(
    flag_ref, first_ref, outer_ref, middle_ref, relayed_ref, weight_ref,
    skip_ref, inside_ref, across_ref,
):
    rows, _, wide = skip_ref.shape
    lanes = wide // 2
    odd_band, odd_frame = flag_ref[2] != 0, flag_ref[3] != 0
    skips = []
    for row in range(rows):
        centre, middle = first_ref[row], middle_ref[row]
        outer = jnp.where(flag_ref[4] != 0, relayed_ref[row], outer_ref[row])
        before = jnp.where(odd_frame, outer, middle)
        after = jnp.where(odd_frame, middle, outer)
        stacked = jnp.concatenate([before, centre, after], axis=0)
        skip = (centre.astype(F32) + dot(weight_ref[...], stacked)).astype(BF16)
        skip_ref[row] = skip
        skips.append(skip)
    inside_ref[0] = jnp.where(odd_band, skips[0], skips[-1])
    across_ref[0] = jnp.where(odd_band, skips[-1], skips[0])
    for pooled_row in range(rows // 2):
        sums = skips[2 * pooled_row].astype(F32) + skips[2 * pooled_row + 1].astype(F32)
        pooled = ((sums[:, :lanes] + sums[:, lanes:]) * 0.25).astype(BF16)
        span = slice(pooled_row * lanes, (pooled_row + 1) * lanes)
        inside_ref[1, :, span] = pooled
        across_ref[1, :, span] = pooled


def own_kernel(skip_ref, pair_ref, mid_ref, skip_weight, mixed_ref, middle_ref, field, pooled, *, half):
    rows, channels, wide = skip_ref.shape
    lanes = wide // 2
    depth = 3 * channels
    for at in range(2):
        row = pair_ref[1, :, at * lanes : (at + 1) * lanes].astype(F32)
        store_row_taps(pooled, 0, at * lanes, row, half)
    for row in range(rows):
        value = skip_ref[row].astype(F32)
        store_taps(field, row * depth, value[:, :lanes], value[:, lanes:], half)
    parts = [dot(mid_ref[:, dr * depth : (dr + 1) * depth], pooled[...]) for dr in range(3)]
    middle_ref[:, :lanes] = parts[2][:, :lanes]
    middle_ref[:, lanes : 2 * lanes] = parts[2][:, lanes:] + parts[1][:, :lanes]
    middle_ref[:, 2 * lanes : 3 * lanes] = parts[1][:, lanes:] + parts[0][:, :lanes]
    middle_ref[:, 3 * lanes :] = parts[0][:, lanes:]
    for row in range(rows):
        first, last = max(row - 1, 0), min(row + 2, rows)
        mixed_ref[row] = dot(
            skip_weight[:, (first - row + 1) * depth : (last - row + 1) * depth],
            field[first * depth : last * depth, :],
        )


def last_kernel(
    flag_ref, mixed_ref, middle_ref, inside_ref, across_ref, mid_ref, skip_weight, phase_weight, field_ref,
    out_ref, low_field, high_field, cross_field, rims, middle_field,
):
    rows, channels, wide = mixed_ref.shape
    clips, _, _, width = out_ref.shape
    half, lanes = width // 2, wide // 2
    inner = mid_ref.shape[0]
    depth = 3 * channels

    odd = flag_ref[2] != 0
    lows = [jnp.where(odd, inside_ref[at], across_ref[at]) for at in range(2)]
    highs = [jnp.where(odd, across_ref[at], inside_ref[at]) for at in range(2)]
    for target, pair, inward in ((low_field, lows[1], 1), (high_field, highs[1], 0)):
        for at in range(2):
            row = pair[:, at * lanes : (at + 1) * lanes].astype(F32)
            store_row_taps(target, 0, at * lanes, row, half)
        cross_field[:, (1 - inward) * lanes : (2 - inward) * lanes] = target[
            :, inward * lanes : (inward + 1) * lanes
        ]
    above = dot(mid_ref[:, :depth], low_field[...])
    cross = dot(mid_ref[:, depth : 2 * depth], cross_field[...])
    below = dot(mid_ref[:, 2 * depth :], high_field[...])
    middles = [
        middle_ref[:, :lanes] + above[:, :lanes] + cross[:, :lanes],
        middle_ref[:, lanes : 2 * lanes] + above[:, lanes:],
        middle_ref[:, 2 * lanes : 3 * lanes] + below[:, :lanes],
        middle_ref[:, 3 * lanes :] + below[:, lanes:] + cross[:, lanes:],
    ]
    kept = (flag_ref[0] == 0, None, None, flag_ref[1] == 0)
    for at, (value, keep) in enumerate(zip(middles, kept)):
        value = silu(value)
        if keep is not None:
            value = jnp.where(keep, value, 0.0)
        store_row_taps(middle_field, at * 3 * inner, 0, value.astype(BF16).astype(F32), half)

    for at, row in enumerate((lows[0], highs[0])):
        value = row.astype(F32)
        store_taps(rims, at * depth, value[:, :lanes], value[:, lanes:], half)
    from_rim = {
        0: dot(skip_weight[:, :depth], rims[:depth, :]),
        rows - 1: dot(skip_weight[:, 2 * depth :], rims[depth:, :]),
    }
    unsort = unsort_pick(width, clips)
    block = 3 * inner
    for row_phase in range(2):
        phases = []
        for column_phase in range(2):
            total = None
            for tap in range(2):
                sides = [
                    middle_field[
                        (row_phase + tap + at) * block
                        + column_phase * inner : (row_phase + tap + at) * block
                        + (column_phase + 2) * inner,
                        :,
                    ]
                    for at in range(rows // 2)
                ]
                part = dot(
                    phase_weight[
                        2 * row_phase + column_phase, :, tap * 2 * inner : (tap + 1) * 2 * inner
                    ],
                    jnp.concatenate(sides, axis=1),
                )
                total = part if total is None else total + part
            phases.append(total)
        for at in range(rows // 2):
            row = 2 * at + row_phase
            latent = field_ref[row * depth + channels : row * depth + 2 * channels, :].astype(F32)
            upper = jnp.concatenate([phase[:, at * lanes : (at + 1) * lanes] for phase in phases], axis=1)
            total = latent + mixed_ref[row] + upper
            if row in from_rim:
                total += from_rim[row]
            natural = dot(total.astype(BF16), unsort).astype(BF16)
            for clip in range(clips):
                out_ref[clip, row] = natural[:, clip * width : (clip + 1) * width]


def call(kernel, name, outputs, limit, scratch=(), flops=0, kept=True, inputs=None, aliases=None):
    shapes = [
        pltpu.VMEM(shape, dtype) if kept else jax.ShapeDtypeStruct(shape, dtype)
        for shape, dtype in outputs
    ]
    specs = {} if inputs is None else {"in_specs": inputs}
    return pl.pallas_call(
        kernel,
        out_shape=shapes,
        scratch_shapes=list(scratch),
        compiler_params=pltpu.CompilerParams(vmem_limit_bytes=limit * MIB),
        cost_estimate=pl.CostEstimate(flops=flops, bytes_accessed=1 << 20, transcendentals=0),
        name=name,
        input_output_aliases=aliases or {},
        **specs,
    )


def in_hbm(value):
    return pltpu.with_memory_space_constraint(value, pltpu.HBM)


def in_vmem(*values):
    return [pltpu.with_memory_space_constraint(value, pltpu.VMEM) for value in values]


def body(latents, in_weight, time_weight, mid_weight, up_weight):
    device_count = lax.axis_size("frames")
    bands = device_count // FRAMES
    offset = bands // 2
    band_of = lambda index: (index + offset) % bands
    frame_of = lambda index: (index + offset) // bands % FRAMES
    swap = lambda step, group, lowest: [
        pair
        for i in range(device_count)
        if group(i) % 2 == lowest and group(i) + 1 < (FRAMES if step == bands else bands)
        for j in [(i + step) % device_count]
        for pair in ((i, j), (j, i))
    ]
    inside, across = swap(1, band_of, 0), swap(1, band_of, 1)
    outer_frames, middle_frames = swap(bands, frame_of, 0), swap(bands, frame_of, 1)
    relayed_pairs = [(i, j) for i, j in outer_frames if abs(i - j) != bands and band_of(i) % 2 == 0]
    hops = [(i, i - offset + 1) for i, _ in relayed_pairs]
    relays = [(i - offset + 1, j) for i, j in relayed_pairs]
    outer_frames = [pair for pair in outer_frames if pair not in relayed_pairs]
    index = lax.axis_index("frames")
    band, frame = band_of(index), frame_of(index)
    is_relayed = jnp.logical_and(jnp.logical_and(frame < 2, band < offset), band % 2 == 0)
    flags = jnp.stack([band == 0, band == bands - 1, band % 2, frame % 2, is_relayed]).astype(jnp.int32)

    clips, rows, width, channels = latents.shape
    inner = mid_weight.shape[3]
    wide = clips * width
    depth = 3 * channels
    anywhere = pl.BlockSpec(memory_space=pl.ANY)
    whole = pl.BlockSpec(memory_space=pltpu.VMEM)
    scalars = pl.BlockSpec(memory_space=pltpu.SMEM)
    turned = jnp.swapaxes(latents, 2, 3)

    inside_rim, across_rim, latent, in_rows = call(
        fetch_kernel,
        "fetch",
        [
            ((clips, channels, width), BF16),
            ((clips, channels, width), BF16),
            (turned.shape, BF16),
            ((3 * depth, channels), BF16),
        ],
        1,
        [pltpu.SemaphoreType.DMA((4,))],
        inputs=[scalars, anywhere, anywhere],
    )(flags, in_hbm(turned), in_hbm(in_weight.reshape(3 * depth, channels)))
    inside_row = lax.ppermute(inside_rim, "frames", inside)
    across_row = lax.ppermute(across_rim, "frames", across)
    in_turned, field = call(
        prepare_kernel,
        "prepare",
        [((channels, 3 * depth), BF16), ((rows * depth, wide), BF16)],
        8,
        flops=2 * rows * wide * channels * wide,
        inputs=[whole] * 2,
    )(*in_vmem(latent, in_rows))
    (first,) = call(
        first_kernel,
        "first",
        [((rows, channels, wide), BF16)],
        8,
        [pltpu.VMEM((2 * depth, wide), BF16)],
        flops=2 * rows * wide * channels * 3 * depth,
        inputs=[scalars] + [whole] * 4,
    )(flags, *in_vmem(inside_row, across_row, in_turned, field))
    hopped = lax.ppermute(first, "frames", hops)
    outer = lax.ppermute(first, "frames", outer_frames)
    middle = lax.ppermute(first, "frames", middle_frames)

    time_rows, mid_rows, up_rows, first = lax.optimization_barrier(
        (
            time_weight.reshape(depth, channels),
            mid_weight.reshape(3 * depth, inner),
            jnp.swapaxes(up_weight, 2, 3),
            first,
        )
    )
    time_turned, mid_turned, skip_weight, phase_weight = call(
        weights_kernel,
        "weights",
        [
            ((channels, depth), BF16),
            ((inner, 3 * depth), BF16),
            ((channels, 3 * depth), BF16),
            ((4, channels, 4 * inner), BF16),
        ],
        20,
        [
            pltpu.VMEM(time_rows.shape, BF16),
            pltpu.VMEM(mid_rows.shape, BF16),
            pltpu.VMEM(up_rows.shape, BF16),
            pltpu.SemaphoreType.DMA((2 + -(-3 * depth // 1024),)),
        ],
        flops=2 * 10**9,
        inputs=[anywhere] * 3,
    )(in_hbm(time_rows), in_hbm(mid_rows), in_hbm(up_rows))

    hopped, time_turned = lax.optimization_barrier((hopped, time_turned))
    relayed = lax.ppermute(hopped, "frames", relays)
    skip, inside_rows, across_rows = call(
        skip_kernel,
        "skip",
        [
            ((rows, channels, wide), BF16),
            ((2, channels, wide), BF16),
            ((2, channels, wide), BF16),
        ],
        8,
        flops=2 * rows * wide * depth * channels,
        inputs=[scalars] + [whole] * 5,
    )(flags, *in_vmem(first, outer, middle, relayed, time_turned))
    from_across = lax.ppermute(across_rows, "frames", across)
    from_inside = lax.ppermute(inside_rows, "frames", inside)

    mixed, middle = call(
        lambda *refs: own_kernel(*refs, half=width // 2),
        "own_rows",
        [((rows, channels, wide), F32), ((inner, 2 * wide), F32)],
        16,
        [pltpu.VMEM((rows * depth, wide), BF16), pltpu.VMEM((depth, wide), BF16)],
        flops=2 * wide * depth * (3 * inner + (3 * rows - 2) * channels),
        inputs=[whole] * 4,
    )(*in_vmem(skip, inside_rows, mid_turned, skip_weight))

    (out,) = call(
        last_kernel,
        "last",
        [(turned.shape, BF16)],
        20,
        [
            pltpu.VMEM((depth, wide), BF16),
            pltpu.VMEM((depth, wide), BF16),
            pltpu.VMEM((depth, wide), BF16),
            pltpu.VMEM((2 * depth, wide), BF16),
            pltpu.VMEM((4 * 3 * inner, wide // 2), BF16),
        ],
        flops=2 * wide * (3 * depth * inner + 2 * depth * channels + rows * 4 * inner * channels),
        kept=False,
        inputs=[scalars] + [whole] * 8,
    )(
        flags,
        *in_vmem(
            mixed, middle, from_inside, from_across, mid_turned, skip_weight, phase_weight, field
        ),
    )
    return jnp.swapaxes(out, 2, 3)


def solution(mesh):
    in_specs = (P("groups", "frames", None, None), P(), P(), P(), P())
    out_specs = P("groups", "frames", None, None)
    return jax.shard_map(body, mesh=mesh, in_specs=in_specs, out_specs=out_specs, check_vma=False)
```

```python
import functools

import jax
import jax.numpy as jnp
from jax import lax
from jax.experimental import pallas as pl
from jax.experimental.pallas import tpu as pltpu
from jax.sharding import PartitionSpec as P


FRAMES = 4
BF16 = jnp.bfloat16
F32 = jnp.float32
MIB = 1024 * 1024


def place(bands):
    index = lax.axis_index("frames") + bands // 2
    return lax.rem(index, bands), lax.rem(lax.div(index, bands), FRAMES)


def dot(left, right):
    return jnp.dot(left, right, preferred_element_type=F32)


def silu(value):
    return value / (1.0 + jnp.exp(-value))


def sort_pick(width, clips):
    wide, half = width * clips, width // 2
    source = lax.broadcasted_iota(jnp.int32, (wide, wide), 0)
    lane = lax.broadcasted_iota(jnp.int32, (wide, wide), 1)
    parity, clip, j = lane // (wide // 2), lane // half % clips, lane % half
    return (source == clip * width + 2 * j + parity).astype(BF16)


def unsort_pick(width, clips):
    wide, half = width * clips, width // 2
    source = lax.broadcasted_iota(jnp.int32, (wide, wide), 0)
    lane = lax.broadcasted_iota(jnp.int32, (wide, wide), 1)
    clip, column = lane // width, lane % width
    return (source == column % 2 * (wide // 2) + clip * half + column // 2).astype(BF16)


def from_left(value, half):
    lane = lax.broadcasted_iota(jnp.int32, (1, value.shape[1]), 1)
    return jnp.where(lane % half == 0, 0.0, pltpu.roll(value, 1, 1))


def from_right(value, half):
    width = value.shape[1]
    lane = lax.broadcasted_iota(jnp.int32, (1, width), 1)
    return jnp.where(lane % half == half - 1, 0.0, pltpu.roll(value, width - 1, 1))


def store_taps(field, base, even, odd, half):
    channels, lanes = even.shape
    e, o = even.astype(BF16), odd.astype(BF16)
    blocks = ((from_left(odd, half).astype(BF16), e), (e, o), (o, from_right(even, half).astype(BF16)))
    for tap, pair in enumerate(blocks):
        rows = slice(base + tap * channels, base + (tap + 1) * channels)
        field[rows, :lanes] = pair[0]
        field[rows, lanes:] = pair[1]


def store_row_taps(field, base, lane_base, value, half):
    channels, lanes = value.shape
    blocks = (from_left(value, half).astype(BF16), value.astype(BF16), from_right(value, half).astype(BF16))
    for tap, block in enumerate(blocks):
        field[base + tap * channels : base + (tap + 1) * channels, lane_base : lane_base + lanes] = block


def fetch_kernel(
    latent_hbm, weight_hbm, inside_ref, across_ref, latent_ref, weight_ref, sems, *, bands
):
    last = latent_hbm.shape[1] - 1
    odd = lax.rem(place(bands)[0], 2)
    pieces = [
        (latent_hbm.at[:, last * odd], across_ref),
        (latent_hbm.at[:, last * (1 - odd)], inside_ref),
        (latent_hbm, latent_ref),
        (weight_hbm, weight_ref),
    ]
    gets = [
        pltpu.make_async_copy(source, target, sems.at[n])
        for n, (source, target) in enumerate(pieces)
    ]
    for get in gets:
        get.start()
    for get in gets:
        get.wait()


def prepare_kernel(latent_ref, weight_ref, turned_ref, field_ref):
    clips, rows, channels, width = latent_ref.shape
    pick = sort_pick(width, clips)
    for row in range(rows):
        value = dot(jnp.concatenate([latent_ref[clip, row] for clip in range(clips)], axis=1), pick)
        lanes = value.shape[1] // 2
        store_taps(field_ref, row * 3 * channels, value[:, :lanes], value[:, lanes:], width // 2)
    turned_ref[...] = weight_ref[...].T


def first_kernel(inside_ref, across_ref, turned_ref, field_ref, first_ref, rim, *, bands):
    clips, channels, width = inside_ref.shape
    depth = 3 * channels
    rows = first_ref.shape[0]
    pick = sort_pick(width, clips)
    odd = lax.rem(place(bands)[0], 2) == 1
    for at in range(2):
        one, other = (inside_ref, across_ref) if at == 0 else (across_ref, inside_ref)
        blocks = [jnp.where(odd, one[clip], other[clip]) for clip in range(clips)]
        value = dot(jnp.concatenate(blocks, axis=1), pick)
        lanes = value.shape[1] // 2
        store_taps(rim, at * depth, value[:, :lanes], value[:, lanes:], width // 2)
    for row in list(range(1, rows - 1)) + [0, rows - 1]:
        start, stop = max(row - 1, 0), min(row + 2, rows)
        total = dot(
            turned_ref[:, (start - row + 1) * depth : (stop - row + 1) * depth],
            field_ref[start * depth : stop * depth, :],
        )
        if row == 0:
            total += dot(turned_ref[:, :depth], rim[:depth, :])
        if row == rows - 1:
            total += dot(turned_ref[:, 2 * depth :], rim[depth:, :])
        first_ref[row] = silu(total).astype(BF16)


def weights_kernel(
    time_hbm, mid_hbm, up_hbm, time_out, mid_out, skip_out, phase_out,
    time_rows, mid_rows, up_rows, sems,
):
    taps, inner = mid_rows.shape
    channels = up_rows.shape[2]
    cuts = list(range(0, taps, 1024)) + [taps]
    pieces = [(time_hbm, time_rows)]
    pieces += [(mid_hbm.at[a:b], mid_rows.at[a:b]) for a, b in zip(cuts, cuts[1:])]
    pieces += [(up_hbm, up_rows)]
    gets = [
        pltpu.make_async_copy(source, target, sems.at[n])
        for n, (source, target) in enumerate(pieces)
    ]
    for get in gets:
        get.start()
    gets[0].wait()
    time_out[...] = time_rows[...].T
    for get, a, b in zip(gets[1:-1], cuts, cuts[1:]):
        get.wait()
        mid_out[:, a:b] = mid_rows[a:b, :].T
    gets[-1].wait()
    skip_out[...] = jnp.concatenate(
        [up_rows[dr, dc, :, :channels] for dr in range(3) for dc in range(3)], axis=1
    )
    taps = [[up_rows[dr, dc, :, channels:].astype(F32) for dc in range(3)] for dr in range(3)]
    groups = ((lambda t: t[0], lambda t: t[1] + t[2]), (lambda t: t[0] + t[1], lambda t: t[2]))
    for row_phase in range(2):
        for row_tap in range(2):
            merged = [groups[row_phase][row_tap]([taps[dr][dc] for dr in range(3)]) for dc in range(3)]
            for column_phase in range(2):
                for column_tap in range(2):
                    value = groups[column_phase][column_tap](merged)
                    start = (2 * row_tap + column_tap) * inner
                    phase_out[2 * row_phase + column_phase, :, start : start + inner] = value.astype(
                        BF16
                    )


def skip_kernel(
    first_ref, outer_ref, middle_ref, relayed_ref, weight_ref, skip_ref, inside_ref, across_ref,
    *, bands
):
    rows, _, wide = skip_ref.shape
    lanes = wide // 2
    band, frame = place(bands)
    odd_band, odd_frame = lax.rem(band, 2) == 1, lax.rem(frame, 2) == 1
    is_relayed = jnp.logical_and(jnp.logical_and(frame < 2, band < bands // 2), lax.rem(band, 2) == 0)
    skips = []
    for row in range(rows):
        centre, middle = first_ref[row], middle_ref[row]
        outer = jnp.where(is_relayed, relayed_ref[row], outer_ref[row])
        before = jnp.where(odd_frame, outer, middle)
        after = jnp.where(odd_frame, middle, outer)
        stacked = jnp.concatenate([before, centre, after], axis=0)
        skip = (centre.astype(F32) + dot(weight_ref[...], stacked)).astype(BF16)
        skip_ref[row] = skip
        skips.append(skip)
    inside_ref[0] = jnp.where(odd_band, skips[0], skips[-1])
    across_ref[0] = jnp.where(odd_band, skips[-1], skips[0])
    for pooled_row in range(rows // 2):
        sums = skips[2 * pooled_row].astype(F32) + skips[2 * pooled_row + 1].astype(F32)
        pooled = ((sums[:, :lanes] + sums[:, lanes:]) * 0.25).astype(BF16)
        span = slice(pooled_row * lanes, (pooled_row + 1) * lanes)
        inside_ref[1, :, span] = pooled
        across_ref[1, :, span] = pooled


def own_kernel(skip_ref, pair_ref, mid_ref, skip_weight, mixed_ref, middle_ref, field, pooled, *, half):
    rows, channels, wide = skip_ref.shape
    lanes = wide // 2
    depth = 3 * channels
    for at in range(2):
        row = pair_ref[1, :, at * lanes : (at + 1) * lanes].astype(F32)
        store_row_taps(pooled, 0, at * lanes, row, half)
    for row in range(rows):
        value = skip_ref[row].astype(F32)
        store_taps(field, row * depth, value[:, :lanes], value[:, lanes:], half)
    parts = [dot(mid_ref[:, dr * depth : (dr + 1) * depth], pooled[...]) for dr in range(3)]
    middle_ref[:, :lanes] = parts[2][:, :lanes]
    middle_ref[:, lanes : 2 * lanes] = parts[2][:, lanes:] + parts[1][:, :lanes]
    middle_ref[:, 2 * lanes : 3 * lanes] = parts[1][:, lanes:] + parts[0][:, :lanes]
    middle_ref[:, 3 * lanes :] = parts[0][:, lanes:]
    for row in range(rows):
        first, last = max(row - 1, 0), min(row + 2, rows)
        mixed_ref[row] = dot(
            skip_weight[:, (first - row + 1) * depth : (last - row + 1) * depth],
            field[first * depth : last * depth, :],
        )


def last_kernel(
    mixed_ref, middle_ref, inside_ref, across_ref, mid_ref, skip_weight, phase_weight, field_ref,
    out_ref, low_field, high_field, cross_field, rims, middle_field, *, bands
):
    rows, channels, wide = mixed_ref.shape
    clips, _, _, width = out_ref.shape
    half, lanes = width // 2, wide // 2
    inner = mid_ref.shape[0]
    depth = 3 * channels

    band = place(bands)[0]
    odd = lax.rem(band, 2) == 1
    lows = [jnp.where(odd, inside_ref[at], across_ref[at]) for at in range(2)]
    highs = [jnp.where(odd, across_ref[at], inside_ref[at]) for at in range(2)]
    for target, pair, inward in ((low_field, lows[1], 1), (high_field, highs[1], 0)):
        for at in range(2):
            row = pair[:, at * lanes : (at + 1) * lanes].astype(F32)
            store_row_taps(target, 0, at * lanes, row, half)
        cross_field[:, (1 - inward) * lanes : (2 - inward) * lanes] = target[
            :, inward * lanes : (inward + 1) * lanes
        ]
    above = dot(mid_ref[:, :depth], low_field[...])
    cross = dot(mid_ref[:, depth : 2 * depth], cross_field[...])
    below = dot(mid_ref[:, 2 * depth :], high_field[...])
    middles = [
        middle_ref[:, :lanes] + above[:, :lanes] + cross[:, :lanes],
        middle_ref[:, lanes : 2 * lanes] + above[:, lanes:],
        middle_ref[:, 2 * lanes : 3 * lanes] + below[:, :lanes],
        middle_ref[:, 3 * lanes :] + below[:, lanes:] + cross[:, lanes:],
    ]
    kept = (band != 0, None, None, band != bands - 1)
    for at, (value, keep) in enumerate(zip(middles, kept)):
        value = silu(value)
        if keep is not None:
            value = jnp.where(keep, value, 0.0)
        store_row_taps(middle_field, at * 3 * inner, 0, value.astype(BF16).astype(F32), half)

    for at, row in enumerate((lows[0], highs[0])):
        value = row.astype(F32)
        store_taps(rims, at * depth, value[:, :lanes], value[:, lanes:], half)
    from_rim = {
        0: dot(skip_weight[:, :depth], rims[:depth, :]),
        rows - 1: dot(skip_weight[:, 2 * depth :], rims[depth:, :]),
    }
    unsort = unsort_pick(width, clips)
    block = 3 * inner
    for row_phase in range(2):
        phases = []
        for column_phase in range(2):
            total = None
            for tap in range(2):
                sides = [
                    middle_field[
                        (row_phase + tap + at) * block
                        + column_phase * inner : (row_phase + tap + at) * block
                        + (column_phase + 2) * inner,
                        :,
                    ]
                    for at in range(rows // 2)
                ]
                part = dot(
                    phase_weight[
                        2 * row_phase + column_phase, :, tap * 2 * inner : (tap + 1) * 2 * inner
                    ],
                    jnp.concatenate(sides, axis=1),
                )
                total = part if total is None else total + part
            phases.append(total)
        for at in range(rows // 2):
            row = 2 * at + row_phase
            latent = field_ref[row * depth + channels : row * depth + 2 * channels, :].astype(F32)
            upper = jnp.concatenate([phase[:, at * lanes : (at + 1) * lanes] for phase in phases], axis=1)
            total = latent + mixed_ref[row] + upper
            if row in from_rim:
                total += from_rim[row]
            natural = dot(total.astype(BF16), unsort).astype(BF16)
            for clip in range(clips):
                out_ref[clip, row] = natural[:, clip * width : (clip + 1) * width]


def call(kernel, name, outputs, limit, scratch=(), flops=0, kept=True, inputs=None, aliases=None):
    shapes = [
        pltpu.VMEM(shape, dtype) if kept else jax.ShapeDtypeStruct(shape, dtype)
        for shape, dtype in outputs
    ]
    specs = {} if inputs is None else {"in_specs": inputs}
    return pl.pallas_call(
        kernel,
        out_shape=shapes,
        scratch_shapes=list(scratch),
        compiler_params=pltpu.CompilerParams(vmem_limit_bytes=limit * MIB),
        cost_estimate=pl.CostEstimate(flops=flops, bytes_accessed=1 << 20, transcendentals=0),
        name=name,
        input_output_aliases=aliases or {},
        **specs,
    )


def in_hbm(value):
    return pltpu.with_memory_space_constraint(value, pltpu.HBM)


def in_vmem(*values):
    return [pltpu.with_memory_space_constraint(value, pltpu.VMEM) for value in values]


def body(latents, in_weight, time_weight, mid_weight, up_weight):
    device_count = lax.axis_size("frames")
    bands = device_count // FRAMES
    offset = bands // 2
    band_of = lambda index: (index + offset) % bands
    frame_of = lambda index: (index + offset) // bands % FRAMES
    swap = lambda step, group, lowest: [
        pair
        for i in range(device_count)
        if group(i) % 2 == lowest and group(i) + 1 < (FRAMES if step == bands else bands)
        for j in [(i + step) % device_count]
        for pair in ((i, j), (j, i))
    ]
    inside, across = swap(1, band_of, 0), swap(1, band_of, 1)
    outer_frames, middle_frames = swap(bands, frame_of, 0), swap(bands, frame_of, 1)
    relayed_pairs = [(i, j) for i, j in outer_frames if abs(i - j) != bands and band_of(i) % 2 == 0]
    hops = [(i, i - offset + 1) for i, _ in relayed_pairs]
    relays = [(i - offset + 1, j) for i, j in relayed_pairs]
    outer_frames = [pair for pair in outer_frames if pair not in relayed_pairs]
    clips, rows, width, channels = latents.shape
    inner = mid_weight.shape[3]
    wide = clips * width
    depth = 3 * channels
    anywhere = pl.BlockSpec(memory_space=pl.ANY)
    whole = pl.BlockSpec(memory_space=pltpu.VMEM)
    turned = jnp.swapaxes(latents, 2, 3)

    inside_rim, across_rim, latent, in_rows = call(
        functools.partial(fetch_kernel, bands=bands),
        "fetch",
        [
            ((clips, channels, width), BF16),
            ((clips, channels, width), BF16),
            (turned.shape, BF16),
            ((3 * depth, channels), BF16),
        ],
        1,
        [pltpu.SemaphoreType.DMA((4,))],
        inputs=[anywhere, anywhere],
    )(in_hbm(turned), in_hbm(in_weight.reshape(3 * depth, channels)))
    inside_row = lax.ppermute(inside_rim, "frames", inside)
    across_row = lax.ppermute(across_rim, "frames", across)
    in_turned, field = call(
        prepare_kernel,
        "prepare",
        [((channels, 3 * depth), BF16), ((rows * depth, wide), BF16)],
        8,
        flops=2 * rows * wide * channels * wide,
        inputs=[whole] * 2,
    )(*in_vmem(latent, in_rows))
    (first,) = call(
        functools.partial(first_kernel, bands=bands),
        "first",
        [((rows, channels, wide), BF16)],
        8,
        [pltpu.VMEM((2 * depth, wide), BF16)],
        flops=2 * rows * wide * channels * 3 * depth,
        inputs=[whole] * 4,
    )(*in_vmem(inside_row, across_row, in_turned, field))
    hopped = lax.ppermute(first, "frames", hops)
    outer = lax.ppermute(first, "frames", outer_frames)
    middle = lax.ppermute(first, "frames", middle_frames)

    time_rows, mid_rows, up_rows, first = lax.optimization_barrier(
        (
            time_weight.reshape(depth, channels),
            mid_weight.reshape(3 * depth, inner),
            jnp.swapaxes(up_weight, 2, 3),
            first,
        )
    )
    time_turned, mid_turned, skip_weight, phase_weight = call(
        weights_kernel,
        "weights",
        [
            ((channels, depth), BF16),
            ((inner, 3 * depth), BF16),
            ((channels, 3 * depth), BF16),
            ((4, channels, 4 * inner), BF16),
        ],
        20,
        [
            pltpu.VMEM(time_rows.shape, BF16),
            pltpu.VMEM(mid_rows.shape, BF16),
            pltpu.VMEM(up_rows.shape, BF16),
            pltpu.SemaphoreType.DMA((2 + -(-3 * depth // 1024),)),
        ],
        flops=2 * 10**9,
        inputs=[anywhere] * 3,
    )(in_hbm(time_rows), in_hbm(mid_rows), in_hbm(up_rows))

    hopped, time_turned = lax.optimization_barrier((hopped, time_turned))
    relayed = lax.ppermute(hopped, "frames", relays)
    skip, inside_rows, across_rows = call(
        functools.partial(skip_kernel, bands=bands),
        "skip",
        [
            ((rows, channels, wide), BF16),
            ((2, channels, wide), BF16),
            ((2, channels, wide), BF16),
        ],
        8,
        flops=2 * rows * wide * depth * channels,
        inputs=[whole] * 5,
    )(*in_vmem(first, outer, middle, relayed, time_turned))
    from_across = lax.ppermute(across_rows, "frames", across)
    from_inside = lax.ppermute(inside_rows, "frames", inside)

    mixed, middle = call(
        lambda *refs: own_kernel(*refs, half=width // 2),
        "own_rows",
        [((rows, channels, wide), F32), ((inner, 2 * wide), F32)],
        16,
        [pltpu.VMEM((rows * depth, wide), BF16), pltpu.VMEM((depth, wide), BF16)],
        flops=2 * wide * depth * (3 * inner + (3 * rows - 2) * channels),
        inputs=[whole] * 4,
    )(*in_vmem(skip, inside_rows, mid_turned, skip_weight))

    (out,) = call(
        functools.partial(last_kernel, bands=bands),
        "last",
        [(turned.shape, BF16)],
        20,
        [
            pltpu.VMEM((depth, wide), BF16),
            pltpu.VMEM((depth, wide), BF16),
            pltpu.VMEM((depth, wide), BF16),
            pltpu.VMEM((2 * depth, wide), BF16),
            pltpu.VMEM((4 * 3 * inner, wide // 2), BF16),
        ],
        flops=2 * wide * (3 * depth * inner + 2 * depth * channels + rows * 4 * inner * channels),
        kept=False,
        inputs=[whole] * 8,
    )(
        *in_vmem(
            mixed, middle, from_inside, from_across, mid_turned, skip_weight, phase_weight, field
        ),
    )
    return jnp.swapaxes(out, 2, 3)


def solution(mesh):
    in_specs = (P("groups", "frames", None, None), P(), P(), P(), P())
    out_specs = P("groups", "frames", None, None)
    return jax.shard_map(body, mesh=mesh, in_specs=in_specs, out_specs=out_specs, check_vma=False)
```

```python
import functools

import jax
import jax.numpy as jnp
from jax import lax
from jax.experimental import pallas as pl
from jax.experimental.pallas import tpu as pltpu
from jax.sharding import PartitionSpec as P


FRAMES = 4
BF16 = jnp.bfloat16
F32 = jnp.float32
MIB = 1024 * 1024


def place(bands):
    index = lax.axis_index("frames") + bands // 2
    return lax.rem(index, bands), lax.rem(lax.div(index, bands), FRAMES)


def dot(left, right):
    return jnp.dot(left, right, preferred_element_type=F32)


def silu(value):
    return value / (1.0 + jnp.exp(-value))


def sort_pick(width, clips):
    wide, half = width * clips, width // 2
    source = lax.broadcasted_iota(jnp.int32, (wide, wide), 0)
    lane = lax.broadcasted_iota(jnp.int32, (wide, wide), 1)
    parity, clip, j = lane // (wide // 2), lane // half % clips, lane % half
    return (source == clip * width + 2 * j + parity).astype(BF16)


def unsort_pick(width, clips):
    wide, half = width * clips, width // 2
    source = lax.broadcasted_iota(jnp.int32, (wide, wide), 0)
    lane = lax.broadcasted_iota(jnp.int32, (wide, wide), 1)
    clip, column = lane // width, lane % width
    return (source == column % 2 * (wide // 2) + clip * half + column // 2).astype(BF16)


def from_left(value, half):
    lane = lax.broadcasted_iota(jnp.int32, (1, value.shape[1]), 1)
    return jnp.where(lane % half == 0, 0.0, pltpu.roll(value, 1, 1))


def from_right(value, half):
    width = value.shape[1]
    lane = lax.broadcasted_iota(jnp.int32, (1, width), 1)
    return jnp.where(lane % half == half - 1, 0.0, pltpu.roll(value, width - 1, 1))


def store_taps(field, base, even, odd, half):
    channels, lanes = even.shape
    e, o = even.astype(BF16), odd.astype(BF16)
    blocks = ((from_left(odd, half).astype(BF16), e), (e, o), (o, from_right(even, half).astype(BF16)))
    for tap, pair in enumerate(blocks):
        rows = slice(base + tap * channels, base + (tap + 1) * channels)
        field[rows, :lanes] = pair[0]
        field[rows, lanes:] = pair[1]


def store_row_taps(field, base, lane_base, value, half):
    channels, lanes = value.shape
    blocks = (from_left(value, half).astype(BF16), value.astype(BF16), from_right(value, half).astype(BF16))
    for tap, block in enumerate(blocks):
        field[base + tap * channels : base + (tap + 1) * channels, lane_base : lane_base + lanes] = block


def fetch_kernel(
    latent_hbm, weight_hbm, inside_ref, across_ref, latent_ref, weight_ref, sems, *, bands
):
    last = latent_hbm.shape[1] - 1
    odd = lax.rem(place(bands)[0], 2)
    pieces = [
        (latent_hbm.at[:, last * odd], across_ref),
        (latent_hbm.at[:, last * (1 - odd)], inside_ref),
        (latent_hbm, latent_ref),
        (weight_hbm, weight_ref),
    ]
    gets = [
        pltpu.make_async_copy(source, target, sems.at[n])
        for n, (source, target) in enumerate(pieces)
    ]
    for get in gets:
        get.start()
    for get in gets:
        get.wait()


def prepare_kernel(latent_ref, weight_ref, turned_ref, field_ref):
    clips, rows, channels, width = latent_ref.shape
    pick = sort_pick(width, clips)
    for row in range(rows):
        value = dot(jnp.concatenate([latent_ref[clip, row] for clip in range(clips)], axis=1), pick)
        lanes = value.shape[1] // 2
        store_taps(field_ref, row * 3 * channels, value[:, :lanes], value[:, lanes:], width // 2)
    turned_ref[...] = weight_ref[...].T


def first_kernel(inside_ref, across_ref, turned_ref, field_ref, first_ref, rim, *, bands):
    clips, channels, width = inside_ref.shape
    depth = 3 * channels
    rows = first_ref.shape[0]
    pick = sort_pick(width, clips)
    odd = lax.rem(place(bands)[0], 2) == 1
    for at in range(2):
        one, other = (inside_ref, across_ref) if at == 0 else (across_ref, inside_ref)
        blocks = [jnp.where(odd, one[clip], other[clip]) for clip in range(clips)]
        value = dot(jnp.concatenate(blocks, axis=1), pick)
        lanes = value.shape[1] // 2
        store_taps(rim, at * depth, value[:, :lanes], value[:, lanes:], width // 2)
    for row in list(range(1, rows - 1)) + [0, rows - 1]:
        start, stop = max(row - 1, 0), min(row + 2, rows)
        total = dot(
            turned_ref[:, (start - row + 1) * depth : (stop - row + 1) * depth],
            field_ref[start * depth : stop * depth, :],
        )
        if row == 0:
            total += dot(turned_ref[:, :depth], rim[:depth, :])
        if row == rows - 1:
            total += dot(turned_ref[:, 2 * depth :], rim[depth:, :])
        first_ref[row] = silu(total).astype(BF16)


def weights_kernel(
    time_hbm, mid_hbm, up_hbm, time_out, mid_out, skip_out, phase_out,
    time_rows, mid_rows, up_rows, sems,
):
    taps, inner = mid_rows.shape
    channels = up_rows.shape[2]
    cuts = list(range(0, taps, 1024)) + [taps]
    pieces = [(time_hbm, time_rows)]
    pieces += [(mid_hbm.at[a:b], mid_rows.at[a:b]) for a, b in zip(cuts, cuts[1:])]
    pieces += [(up_hbm, up_rows)]
    gets = [
        pltpu.make_async_copy(source, target, sems.at[n])
        for n, (source, target) in enumerate(pieces)
    ]
    for get in gets:
        get.start()
    gets[0].wait()
    time_out[...] = time_rows[...].T
    for get, a, b in zip(gets[1:-1], cuts, cuts[1:]):
        get.wait()
        mid_out[:, a:b] = mid_rows[a:b, :].T
    gets[-1].wait()
    skip_out[...] = jnp.concatenate(
        [up_rows[dr, dc, :, :channels] for dr in range(3) for dc in range(3)], axis=1
    )
    taps = [[up_rows[dr, dc, :, channels:].astype(F32) for dc in range(3)] for dr in range(3)]
    groups = ((lambda t: t[0], lambda t: t[1] + t[2]), (lambda t: t[0] + t[1], lambda t: t[2]))
    for row_phase in range(2):
        for row_tap in range(2):
            merged = [groups[row_phase][row_tap]([taps[dr][dc] for dr in range(3)]) for dc in range(3)]
            for column_phase in range(2):
                for column_tap in range(2):
                    value = groups[column_phase][column_tap](merged)
                    start = (2 * row_tap + column_tap) * inner
                    phase_out[2 * row_phase + column_phase, :, start : start + inner] = value.astype(
                        BF16
                    )


def skip_kernel(
    first_ref, middle_ref, outer_ref, relayed_ref, weight_ref, skip_ref, inside_ref, across_ref,
    *, bands
):
    rows, _, wide = skip_ref.shape
    lanes = wide // 2
    band, frame = place(bands)
    odd_band, odd_frame = lax.rem(band, 2) == 1, lax.rem(frame, 2) == 1
    is_relayed = jnp.logical_and(jnp.logical_and(frame < 2, band < bands // 2), lax.rem(band, 2) == 0)
    skips = []
    for row in range(rows):
        centre, middle = first_ref[row], middle_ref[row]
        outer = jnp.where(is_relayed, relayed_ref[row], outer_ref[row])
        before = jnp.where(odd_frame, outer, middle)
        after = jnp.where(odd_frame, middle, outer)
        stacked = jnp.concatenate([before, centre, after], axis=0)
        skip = (centre.astype(F32) + dot(weight_ref[...], stacked)).astype(BF16)
        skip_ref[row] = skip
        skips.append(skip)
    inside_ref[0] = jnp.where(odd_band, skips[0], skips[-1])
    across_ref[0] = jnp.where(odd_band, skips[-1], skips[0])
    for pooled_row in range(rows // 2):
        sums = skips[2 * pooled_row].astype(F32) + skips[2 * pooled_row + 1].astype(F32)
        pooled = ((sums[:, :lanes] + sums[:, lanes:]) * 0.25).astype(BF16)
        span = slice(pooled_row * lanes, (pooled_row + 1) * lanes)
        inside_ref[1, :, span] = pooled
        across_ref[1, :, span] = pooled


def own_kernel(skip_ref, pair_ref, mid_ref, skip_weight, mixed_ref, middle_ref, field, pooled, *, half):
    rows, channels, wide = skip_ref.shape
    lanes = wide // 2
    depth = 3 * channels
    for at in range(2):
        row = pair_ref[1, :, at * lanes : (at + 1) * lanes].astype(F32)
        store_row_taps(pooled, 0, at * lanes, row, half)
    for row in range(rows):
        value = skip_ref[row].astype(F32)
        store_taps(field, row * depth, value[:, :lanes], value[:, lanes:], half)
    parts = [dot(mid_ref[:, dr * depth : (dr + 1) * depth], pooled[...]) for dr in range(3)]
    middle_ref[:, :lanes] = parts[2][:, :lanes]
    middle_ref[:, lanes : 2 * lanes] = parts[2][:, lanes:] + parts[1][:, :lanes]
    middle_ref[:, 2 * lanes : 3 * lanes] = parts[1][:, lanes:] + parts[0][:, :lanes]
    middle_ref[:, 3 * lanes :] = parts[0][:, lanes:]
    for row in range(rows):
        first, last = max(row - 1, 0), min(row + 2, rows)
        mixed_ref[row] = dot(
            skip_weight[:, (first - row + 1) * depth : (last - row + 1) * depth],
            field[first * depth : last * depth, :],
        )


def last_kernel(
    mixed_ref, middle_ref, inside_ref, across_ref, mid_ref, skip_weight, phase_weight, field_ref,
    out_ref, low_field, high_field, cross_field, rims, middle_field, *, bands
):
    rows, channels, wide = mixed_ref.shape
    clips, _, _, width = out_ref.shape
    half, lanes = width // 2, wide // 2
    inner = mid_ref.shape[0]
    depth = 3 * channels

    band = place(bands)[0]
    odd = lax.rem(band, 2) == 1
    lows = [jnp.where(odd, inside_ref[at], across_ref[at]) for at in range(2)]
    highs = [jnp.where(odd, across_ref[at], inside_ref[at]) for at in range(2)]
    for target, pair, inward in ((low_field, lows[1], 1), (high_field, highs[1], 0)):
        for at in range(2):
            row = pair[:, at * lanes : (at + 1) * lanes].astype(F32)
            store_row_taps(target, 0, at * lanes, row, half)
        cross_field[:, (1 - inward) * lanes : (2 - inward) * lanes] = target[
            :, inward * lanes : (inward + 1) * lanes
        ]
    above = dot(mid_ref[:, :depth], low_field[...])
    cross = dot(mid_ref[:, depth : 2 * depth], cross_field[...])
    below = dot(mid_ref[:, 2 * depth :], high_field[...])
    middles = [
        middle_ref[:, :lanes] + above[:, :lanes] + cross[:, :lanes],
        middle_ref[:, lanes : 2 * lanes] + above[:, lanes:],
        middle_ref[:, 2 * lanes : 3 * lanes] + below[:, :lanes],
        middle_ref[:, 3 * lanes :] + below[:, lanes:] + cross[:, lanes:],
    ]
    kept = (band != 0, None, None, band != bands - 1)
    for at, (value, keep) in enumerate(zip(middles, kept)):
        value = silu(value)
        if keep is not None:
            value = jnp.where(keep, value, 0.0)
        store_row_taps(middle_field, at * 3 * inner, 0, value.astype(BF16).astype(F32), half)

    for at, row in enumerate((lows[0], highs[0])):
        value = row.astype(F32)
        store_taps(rims, at * depth, value[:, :lanes], value[:, lanes:], half)
    from_rim = {
        0: dot(skip_weight[:, :depth], rims[:depth, :]),
        rows - 1: dot(skip_weight[:, 2 * depth :], rims[depth:, :]),
    }
    unsort = unsort_pick(width, clips)
    block = 3 * inner
    for row_phase in range(2):
        phases = []
        for column_phase in range(2):
            total = None
            for tap in range(2):
                sides = [
                    middle_field[
                        (row_phase + tap + at) * block
                        + column_phase * inner : (row_phase + tap + at) * block
                        + (column_phase + 2) * inner,
                        :,
                    ]
                    for at in range(rows // 2)
                ]
                part = dot(
                    phase_weight[
                        2 * row_phase + column_phase, :, tap * 2 * inner : (tap + 1) * 2 * inner
                    ],
                    jnp.concatenate(sides, axis=1),
                )
                total = part if total is None else total + part
            phases.append(total)
        for at in range(rows // 2):
            row = 2 * at + row_phase
            latent = field_ref[row * depth + channels : row * depth + 2 * channels, :].astype(F32)
            upper = jnp.concatenate([phase[:, at * lanes : (at + 1) * lanes] for phase in phases], axis=1)
            total = latent + mixed_ref[row] + upper
            if row in from_rim:
                total += from_rim[row]
            natural = dot(total.astype(BF16), unsort).astype(BF16)
            for clip in range(clips):
                out_ref[clip, row] = natural[:, clip * width : (clip + 1) * width]


def call(kernel, name, outputs, limit, scratch=(), flops=0, kept=True, inputs=None, aliases=None):
    shapes = [
        pltpu.VMEM(shape, dtype) if kept else jax.ShapeDtypeStruct(shape, dtype)
        for shape, dtype in outputs
    ]
    specs = {} if inputs is None else {"in_specs": inputs}
    return pl.pallas_call(
        kernel,
        out_shape=shapes,
        scratch_shapes=list(scratch),
        compiler_params=pltpu.CompilerParams(vmem_limit_bytes=limit * MIB),
        cost_estimate=pl.CostEstimate(flops=flops, bytes_accessed=1 << 20, transcendentals=0),
        name=name,
        input_output_aliases=aliases or {},
        **specs,
    )


def in_hbm(value):
    return pltpu.with_memory_space_constraint(value, pltpu.HBM)


def in_vmem(*values):
    return [pltpu.with_memory_space_constraint(value, pltpu.VMEM) for value in values]


def body(latents, in_weight, time_weight, mid_weight, up_weight):
    device_count = lax.axis_size("frames")
    bands = device_count // FRAMES
    offset = bands // 2
    band_of = lambda index: (index + offset) % bands
    frame_of = lambda index: (index + offset) // bands % FRAMES
    swap = lambda step, group, lowest: [
        pair
        for i in range(device_count)
        if group(i) % 2 == lowest and group(i) + 1 < (FRAMES if step == bands else bands)
        for j in [(i + step) % device_count]
        for pair in ((i, j), (j, i))
    ]
    inside, across = swap(1, band_of, 0), swap(1, band_of, 1)
    outer_frames, middle_frames = swap(bands, frame_of, 0), swap(bands, frame_of, 1)
    relayed_pairs = [(i, j) for i, j in outer_frames if abs(i - j) != bands and band_of(i) % 2 == 0]
    hops = [(i, i - offset + 1) for i, _ in relayed_pairs]
    relays = [(i - offset + 1, j) for i, j in relayed_pairs]
    outer_frames = [pair for pair in outer_frames if pair not in relayed_pairs]
    clips, rows, width, channels = latents.shape
    inner = mid_weight.shape[3]
    wide = clips * width
    depth = 3 * channels
    anywhere = pl.BlockSpec(memory_space=pl.ANY)
    whole = pl.BlockSpec(memory_space=pltpu.VMEM)
    turned = jnp.swapaxes(latents, 2, 3)

    inside_rim, across_rim, latent, in_rows = call(
        functools.partial(fetch_kernel, bands=bands),
        "fetch",
        [
            ((clips, channels, width), BF16),
            ((clips, channels, width), BF16),
            (turned.shape, BF16),
            ((3 * depth, channels), BF16),
        ],
        1,
        [pltpu.SemaphoreType.DMA((4,))],
        inputs=[anywhere, anywhere],
    )(in_hbm(turned), in_hbm(in_weight.reshape(3 * depth, channels)))
    inside_row = lax.ppermute(inside_rim, "frames", inside)
    across_row = lax.ppermute(across_rim, "frames", across)
    in_turned, field = call(
        prepare_kernel,
        "prepare",
        [((channels, 3 * depth), BF16), ((rows * depth, wide), BF16)],
        8,
        flops=2 * rows * wide * channels * wide,
        inputs=[whole] * 2,
    )(*in_vmem(latent, in_rows))
    (first,) = call(
        functools.partial(first_kernel, bands=bands),
        "first",
        [((rows, channels, wide), BF16)],
        8,
        [pltpu.VMEM((2 * depth, wide), BF16)],
        flops=2 * rows * wide * channels * 3 * depth,
        inputs=[whole] * 4,
    )(*in_vmem(inside_row, across_row, in_turned, field))
    hopped = lax.ppermute(first, "frames", hops)
    middle = lax.ppermute(first, "frames", middle_frames)
    outer = lax.ppermute(first, "frames", outer_frames)

    time_rows, mid_rows, up_rows, first = lax.optimization_barrier(
        (
            time_weight.reshape(depth, channels),
            mid_weight.reshape(3 * depth, inner),
            jnp.swapaxes(up_weight, 2, 3),
            first,
        )
    )
    time_turned, mid_turned, skip_weight, phase_weight = call(
        weights_kernel,
        "weights",
        [
            ((channels, depth), BF16),
            ((inner, 3 * depth), BF16),
            ((channels, 3 * depth), BF16),
            ((4, channels, 4 * inner), BF16),
        ],
        20,
        [
            pltpu.VMEM(time_rows.shape, BF16),
            pltpu.VMEM(mid_rows.shape, BF16),
            pltpu.VMEM(up_rows.shape, BF16),
            pltpu.SemaphoreType.DMA((2 + -(-3 * depth // 1024),)),
        ],
        flops=2 * 10**9,
        inputs=[anywhere] * 3,
    )(in_hbm(time_rows), in_hbm(mid_rows), in_hbm(up_rows))

    hopped, time_turned = lax.optimization_barrier((hopped, time_turned))
    relayed = lax.ppermute(hopped, "frames", relays)
    skip, inside_rows, across_rows = call(
        functools.partial(skip_kernel, bands=bands),
        "skip",
        [
            ((rows, channels, wide), BF16),
            ((2, channels, wide), BF16),
            ((2, channels, wide), BF16),
        ],
        8,
        flops=2 * rows * wide * depth * channels,
        inputs=[whole] * 5,
    )(*in_vmem(first, middle, outer, relayed, time_turned))
    from_across = lax.ppermute(across_rows, "frames", across)
    from_inside = lax.ppermute(inside_rows, "frames", inside)

    mixed, middle = call(
        lambda *refs: own_kernel(*refs, half=width // 2),
        "own_rows",
        [((rows, channels, wide), F32), ((inner, 2 * wide), F32)],
        16,
        [pltpu.VMEM((rows * depth, wide), BF16), pltpu.VMEM((depth, wide), BF16)],
        flops=2 * wide * depth * (3 * inner + (3 * rows - 2) * channels),
        inputs=[whole] * 4,
    )(*in_vmem(skip, inside_rows, mid_turned, skip_weight))

    (out,) = call(
        functools.partial(last_kernel, bands=bands),
        "last",
        [(turned.shape, BF16)],
        20,
        [
            pltpu.VMEM((depth, wide), BF16),
            pltpu.VMEM((depth, wide), BF16),
            pltpu.VMEM((depth, wide), BF16),
            pltpu.VMEM((2 * depth, wide), BF16),
            pltpu.VMEM((4 * 3 * inner, wide // 2), BF16),
        ],
        flops=2 * wide * (3 * depth * inner + 2 * depth * channels + rows * 4 * inner * channels),
        kept=False,
        inputs=[whole] * 8,
    )(
        *in_vmem(
            mixed, middle, from_inside, from_across, mid_turned, skip_weight, phase_weight, field
        ),
    )
    return jnp.swapaxes(out, 2, 3)


def solution(mesh):
    in_specs = (P("groups", "frames", None, None), P(), P(), P(), P())
    out_specs = P("groups", "frames", None, None)
    return jax.shard_map(body, mesh=mesh, in_specs=in_specs, out_specs=out_specs, check_vma=False)
```

```python
import functools

import jax
import jax.numpy as jnp
from jax import lax
from jax.experimental import pallas as pl
from jax.experimental.pallas import tpu as pltpu
from jax.sharding import PartitionSpec as P


FRAMES = 4
BF16 = jnp.bfloat16
F32 = jnp.float32
MIB = 1024 * 1024


def place(bands):
    index = lax.axis_index("frames") + bands // 2
    return lax.rem(index, bands), lax.rem(lax.div(index, bands), FRAMES)


def dot(left, right):
    return jnp.dot(left, right, preferred_element_type=F32)


def silu(value):
    return value / (1.0 + jnp.exp(-value))


def sort_pick(width, clips):
    wide, half = width * clips, width // 2
    source = lax.broadcasted_iota(jnp.int32, (wide, wide), 0)
    lane = lax.broadcasted_iota(jnp.int32, (wide, wide), 1)
    parity, clip, j = lane // (wide // 2), lane // half % clips, lane % half
    return (source == clip * width + 2 * j + parity).astype(BF16)


def unsort_pick(width, clips):
    wide, half = width * clips, width // 2
    source = lax.broadcasted_iota(jnp.int32, (wide, wide), 0)
    lane = lax.broadcasted_iota(jnp.int32, (wide, wide), 1)
    clip, column = lane // width, lane % width
    return (source == column % 2 * (wide // 2) + clip * half + column // 2).astype(BF16)


def from_left(value, half):
    lane = lax.broadcasted_iota(jnp.int32, (1, value.shape[1]), 1)
    return jnp.where(lane % half == 0, 0.0, pltpu.roll(value, 1, 1))


def from_right(value, half):
    width = value.shape[1]
    lane = lax.broadcasted_iota(jnp.int32, (1, width), 1)
    return jnp.where(lane % half == half - 1, 0.0, pltpu.roll(value, width - 1, 1))


def store_taps(field, base, even, odd, half):
    channels, lanes = even.shape
    e, o = even.astype(BF16), odd.astype(BF16)
    blocks = ((from_left(odd, half).astype(BF16), e), (e, o), (o, from_right(even, half).astype(BF16)))
    for tap, pair in enumerate(blocks):
        rows = slice(base + tap * channels, base + (tap + 1) * channels)
        field[rows, :lanes] = pair[0]
        field[rows, lanes:] = pair[1]


def store_row_taps(field, base, lane_base, value, half):
    channels, lanes = value.shape
    blocks = (from_left(value, half).astype(BF16), value.astype(BF16), from_right(value, half).astype(BF16))
    for tap, block in enumerate(blocks):
        field[base + tap * channels : base + (tap + 1) * channels, lane_base : lane_base + lanes] = block


def fetch_kernel(
    latent_hbm, weight_hbm, inside_ref, across_ref, latent_ref, weight_ref, sems, *, bands
):
    last = latent_hbm.shape[1] - 1
    odd = lax.rem(place(bands)[0], 2)
    pieces = [
        (latent_hbm.at[:, last * odd], across_ref),
        (latent_hbm.at[:, last * (1 - odd)], inside_ref),
        (latent_hbm, latent_ref),
        (weight_hbm, weight_ref),
    ]
    gets = [
        pltpu.make_async_copy(source, target, sems.at[n])
        for n, (source, target) in enumerate(pieces)
    ]
    for get in gets:
        get.start()
    for get in gets:
        get.wait()


def prepare_kernel(latent_ref, weight_ref, turned_ref, field_ref):
    clips, rows, channels, width = latent_ref.shape
    pick = sort_pick(width, clips)
    for row in range(rows):
        value = dot(jnp.concatenate([latent_ref[clip, row] for clip in range(clips)], axis=1), pick)
        lanes = value.shape[1] // 2
        store_taps(field_ref, row * 3 * channels, value[:, :lanes], value[:, lanes:], width // 2)
    turned_ref[...] = weight_ref[...].T


def first_kernel(inside_ref, across_ref, turned_ref, field_ref, first_ref, rim, *, bands):
    clips, channels, width = inside_ref.shape
    depth = 3 * channels
    rows = first_ref.shape[0]
    pick = sort_pick(width, clips)
    odd = lax.rem(place(bands)[0], 2) == 1
    for at in range(2):
        one, other = (inside_ref, across_ref) if at == 0 else (across_ref, inside_ref)
        blocks = [jnp.where(odd, one[clip], other[clip]) for clip in range(clips)]
        value = dot(jnp.concatenate(blocks, axis=1), pick)
        lanes = value.shape[1] // 2
        store_taps(rim, at * depth, value[:, :lanes], value[:, lanes:], width // 2)
    for row in list(range(1, rows - 1)) + [0, rows - 1]:
        start, stop = max(row - 1, 0), min(row + 2, rows)
        total = dot(
            turned_ref[:, (start - row + 1) * depth : (stop - row + 1) * depth],
            field_ref[start * depth : stop * depth, :],
        )
        if row == 0:
            total += dot(turned_ref[:, :depth], rim[:depth, :])
        if row == rows - 1:
            total += dot(turned_ref[:, 2 * depth :], rim[depth:, :])
        first_ref[row] = silu(total).astype(BF16)


def weights_kernel(
    time_hbm, mid_hbm, up_hbm, time_out, mid_out, skip_out, phase_out,
    time_rows, mid_rows, up_rows, sems,
):
    taps, inner = mid_rows.shape
    channels = up_rows.shape[2]
    cuts = list(range(0, taps, 1024)) + [taps]
    pieces = [(time_hbm, time_rows)]
    pieces += [(mid_hbm.at[a:b], mid_rows.at[a:b]) for a, b in zip(cuts, cuts[1:])]
    pieces += [(up_hbm, up_rows)]
    gets = [
        pltpu.make_async_copy(source, target, sems.at[n])
        for n, (source, target) in enumerate(pieces)
    ]
    for get in gets:
        get.start()
    gets[0].wait()
    time_out[...] = time_rows[...].T
    for get, a, b in zip(gets[1:-1], cuts, cuts[1:]):
        get.wait()
        mid_out[:, a:b] = mid_rows[a:b, :].T
    gets[-1].wait()
    skip_out[...] = jnp.concatenate(
        [up_rows[dr, dc, :, :channels] for dr in range(3) for dc in range(3)], axis=1
    )
    taps = [[up_rows[dr, dc, :, channels:].astype(F32) for dc in range(3)] for dr in range(3)]
    groups = ((lambda t: t[0], lambda t: t[1] + t[2]), (lambda t: t[0] + t[1], lambda t: t[2]))
    for row_phase in range(2):
        for row_tap in range(2):
            merged = [groups[row_phase][row_tap]([taps[dr][dc] for dr in range(3)]) for dc in range(3)]
            for column_phase in range(2):
                for column_tap in range(2):
                    value = groups[column_phase][column_tap](merged)
                    start = (2 * row_tap + column_tap) * inner
                    phase_out[2 * row_phase + column_phase, :, start : start + inner] = value.astype(
                        BF16
                    )


def skip_kernel(
    first_ref, second_swap, first_swap, relayed_ref, weight_ref, skip_ref, inside_ref, across_ref,
    *, bands
):
    rows, _, wide = skip_ref.shape
    lanes = wide // 2
    band, frame = place(bands)
    odd_band, odd_frame = lax.rem(band, 2) == 1, lax.rem(frame, 2) == 1
    is_relayed = jnp.logical_and(jnp.logical_and(frame < 2, band < bands // 2), lax.rem(band, 2) == 0)
    upper = band < bands // 2
    first_is_before = upper == odd_frame
    is_host = jnp.logical_and(
        jnp.logical_not(upper), jnp.logical_or(frame == 0, frame == FRAMES - 1)
    )
    skips = []
    for row in range(rows):
        centre, second = first_ref[row], second_swap[row]
        first = jnp.where(is_host, jnp.zeros((), BF16), first_swap[row])
        first = jnp.where(is_relayed, relayed_ref[row], first)
        before = jnp.where(first_is_before, first, second)
        after = jnp.where(first_is_before, second, first)
        stacked = jnp.concatenate([before, centre, after], axis=0)
        skip = (centre.astype(F32) + dot(weight_ref[...], stacked)).astype(BF16)
        skip_ref[row] = skip
        skips.append(skip)
    inside_ref[0] = jnp.where(odd_band, skips[0], skips[-1])
    across_ref[0] = jnp.where(odd_band, skips[-1], skips[0])
    for pooled_row in range(rows // 2):
        sums = skips[2 * pooled_row].astype(F32) + skips[2 * pooled_row + 1].astype(F32)
        pooled = ((sums[:, :lanes] + sums[:, lanes:]) * 0.25).astype(BF16)
        span = slice(pooled_row * lanes, (pooled_row + 1) * lanes)
        inside_ref[1, :, span] = pooled
        across_ref[1, :, span] = pooled


def own_kernel(skip_ref, pair_ref, mid_ref, skip_weight, mixed_ref, middle_ref, field, pooled, *, half):
    rows, channels, wide = skip_ref.shape
    lanes = wide // 2
    depth = 3 * channels
    for at in range(2):
        row = pair_ref[1, :, at * lanes : (at + 1) * lanes].astype(F32)
        store_row_taps(pooled, 0, at * lanes, row, half)
    for row in range(rows):
        value = skip_ref[row].astype(F32)
        store_taps(field, row * depth, value[:, :lanes], value[:, lanes:], half)
    parts = [dot(mid_ref[:, dr * depth : (dr + 1) * depth], pooled[...]) for dr in range(3)]
    middle_ref[:, :lanes] = parts[2][:, :lanes]
    middle_ref[:, lanes : 2 * lanes] = parts[2][:, lanes:] + parts[1][:, :lanes]
    middle_ref[:, 2 * lanes : 3 * lanes] = parts[1][:, lanes:] + parts[0][:, :lanes]
    middle_ref[:, 3 * lanes :] = parts[0][:, lanes:]
    for row in range(rows):
        first, last = max(row - 1, 0), min(row + 2, rows)
        mixed_ref[row] = dot(
            skip_weight[:, (first - row + 1) * depth : (last - row + 1) * depth],
            field[first * depth : last * depth, :],
        )


def last_kernel(
    mixed_ref, middle_ref, inside_ref, across_ref, mid_ref, skip_weight, phase_weight, field_ref,
    out_ref, low_field, high_field, cross_field, rims, middle_field, *, bands
):
    rows, channels, wide = mixed_ref.shape
    clips, _, _, width = out_ref.shape
    half, lanes = width // 2, wide // 2
    inner = mid_ref.shape[0]
    depth = 3 * channels

    band = place(bands)[0]
    odd = lax.rem(band, 2) == 1
    lows = [jnp.where(odd, inside_ref[at], across_ref[at]) for at in range(2)]
    highs = [jnp.where(odd, across_ref[at], inside_ref[at]) for at in range(2)]
    for target, pair, inward in ((low_field, lows[1], 1), (high_field, highs[1], 0)):
        for at in range(2):
            row = pair[:, at * lanes : (at + 1) * lanes].astype(F32)
            store_row_taps(target, 0, at * lanes, row, half)
        cross_field[:, (1 - inward) * lanes : (2 - inward) * lanes] = target[
            :, inward * lanes : (inward + 1) * lanes
        ]
    above = dot(mid_ref[:, :depth], low_field[...])
    cross = dot(mid_ref[:, depth : 2 * depth], cross_field[...])
    below = dot(mid_ref[:, 2 * depth :], high_field[...])
    middles = [
        middle_ref[:, :lanes] + above[:, :lanes] + cross[:, :lanes],
        middle_ref[:, lanes : 2 * lanes] + above[:, lanes:],
        middle_ref[:, 2 * lanes : 3 * lanes] + below[:, :lanes],
        middle_ref[:, 3 * lanes :] + below[:, lanes:] + cross[:, lanes:],
    ]
    kept = (band != 0, None, None, band != bands - 1)
    for at, (value, keep) in enumerate(zip(middles, kept)):
        value = silu(value)
        if keep is not None:
            value = jnp.where(keep, value, 0.0)
        store_row_taps(middle_field, at * 3 * inner, 0, value.astype(BF16).astype(F32), half)

    for at, row in enumerate((lows[0], highs[0])):
        value = row.astype(F32)
        store_taps(rims, at * depth, value[:, :lanes], value[:, lanes:], half)
    from_rim = {
        0: dot(skip_weight[:, :depth], rims[:depth, :]),
        rows - 1: dot(skip_weight[:, 2 * depth :], rims[depth:, :]),
    }
    unsort = unsort_pick(width, clips)
    block = 3 * inner
    for row_phase in range(2):
        phases = []
        for column_phase in range(2):
            total = None
            for tap in range(2):
                sides = [
                    middle_field[
                        (row_phase + tap + at) * block
                        + column_phase * inner : (row_phase + tap + at) * block
                        + (column_phase + 2) * inner,
                        :,
                    ]
                    for at in range(rows // 2)
                ]
                part = dot(
                    phase_weight[
                        2 * row_phase + column_phase, :, tap * 2 * inner : (tap + 1) * 2 * inner
                    ],
                    jnp.concatenate(sides, axis=1),
                )
                total = part if total is None else total + part
            phases.append(total)
        for at in range(rows // 2):
            row = 2 * at + row_phase
            latent = field_ref[row * depth + channels : row * depth + 2 * channels, :].astype(F32)
            upper = jnp.concatenate([phase[:, at * lanes : (at + 1) * lanes] for phase in phases], axis=1)
            total = latent + mixed_ref[row] + upper
            if row in from_rim:
                total += from_rim[row]
            natural = dot(total.astype(BF16), unsort).astype(BF16)
            for clip in range(clips):
                out_ref[clip, row] = natural[:, clip * width : (clip + 1) * width]


def call(kernel, name, outputs, limit, scratch=(), flops=0, kept=True, inputs=None, aliases=None):
    shapes = [
        pltpu.VMEM(shape, dtype) if kept else jax.ShapeDtypeStruct(shape, dtype)
        for shape, dtype in outputs
    ]
    specs = {} if inputs is None else {"in_specs": inputs}
    return pl.pallas_call(
        kernel,
        out_shape=shapes,
        scratch_shapes=list(scratch),
        compiler_params=pltpu.CompilerParams(vmem_limit_bytes=limit * MIB),
        cost_estimate=pl.CostEstimate(flops=flops, bytes_accessed=1 << 20, transcendentals=0),
        name=name,
        input_output_aliases=aliases or {},
        **specs,
    )


def in_hbm(value):
    return pltpu.with_memory_space_constraint(value, pltpu.HBM)


def in_vmem(*values):
    return [pltpu.with_memory_space_constraint(value, pltpu.VMEM) for value in values]


def body(latents, in_weight, time_weight, mid_weight, up_weight):
    device_count = lax.axis_size("frames")
    bands = device_count // FRAMES
    offset = bands // 2
    band_of = lambda index: (index + offset) % bands
    frame_of = lambda index: (index + offset) // bands % FRAMES
    swap = lambda step, group, lowest: [
        pair
        for i in range(device_count)
        if group(i) % 2 == lowest and group(i) + 1 < (FRAMES if step == bands else bands)
        for j in [(i + step) % device_count]
        for pair in ((i, j), (j, i))
    ]
    inside, across = swap(1, band_of, 0), swap(1, band_of, 1)
    outer_frames, middle_frames = swap(bands, frame_of, 0), swap(bands, frame_of, 1)
    relayed_pairs = [(i, j) for i, j in outer_frames if abs(i - j) != bands and band_of(i) % 2 == 0]
    hops = [(i, i - offset + 1) for i, _ in relayed_pairs]
    relays = [(i - offset + 1, j) for i, j in relayed_pairs]
    outer_frames = [pair for pair in outer_frames if pair not in relayed_pairs]
    clips, rows, width, channels = latents.shape
    inner = mid_weight.shape[3]
    wide = clips * width
    depth = 3 * channels
    anywhere = pl.BlockSpec(memory_space=pl.ANY)
    whole = pl.BlockSpec(memory_space=pltpu.VMEM)
    turned = jnp.swapaxes(latents, 2, 3)

    inside_rim, across_rim, latent, in_rows = call(
        functools.partial(fetch_kernel, bands=bands),
        "fetch",
        [
            ((clips, channels, width), BF16),
            ((clips, channels, width), BF16),
            (turned.shape, BF16),
            ((3 * depth, channels), BF16),
        ],
        1,
        [pltpu.SemaphoreType.DMA((4,))],
        inputs=[anywhere, anywhere],
    )(in_hbm(turned), in_hbm(in_weight.reshape(3 * depth, channels)))
    inside_row = lax.ppermute(inside_rim, "frames", inside)
    across_row = lax.ppermute(across_rim, "frames", across)
    in_turned, field = call(
        prepare_kernel,
        "prepare",
        [((channels, 3 * depth), BF16), ((rows * depth, wide), BF16)],
        8,
        flops=2 * rows * wide * channels * wide,
        inputs=[whole] * 2,
    )(*in_vmem(latent, in_rows))
    (first,) = call(
        functools.partial(first_kernel, bands=bands),
        "first",
        [((rows, channels, wide), BF16)],
        8,
        [pltpu.VMEM((2 * depth, wide), BF16)],
        flops=2 * rows * wide * channels * 3 * depth,
        inputs=[whole] * 4,
    )(*in_vmem(inside_row, across_row, in_turned, field))
    of_bands = lambda pairs, upper: [pair for pair in pairs if (band_of(pair[0]) < offset) == upper]
    first_pairs = of_bands(outer_frames, True) + of_bands(middle_frames, False) + hops
    second_pairs = of_bands(middle_frames, True) + of_bands(outer_frames, False)
    first_swap = lax.ppermute(first, "frames", first_pairs)
    second_swap = lax.ppermute(first, "frames", second_pairs)

    time_rows, mid_rows, up_rows, first = lax.optimization_barrier(
        (
            time_weight.reshape(depth, channels),
            mid_weight.reshape(3 * depth, inner),
            jnp.swapaxes(up_weight, 2, 3),
            first,
        )
    )
    time_turned, mid_turned, skip_weight, phase_weight = call(
        weights_kernel,
        "weights",
        [
            ((channels, depth), BF16),
            ((inner, 3 * depth), BF16),
            ((channels, 3 * depth), BF16),
            ((4, channels, 4 * inner), BF16),
        ],
        20,
        [
            pltpu.VMEM(time_rows.shape, BF16),
            pltpu.VMEM(mid_rows.shape, BF16),
            pltpu.VMEM(up_rows.shape, BF16),
            pltpu.SemaphoreType.DMA((2 + -(-3 * depth // 1024),)),
        ],
        flops=2 * 10**9,
        inputs=[anywhere] * 3,
    )(in_hbm(time_rows), in_hbm(mid_rows), in_hbm(up_rows))

    hopped, time_turned = lax.optimization_barrier((first_swap, time_turned))
    relayed = lax.ppermute(hopped, "frames", relays)
    skip, inside_rows, across_rows = call(
        functools.partial(skip_kernel, bands=bands),
        "skip",
        [
            ((rows, channels, wide), BF16),
            ((2, channels, wide), BF16),
            ((2, channels, wide), BF16),
        ],
        8,
        flops=2 * rows * wide * depth * channels,
        inputs=[whole] * 5,
    )(*in_vmem(first, second_swap, first_swap, relayed, time_turned))
    from_across = lax.ppermute(across_rows, "frames", across)
    from_inside = lax.ppermute(inside_rows, "frames", inside)

    mixed, middle = call(
        lambda *refs: own_kernel(*refs, half=width // 2),
        "own_rows",
        [((rows, channels, wide), F32), ((inner, 2 * wide), F32)],
        16,
        [pltpu.VMEM((rows * depth, wide), BF16), pltpu.VMEM((depth, wide), BF16)],
        flops=2 * wide * depth * (3 * inner + (3 * rows - 2) * channels),
        inputs=[whole] * 4,
    )(*in_vmem(skip, inside_rows, mid_turned, skip_weight))

    (out,) = call(
        functools.partial(last_kernel, bands=bands),
        "last",
        [(turned.shape, BF16)],
        20,
        [
            pltpu.VMEM((depth, wide), BF16),
            pltpu.VMEM((depth, wide), BF16),
            pltpu.VMEM((depth, wide), BF16),
            pltpu.VMEM((2 * depth, wide), BF16),
            pltpu.VMEM((4 * 3 * inner, wide // 2), BF16),
        ],
        flops=2 * wide * (3 * depth * inner + 2 * depth * channels + rows * 4 * inner * channels),
        kept=False,
        inputs=[whole] * 8,
    )(
        *in_vmem(
            mixed, middle, from_inside, from_across, mid_turned, skip_weight, phase_weight, field
        ),
    )
    return jnp.swapaxes(out, 2, 3)


def solution(mesh):
    in_specs = (P("groups", "frames", None, None), P(), P(), P(), P())
    out_specs = P("groups", "frames", None, None)
    return jax.shard_map(body, mesh=mesh, in_specs=in_specs, out_specs=out_specs, check_vma=False)
```

```python
import functools

import jax
import jax.numpy as jnp
from jax import lax
from jax.experimental import pallas as pl
from jax.experimental.pallas import tpu as pltpu
from jax.sharding import PartitionSpec as P


FRAMES = 4
BF16 = jnp.bfloat16
F32 = jnp.float32
MIB = 1024 * 1024


def place(bands):
    index = lax.axis_index("frames") + bands // 2
    return lax.rem(index, bands), lax.rem(lax.div(index, bands), FRAMES)


def dot(left, right):
    return jnp.dot(left, right, preferred_element_type=F32)


def silu(value):
    return value / (1.0 + jnp.exp(-value))


def sort_pick(width, clips):
    wide, half = width * clips, width // 2
    source = lax.broadcasted_iota(jnp.int32, (wide, wide), 0)
    lane = lax.broadcasted_iota(jnp.int32, (wide, wide), 1)
    parity, clip, j = lane // (wide // 2), lane // half % clips, lane % half
    return (source == clip * width + 2 * j + parity).astype(BF16)


def unsort_pick(width, clips):
    wide, half = width * clips, width // 2
    source = lax.broadcasted_iota(jnp.int32, (wide, wide), 0)
    lane = lax.broadcasted_iota(jnp.int32, (wide, wide), 1)
    clip, column = lane // width, lane % width
    return (source == column % 2 * (wide // 2) + clip * half + column // 2).astype(BF16)


def from_left(value, half):
    lane = lax.broadcasted_iota(jnp.int32, (1, value.shape[1]), 1)
    return jnp.where(lane % half == 0, 0.0, pltpu.roll(value, 1, 1))


def from_right(value, half):
    width = value.shape[1]
    lane = lax.broadcasted_iota(jnp.int32, (1, width), 1)
    return jnp.where(lane % half == half - 1, 0.0, pltpu.roll(value, width - 1, 1))


def store_taps(field, base, even, odd, half):
    channels, lanes = even.shape
    e, o = even.astype(BF16), odd.astype(BF16)
    blocks = ((from_left(odd, half).astype(BF16), e), (e, o), (o, from_right(even, half).astype(BF16)))
    for tap, pair in enumerate(blocks):
        rows = slice(base + tap * channels, base + (tap + 1) * channels)
        field[rows, :lanes] = pair[0]
        field[rows, lanes:] = pair[1]


def store_row_taps(field, base, lane_base, value, half):
    channels, lanes = value.shape
    blocks = (from_left(value, half).astype(BF16), value.astype(BF16), from_right(value, half).astype(BF16))
    for tap, block in enumerate(blocks):
        field[base + tap * channels : base + (tap + 1) * channels, lane_base : lane_base + lanes] = block


def fetch_kernel(
    latent_hbm, weight_hbm, inside_ref, across_ref, latent_ref, weight_ref, sems, *, bands
):
    last = latent_hbm.shape[1] - 1
    odd = lax.rem(place(bands)[0], 2)
    pieces = [
        (latent_hbm.at[:, last * odd], across_ref),
        (latent_hbm.at[:, last * (1 - odd)], inside_ref),
        (latent_hbm, latent_ref),
        (weight_hbm, weight_ref),
    ]
    gets = [
        pltpu.make_async_copy(source, target, sems.at[n])
        for n, (source, target) in enumerate(pieces)
    ]
    for get in gets:
        get.start()
    for get in gets:
        get.wait()


def prepare_kernel(latent_ref, weight_ref, turned_ref, field_ref):
    clips, rows, channels, width = latent_ref.shape
    pick = sort_pick(width, clips)
    for row in range(rows):
        value = dot(jnp.concatenate([latent_ref[clip, row] for clip in range(clips)], axis=1), pick)
        lanes = value.shape[1] // 2
        store_taps(field_ref, row * 3 * channels, value[:, :lanes], value[:, lanes:], width // 2)
    turned_ref[...] = weight_ref[...].T


def first_kernel(inside_ref, across_ref, turned_ref, field_ref, first_ref, rim, *, bands):
    clips, channels, width = inside_ref.shape
    depth = 3 * channels
    rows = first_ref.shape[0]
    pick = sort_pick(width, clips)
    odd = lax.rem(place(bands)[0], 2) == 1
    for at in range(2):
        one, other = (inside_ref, across_ref) if at == 0 else (across_ref, inside_ref)
        blocks = [jnp.where(odd, one[clip], other[clip]) for clip in range(clips)]
        value = dot(jnp.concatenate(blocks, axis=1), pick)
        lanes = value.shape[1] // 2
        store_taps(rim, at * depth, value[:, :lanes], value[:, lanes:], width // 2)
    for row in list(range(1, rows - 1)) + [0, rows - 1]:
        start, stop = max(row - 1, 0), min(row + 2, rows)
        total = dot(
            turned_ref[:, (start - row + 1) * depth : (stop - row + 1) * depth],
            field_ref[start * depth : stop * depth, :],
        )
        if row == 0:
            total += dot(turned_ref[:, :depth], rim[:depth, :])
        if row == rows - 1:
            total += dot(turned_ref[:, 2 * depth :], rim[depth:, :])
        first_ref[row] = silu(total).astype(BF16)


def weights_kernel(
    time_hbm, mid_hbm, up_hbm, time_out, mid_out, skip_out, phase_out,
    time_rows, mid_rows, up_rows, sems,
):
    taps, inner = mid_rows.shape
    channels = up_rows.shape[2]
    cuts = list(range(0, taps, 1024)) + [taps]
    pieces = [(time_hbm, time_rows)]
    pieces += [(mid_hbm.at[a:b], mid_rows.at[a:b]) for a, b in zip(cuts, cuts[1:])]
    pieces += [(up_hbm, up_rows)]
    gets = [
        pltpu.make_async_copy(source, target, sems.at[n])
        for n, (source, target) in enumerate(pieces)
    ]
    for get in gets:
        get.start()
    gets[0].wait()
    time_out[...] = time_rows[...].T
    for get, a, b in zip(gets[1:-1], cuts, cuts[1:]):
        get.wait()
        mid_out[:, a:b] = mid_rows[a:b, :].T
    gets[-1].wait()
    skip_out[...] = jnp.concatenate(
        [up_rows[dr, dc, :, :channels] for dr in range(3) for dc in range(3)], axis=1
    )
    taps = [[up_rows[dr, dc, :, channels:].astype(F32) for dc in range(3)] for dr in range(3)]
    groups = ((lambda t: t[0], lambda t: t[1] + t[2]), (lambda t: t[0] + t[1], lambda t: t[2]))
    for row_phase in range(2):
        for row_tap in range(2):
            merged = [groups[row_phase][row_tap]([taps[dr][dc] for dr in range(3)]) for dc in range(3)]
            for column_phase in range(2):
                for column_tap in range(2):
                    value = groups[column_phase][column_tap](merged)
                    start = (2 * row_tap + column_tap) * inner
                    phase_out[2 * row_phase + column_phase, :, start : start + inner] = value.astype(
                        BF16
                    )


def skip_kernel(
    first_ref, second_swap, first_swap, relayed_ref, weight_ref, skip_ref, inside_ref, across_ref,
    *, bands
):
    rows, _, wide = skip_ref.shape
    lanes = wide // 2
    band, frame = place(bands)
    odd_band, odd_frame = lax.rem(band, 2) == 1, lax.rem(frame, 2) == 1
    is_relayed = jnp.logical_and(jnp.logical_and(frame < 2, band < bands // 2), lax.rem(band, 2) == 0)
    upper = band < bands // 2
    first_is_before = upper == odd_frame
    is_host = jnp.logical_and(
        jnp.logical_not(upper), jnp.logical_or(frame == 0, frame == FRAMES - 1)
    )
    skips = []
    for row in range(rows):
        centre, second = first_ref[row], second_swap[row]
        first = jnp.where(is_host, jnp.zeros((), BF16), first_swap[row])
        first = jnp.where(is_relayed, relayed_ref[row], first)
        before = jnp.where(first_is_before, first, second)
        after = jnp.where(first_is_before, second, first)
        stacked = jnp.concatenate([before, centre, after], axis=0)
        skip = (centre.astype(F32) + dot(weight_ref[...], stacked)).astype(BF16)
        skip_ref[row] = skip
        skips.append(skip)
    inside_ref[0] = jnp.where(odd_band, skips[0], skips[-1])
    across_ref[0] = jnp.where(odd_band, skips[-1], skips[0])
    for pooled_row in range(rows // 2):
        sums = skips[2 * pooled_row].astype(F32) + skips[2 * pooled_row + 1].astype(F32)
        pooled = ((sums[:, :lanes] + sums[:, lanes:]) * 0.25).astype(BF16)
        span = slice(pooled_row * lanes, (pooled_row + 1) * lanes)
        inside_ref[1, :, span] = pooled
        across_ref[1, :, span] = pooled


def own_kernel(skip_ref, pair_ref, mid_ref, skip_weight, mixed_ref, middle_ref, field, pooled, *, half):
    rows, channels, wide = skip_ref.shape
    lanes = wide // 2
    depth = 3 * channels
    for at in range(2):
        row = pair_ref[1, :, at * lanes : (at + 1) * lanes].astype(F32)
        store_row_taps(pooled, 0, at * lanes, row, half)
    for row in range(rows):
        value = skip_ref[row].astype(F32)
        store_taps(field, row * depth, value[:, :lanes], value[:, lanes:], half)
    parts = [dot(mid_ref[:, dr * depth : (dr + 1) * depth], pooled[...]) for dr in range(3)]
    middle_ref[:, :lanes] = parts[2][:, :lanes]
    middle_ref[:, lanes : 2 * lanes] = parts[2][:, lanes:] + parts[1][:, :lanes]
    middle_ref[:, 2 * lanes : 3 * lanes] = parts[1][:, lanes:] + parts[0][:, :lanes]
    middle_ref[:, 3 * lanes :] = parts[0][:, lanes:]
    for row in range(rows):
        first, last = max(row - 1, 0), min(row + 2, rows)
        mixed_ref[row] = dot(
            skip_weight[:, (first - row + 1) * depth : (last - row + 1) * depth],
            field[first * depth : last * depth, :],
        )


def last_kernel(
    mixed_ref, middle_ref, inside_ref, across_ref, mid_ref, skip_weight, phase_weight, field_ref,
    out_ref, low_field, high_field, cross_field, rims, middle_field, *, bands
):
    rows, channels, wide = mixed_ref.shape
    clips, _, _, width = out_ref.shape
    half, lanes = width // 2, wide // 2
    inner = mid_ref.shape[0]
    depth = 3 * channels

    band = place(bands)[0]
    odd = lax.rem(band, 2) == 1
    lows = [jnp.where(odd, inside_ref[at], across_ref[at]) for at in range(2)]
    highs = [jnp.where(odd, across_ref[at], inside_ref[at]) for at in range(2)]
    for target, pair, inward in ((low_field, lows[1], 1), (high_field, highs[1], 0)):
        for at in range(2):
            row = pair[:, at * lanes : (at + 1) * lanes].astype(F32)
            store_row_taps(target, 0, at * lanes, row, half)
        cross_field[:, (1 - inward) * lanes : (2 - inward) * lanes] = target[
            :, inward * lanes : (inward + 1) * lanes
        ]
    above = dot(mid_ref[:, :depth], low_field[...])
    cross = dot(mid_ref[:, depth : 2 * depth], cross_field[...])
    below = dot(mid_ref[:, 2 * depth :], high_field[...])
    middles = [
        middle_ref[:, :lanes] + above[:, :lanes] + cross[:, :lanes],
        middle_ref[:, lanes : 2 * lanes] + above[:, lanes:],
        middle_ref[:, 2 * lanes : 3 * lanes] + below[:, :lanes],
        middle_ref[:, 3 * lanes :] + below[:, lanes:] + cross[:, lanes:],
    ]
    kept = (band != 0, None, None, band != bands - 1)
    for at, (value, keep) in enumerate(zip(middles, kept)):
        value = silu(value)
        if keep is not None:
            value = jnp.where(keep, value, 0.0)
        store_row_taps(middle_field, at * 3 * inner, 0, value.astype(BF16).astype(F32), half)

    for at, row in enumerate((lows[0], highs[0])):
        value = row.astype(F32)
        store_taps(rims, at * depth, value[:, :lanes], value[:, lanes:], half)
    from_rim = {
        0: dot(skip_weight[:, :depth], rims[:depth, :]),
        rows - 1: dot(skip_weight[:, 2 * depth :], rims[depth:, :]),
    }
    unsort = unsort_pick(width, clips)
    block = 3 * inner
    for row_phase in range(2):
        phases = []
        for column_phase in range(2):
            start = column_phase * inner
            taps = [
                jnp.concatenate(
                    [
                        middle_field[
                            (row_phase + tap + at) * block + start : (row_phase + tap + at) * block
                            + start + 2 * inner,
                            :,
                        ]
                        for at in range(rows // 2)
                    ],
                    axis=1,
                )
                for tap in range(2)
            ]
            total = dot(phase_weight[2 * row_phase + column_phase], jnp.concatenate(taps, axis=0))
            phases.append(total)
        for at in range(rows // 2):
            row = 2 * at + row_phase
            latent = field_ref[row * depth + channels : row * depth + 2 * channels, :].astype(F32)
            upper = jnp.concatenate([phase[:, at * lanes : (at + 1) * lanes] for phase in phases], axis=1)
            total = latent + mixed_ref[row] + upper
            if row in from_rim:
                total += from_rim[row]
            natural = dot(total.astype(BF16), unsort).astype(BF16)
            for clip in range(clips):
                out_ref[clip, row] = natural[:, clip * width : (clip + 1) * width]


def call(kernel, name, outputs, limit, scratch=(), flops=0, kept=True, inputs=None, aliases=None):
    shapes = [
        pltpu.VMEM(shape, dtype) if kept else jax.ShapeDtypeStruct(shape, dtype)
        for shape, dtype in outputs
    ]
    specs = {} if inputs is None else {"in_specs": inputs}
    return pl.pallas_call(
        kernel,
        out_shape=shapes,
        scratch_shapes=list(scratch),
        compiler_params=pltpu.CompilerParams(vmem_limit_bytes=limit * MIB),
        cost_estimate=pl.CostEstimate(flops=flops, bytes_accessed=1 << 20, transcendentals=0),
        name=name,
        input_output_aliases=aliases or {},
        **specs,
    )


def in_hbm(value):
    return pltpu.with_memory_space_constraint(value, pltpu.HBM)


def in_vmem(*values):
    return [pltpu.with_memory_space_constraint(value, pltpu.VMEM) for value in values]


def body(latents, in_weight, time_weight, mid_weight, up_weight):
    device_count = lax.axis_size("frames")
    bands = device_count // FRAMES
    offset = bands // 2
    band_of = lambda index: (index + offset) % bands
    frame_of = lambda index: (index + offset) // bands % FRAMES
    swap = lambda step, group, lowest: [
        pair
        for i in range(device_count)
        if group(i) % 2 == lowest and group(i) + 1 < (FRAMES if step == bands else bands)
        for j in [(i + step) % device_count]
        for pair in ((i, j), (j, i))
    ]
    inside, across = swap(1, band_of, 0), swap(1, band_of, 1)
    outer_frames, middle_frames = swap(bands, frame_of, 0), swap(bands, frame_of, 1)
    relayed_pairs = [(i, j) for i, j in outer_frames if abs(i - j) != bands and band_of(i) % 2 == 0]
    hops = [(i, i - offset + 1) for i, _ in relayed_pairs]
    relays = [(i - offset + 1, j) for i, j in relayed_pairs]
    outer_frames = [pair for pair in outer_frames if pair not in relayed_pairs]
    clips, rows, width, channels = latents.shape
    inner = mid_weight.shape[3]
    wide = clips * width
    depth = 3 * channels
    anywhere = pl.BlockSpec(memory_space=pl.ANY)
    whole = pl.BlockSpec(memory_space=pltpu.VMEM)
    turned = jnp.swapaxes(latents, 2, 3)

    inside_rim, across_rim, latent, in_rows = call(
        functools.partial(fetch_kernel, bands=bands),
        "fetch",
        [
            ((clips, channels, width), BF16),
            ((clips, channels, width), BF16),
            (turned.shape, BF16),
            ((3 * depth, channels), BF16),
        ],
        1,
        [pltpu.SemaphoreType.DMA((4,))],
        inputs=[anywhere, anywhere],
    )(in_hbm(turned), in_hbm(in_weight.reshape(3 * depth, channels)))
    inside_row = lax.ppermute(inside_rim, "frames", inside)
    across_row = lax.ppermute(across_rim, "frames", across)
    in_turned, field = call(
        prepare_kernel,
        "prepare",
        [((channels, 3 * depth), BF16), ((rows * depth, wide), BF16)],
        8,
        flops=2 * rows * wide * channels * wide,
        inputs=[whole] * 2,
    )(*in_vmem(latent, in_rows))
    (first,) = call(
        functools.partial(first_kernel, bands=bands),
        "first",
        [((rows, channels, wide), BF16)],
        8,
        [pltpu.VMEM((2 * depth, wide), BF16)],
        flops=2 * rows * wide * channels * 3 * depth,
        inputs=[whole] * 4,
    )(*in_vmem(inside_row, across_row, in_turned, field))
    of_bands = lambda pairs, upper: [pair for pair in pairs if (band_of(pair[0]) < offset) == upper]
    first_pairs = of_bands(outer_frames, True) + of_bands(middle_frames, False) + hops
    second_pairs = of_bands(middle_frames, True) + of_bands(outer_frames, False)
    first_swap = lax.ppermute(first, "frames", first_pairs)
    second_swap = lax.ppermute(first, "frames", second_pairs)

    time_rows, mid_rows, up_rows, first = lax.optimization_barrier(
        (
            time_weight.reshape(depth, channels),
            mid_weight.reshape(3 * depth, inner),
            jnp.swapaxes(up_weight, 2, 3),
            first,
        )
    )
    time_turned, mid_turned, skip_weight, phase_weight = call(
        weights_kernel,
        "weights",
        [
            ((channels, depth), BF16),
            ((inner, 3 * depth), BF16),
            ((channels, 3 * depth), BF16),
            ((4, channels, 4 * inner), BF16),
        ],
        20,
        [
            pltpu.VMEM(time_rows.shape, BF16),
            pltpu.VMEM(mid_rows.shape, BF16),
            pltpu.VMEM(up_rows.shape, BF16),
            pltpu.SemaphoreType.DMA((2 + -(-3 * depth // 1024),)),
        ],
        flops=2 * 10**9,
        inputs=[anywhere] * 3,
    )(in_hbm(time_rows), in_hbm(mid_rows), in_hbm(up_rows))

    hopped, time_turned = lax.optimization_barrier((first_swap, time_turned))
    relayed = lax.ppermute(hopped, "frames", relays)
    skip, inside_rows, across_rows = call(
        functools.partial(skip_kernel, bands=bands),
        "skip",
        [
            ((rows, channels, wide), BF16),
            ((2, channels, wide), BF16),
            ((2, channels, wide), BF16),
        ],
        8,
        flops=2 * rows * wide * depth * channels,
        inputs=[whole] * 5,
    )(*in_vmem(first, second_swap, first_swap, relayed, time_turned))
    from_across = lax.ppermute(across_rows, "frames", across)
    from_inside = lax.ppermute(inside_rows, "frames", inside)

    mixed, middle = call(
        lambda *refs: own_kernel(*refs, half=width // 2),
        "own_rows",
        [((rows, channels, wide), F32), ((inner, 2 * wide), F32)],
        16,
        [pltpu.VMEM((rows * depth, wide), BF16), pltpu.VMEM((depth, wide), BF16)],
        flops=2 * wide * depth * (3 * inner + (3 * rows - 2) * channels),
        inputs=[whole] * 4,
    )(*in_vmem(skip, inside_rows, mid_turned, skip_weight))

    (out,) = call(
        functools.partial(last_kernel, bands=bands),
        "last",
        [(turned.shape, BF16)],
        20,
        [
            pltpu.VMEM((depth, wide), BF16),
            pltpu.VMEM((depth, wide), BF16),
            pltpu.VMEM((depth, wide), BF16),
            pltpu.VMEM((2 * depth, wide), BF16),
            pltpu.VMEM((4 * 3 * inner, wide // 2), BF16),
        ],
        flops=2 * wide * (3 * depth * inner + 2 * depth * channels + rows * 4 * inner * channels),
        kept=False,
        inputs=[whole] * 8,
    )(
        *in_vmem(
            mixed, middle, from_inside, from_across, mid_turned, skip_weight, phase_weight, field
        ),
    )
    return jnp.swapaxes(out, 2, 3)


def solution(mesh):
    in_specs = (P("groups", "frames", None, None), P(), P(), P(), P())
    out_specs = P("groups", "frames", None, None)
    return jax.shard_map(body, mesh=mesh, in_specs=in_specs, out_specs=out_specs, check_vma=False)
```

```python
import functools

import jax
import jax.numpy as jnp
from jax import lax
from jax.experimental import pallas as pl
from jax.experimental.pallas import tpu as pltpu
from jax.sharding import PartitionSpec as P


FRAMES = 4
BF16 = jnp.bfloat16
F32 = jnp.float32
MIB = 1024 * 1024


def place(bands):
    index = lax.axis_index("frames") + bands // 2
    return lax.rem(index, bands), lax.rem(lax.div(index, bands), FRAMES)


def dot(left, right):
    return jnp.dot(left, right, preferred_element_type=F32)


def silu(value):
    return value / (1.0 + jnp.exp(-value))


def sort_pick(width, clips):
    wide, half = width * clips, width // 2
    source = lax.broadcasted_iota(jnp.int32, (wide, wide), 0)
    lane = lax.broadcasted_iota(jnp.int32, (wide, wide), 1)
    parity, clip, j = lane // (wide // 2), lane // half % clips, lane % half
    return (source == clip * width + 2 * j + parity).astype(BF16)


def unsort_pick(width, clips):
    wide, half = width * clips, width // 2
    source = lax.broadcasted_iota(jnp.int32, (wide, wide), 0)
    lane = lax.broadcasted_iota(jnp.int32, (wide, wide), 1)
    clip, column = lane // width, lane % width
    return (source == column % 2 * (wide // 2) + clip * half + column // 2).astype(BF16)


def from_left(value, half):
    lane = lax.broadcasted_iota(jnp.int32, (1, value.shape[1]), 1)
    return jnp.where(lane % half == 0, 0.0, pltpu.roll(value, 1, 1))


def from_right(value, half):
    width = value.shape[1]
    lane = lax.broadcasted_iota(jnp.int32, (1, width), 1)
    return jnp.where(lane % half == half - 1, 0.0, pltpu.roll(value, width - 1, 1))


def store_taps(field, base, even, odd, half):
    channels, lanes = even.shape
    e, o = even.astype(BF16), odd.astype(BF16)
    blocks = ((from_left(odd, half).astype(BF16), e), (e, o), (o, from_right(even, half).astype(BF16)))
    for tap, pair in enumerate(blocks):
        rows = slice(base + tap * channels, base + (tap + 1) * channels)
        field[rows, :lanes] = pair[0]
        field[rows, lanes:] = pair[1]


def store_row_taps(field, base, lane_base, value, half):
    channels, lanes = value.shape
    blocks = (from_left(value, half).astype(BF16), value.astype(BF16), from_right(value, half).astype(BF16))
    for tap, block in enumerate(blocks):
        field[base + tap * channels : base + (tap + 1) * channels, lane_base : lane_base + lanes] = block


def fetch_kernel(
    latent_hbm, weight_hbm, inside_ref, across_ref, latent_ref, weight_ref, sems, *, bands
):
    last = latent_hbm.shape[1] - 1
    odd = lax.rem(place(bands)[0], 2)
    pieces = [
        (latent_hbm.at[:, last * odd], across_ref),
        (latent_hbm.at[:, last * (1 - odd)], inside_ref),
        (latent_hbm, latent_ref),
        (weight_hbm, weight_ref),
    ]
    gets = [
        pltpu.make_async_copy(source, target, sems.at[n])
        for n, (source, target) in enumerate(pieces)
    ]
    for get in gets:
        get.start()
    for get in gets:
        get.wait()


def prepare_kernel(latent_ref, weight_ref, turned_ref, field_ref):
    clips, rows, channels, width = latent_ref.shape
    pick = sort_pick(width, clips)
    for row in range(rows):
        value = dot(jnp.concatenate([latent_ref[clip, row] for clip in range(clips)], axis=1), pick)
        lanes = value.shape[1] // 2
        store_taps(field_ref, row * 3 * channels, value[:, :lanes], value[:, lanes:], width // 2)
    turned_ref[...] = weight_ref[...].T


def first_kernel(inside_ref, across_ref, turned_ref, field_ref, first_ref, rim, *, bands):
    clips, channels, width = inside_ref.shape
    depth = 3 * channels
    rows = first_ref.shape[0]
    pick = sort_pick(width, clips)
    odd = lax.rem(place(bands)[0], 2) == 1
    for at in range(2):
        one, other = (inside_ref, across_ref) if at == 0 else (across_ref, inside_ref)
        blocks = [jnp.where(odd, one[clip], other[clip]) for clip in range(clips)]
        value = dot(jnp.concatenate(blocks, axis=1), pick)
        lanes = value.shape[1] // 2
        store_taps(rim, at * depth, value[:, :lanes], value[:, lanes:], width // 2)
    for row in list(range(1, rows - 1)) + [0, rows - 1]:
        start, stop = max(row - 1, 0), min(row + 2, rows)
        total = dot(
            turned_ref[:, (start - row + 1) * depth : (stop - row + 1) * depth],
            field_ref[start * depth : stop * depth, :],
        )
        if row == 0:
            total += dot(turned_ref[:, :depth], rim[:depth, :])
        if row == rows - 1:
            total += dot(turned_ref[:, 2 * depth :], rim[depth:, :])
        first_ref[row] = silu(total).astype(BF16)


def weights_kernel(
    time_hbm, mid_hbm, up_hbm, time_out, mid_out, skip_out, phase_out,
    time_rows, mid_rows, up_rows, sems,
):
    taps, inner = mid_rows.shape
    channels = up_rows.shape[2]
    cuts = list(range(0, taps, 1024)) + [taps]
    pieces = [(time_hbm, time_rows)]
    pieces += [(mid_hbm.at[a:b], mid_rows.at[a:b]) for a, b in zip(cuts, cuts[1:])]
    pieces += [(up_hbm, up_rows)]
    gets = [
        pltpu.make_async_copy(source, target, sems.at[n])
        for n, (source, target) in enumerate(pieces)
    ]
    for get in gets:
        get.start()
    gets[0].wait()
    time_out[...] = time_rows[...].T
    for get, a, b in zip(gets[1:-1], cuts, cuts[1:]):
        get.wait()
        mid_out[:, a:b] = mid_rows[a:b, :].T
    gets[-1].wait()
    skip_out[...] = jnp.concatenate(
        [up_rows[dr, dc, :, :channels] for dr in range(3) for dc in range(3)], axis=1
    )
    taps = [[up_rows[dr, dc, :, channels:].astype(F32) for dc in range(3)] for dr in range(3)]
    groups = ((lambda t: t[0], lambda t: t[1] + t[2]), (lambda t: t[0] + t[1], lambda t: t[2]))
    for row_phase in range(2):
        for row_tap in range(2):
            merged = [groups[row_phase][row_tap]([taps[dr][dc] for dr in range(3)]) for dc in range(3)]
            for column_phase in range(2):
                for column_tap in range(2):
                    value = groups[column_phase][column_tap](merged)
                    start = (2 * row_tap + column_tap) * inner
                    phase_out[2 * row_phase + column_phase, :, start : start + inner] = value.astype(
                        BF16
                    )


def skip_rows(first_ref, before_of, after_of, weight_ref, skip_ref, inside_ref, across_ref, odd_band):
    rows, _, wide = skip_ref.shape
    lanes = wide // 2
    skips = []
    for row in range(rows):
        centre = first_ref[row]
        stacked = jnp.concatenate([before_of(row), centre, after_of(row)], axis=0)
        skip = (centre.astype(F32) + dot(weight_ref[...], stacked)).astype(BF16)
        skip_ref[row] = skip
        skips.append(skip)
    inside_ref[0] = jnp.where(odd_band, skips[0], skips[-1])
    across_ref[0] = jnp.where(odd_band, skips[-1], skips[0])
    for pooled_row in range(rows // 2):
        sums = skips[2 * pooled_row].astype(F32) + skips[2 * pooled_row + 1].astype(F32)
        pooled = ((sums[:, :lanes] + sums[:, lanes:]) * 0.25).astype(BF16)
        span = slice(pooled_row * lanes, (pooled_row + 1) * lanes)
        inside_ref[1, :, span] = pooled
        across_ref[1, :, span] = pooled


def skip_lower_kernel(
    first_ref, outer_ref, middle_ref, weight_ref, skip_ref, inside_ref, across_ref, *, bands
):
    band, frame = place(bands)
    odd_frame = lax.rem(frame, 2) == 1
    is_host = jnp.logical_or(frame == 0, frame == FRAMES - 1)

    def middle(row):
        return jnp.where(is_host, jnp.zeros((), BF16), middle_ref[row])

    @pl.when(band >= bands // 2)
    def _():
        skip_rows(
            first_ref,
            lambda row: jnp.where(odd_frame, outer_ref[row], middle(row)),
            lambda row: jnp.where(odd_frame, middle(row), outer_ref[row]),
            weight_ref, skip_ref, inside_ref, across_ref, lax.rem(band, 2) == 1,
        )


def skip_upper_kernel(
    first_ref, middle_ref, outer_ref, relayed_ref, weight_ref, old_skip, old_inside,
    skip_ref, inside_ref, across_ref, *, bands
):
    band, frame = place(bands)
    odd_frame = lax.rem(frame, 2) == 1
    is_relayed = jnp.logical_and(frame < 2, lax.rem(band, 2) == 0)

    def outer(row):
        return jnp.where(is_relayed, relayed_ref[row], outer_ref[row])

    @pl.when(band < bands // 2)
    def _():
        skip_rows(
            first_ref,
            lambda row: jnp.where(odd_frame, outer(row), middle_ref[row]),
            lambda row: jnp.where(odd_frame, middle_ref[row], outer(row)),
            weight_ref, skip_ref, inside_ref, across_ref, lax.rem(band, 2) == 1,
        )


def own_kernel(skip_ref, pair_ref, mid_ref, skip_weight, mixed_ref, middle_ref, field, pooled, *, half):
    rows, channels, wide = skip_ref.shape
    lanes = wide // 2
    depth = 3 * channels
    for at in range(2):
        row = pair_ref[1, :, at * lanes : (at + 1) * lanes].astype(F32)
        store_row_taps(pooled, 0, at * lanes, row, half)
    for row in range(rows):
        value = skip_ref[row].astype(F32)
        store_taps(field, row * depth, value[:, :lanes], value[:, lanes:], half)
    parts = [dot(mid_ref[:, dr * depth : (dr + 1) * depth], pooled[...]) for dr in range(3)]
    middle_ref[:, :lanes] = parts[2][:, :lanes]
    middle_ref[:, lanes : 2 * lanes] = parts[2][:, lanes:] + parts[1][:, :lanes]
    middle_ref[:, 2 * lanes : 3 * lanes] = parts[1][:, lanes:] + parts[0][:, :lanes]
    middle_ref[:, 3 * lanes :] = parts[0][:, lanes:]
    for row in range(rows):
        first, last = max(row - 1, 0), min(row + 2, rows)
        mixed_ref[row] = dot(
            skip_weight[:, (first - row + 1) * depth : (last - row + 1) * depth],
            field[first * depth : last * depth, :],
        )


def last_kernel(
    mixed_ref, middle_ref, inside_ref, lower_ref, upper_ref, mid_ref, skip_weight, phase_weight,
    field_ref, out_ref, low_field, high_field, cross_field, rims, middle_field, *, bands
):
    rows, channels, wide = mixed_ref.shape
    clips, _, _, width = out_ref.shape
    half, lanes = width // 2, wide // 2
    inner = mid_ref.shape[0]
    depth = 3 * channels

    band = place(bands)[0]
    odd = lax.rem(band, 2) == 1
    across = [lower_ref[at] + upper_ref[at] for at in range(2)]
    lows = [jnp.where(odd, inside_ref[at], across[at]) for at in range(2)]
    highs = [jnp.where(odd, across[at], inside_ref[at]) for at in range(2)]
    for target, pair, inward in ((low_field, lows[1], 1), (high_field, highs[1], 0)):
        for at in range(2):
            row = pair[:, at * lanes : (at + 1) * lanes].astype(F32)
            store_row_taps(target, 0, at * lanes, row, half)
        cross_field[:, (1 - inward) * lanes : (2 - inward) * lanes] = target[
            :, inward * lanes : (inward + 1) * lanes
        ]
    above = dot(mid_ref[:, :depth], low_field[...])
    cross = dot(mid_ref[:, depth : 2 * depth], cross_field[...])
    below = dot(mid_ref[:, 2 * depth :], high_field[...])
    middles = [
        middle_ref[:, :lanes] + above[:, :lanes] + cross[:, :lanes],
        middle_ref[:, lanes : 2 * lanes] + above[:, lanes:],
        middle_ref[:, 2 * lanes : 3 * lanes] + below[:, :lanes],
        middle_ref[:, 3 * lanes :] + below[:, lanes:] + cross[:, lanes:],
    ]
    kept = (band != 0, None, None, band != bands - 1)
    for at, (value, keep) in enumerate(zip(middles, kept)):
        value = silu(value)
        if keep is not None:
            value = jnp.where(keep, value, 0.0)
        store_row_taps(middle_field, at * 3 * inner, 0, value.astype(BF16).astype(F32), half)

    for at, row in enumerate((lows[0], highs[0])):
        value = row.astype(F32)
        store_taps(rims, at * depth, value[:, :lanes], value[:, lanes:], half)
    from_rim = {
        0: dot(skip_weight[:, :depth], rims[:depth, :]),
        rows - 1: dot(skip_weight[:, 2 * depth :], rims[depth:, :]),
    }
    unsort = unsort_pick(width, clips)
    block = 3 * inner
    for row_phase in range(2):
        phases = []
        for column_phase in range(2):
            start = column_phase * inner
            taps = [
                jnp.concatenate(
                    [
                        middle_field[
                            (row_phase + tap + at) * block + start : (row_phase + tap + at) * block
                            + start + 2 * inner,
                            :,
                        ]
                        for at in range(rows // 2)
                    ],
                    axis=1,
                )
                for tap in range(2)
            ]
            total = dot(phase_weight[2 * row_phase + column_phase], jnp.concatenate(taps, axis=0))
            phases.append(total)
        for at in range(rows // 2):
            row = 2 * at + row_phase
            latent = field_ref[row * depth + channels : row * depth + 2 * channels, :].astype(F32)
            upper = jnp.concatenate([phase[:, at * lanes : (at + 1) * lanes] for phase in phases], axis=1)
            total = latent + mixed_ref[row] + upper
            if row in from_rim:
                total += from_rim[row]
            natural = dot(total.astype(BF16), unsort).astype(BF16)
            for clip in range(clips):
                out_ref[clip, row] = natural[:, clip * width : (clip + 1) * width]


def call(kernel, name, outputs, limit, scratch=(), flops=0, kept=True, inputs=None, aliases=None):
    shapes = [
        pltpu.VMEM(shape, dtype) if kept else jax.ShapeDtypeStruct(shape, dtype)
        for shape, dtype in outputs
    ]
    specs = {} if inputs is None else {"in_specs": inputs}
    return pl.pallas_call(
        kernel,
        out_shape=shapes,
        scratch_shapes=list(scratch),
        compiler_params=pltpu.CompilerParams(vmem_limit_bytes=limit * MIB),
        cost_estimate=pl.CostEstimate(flops=flops, bytes_accessed=1 << 20, transcendentals=0),
        name=name,
        input_output_aliases=aliases or {},
        **specs,
    )


def in_hbm(value):
    return pltpu.with_memory_space_constraint(value, pltpu.HBM)


def in_vmem(*values):
    return [pltpu.with_memory_space_constraint(value, pltpu.VMEM) for value in values]


def body(latents, in_weight, time_weight, mid_weight, up_weight):
    device_count = lax.axis_size("frames")
    bands = device_count // FRAMES
    offset = bands // 2
    band_of = lambda index: (index + offset) % bands
    frame_of = lambda index: (index + offset) // bands % FRAMES
    swap = lambda step, group, lowest: [
        pair
        for i in range(device_count)
        if group(i) % 2 == lowest and group(i) + 1 < (FRAMES if step == bands else bands)
        for j in [(i + step) % device_count]
        for pair in ((i, j), (j, i))
    ]
    inside, across = swap(1, band_of, 0), swap(1, band_of, 1)
    outer_frames, middle_frames = swap(bands, frame_of, 0), swap(bands, frame_of, 1)
    relayed_pairs = [(i, j) for i, j in outer_frames if abs(i - j) != bands and band_of(i) % 2 == 0]
    hops = [(i, i - offset + 1) for i, _ in relayed_pairs]
    relays = [(i - offset + 1, j) for i, j in relayed_pairs]
    outer_frames = [pair for pair in outer_frames if pair not in relayed_pairs]
    clips, rows, width, channels = latents.shape
    inner = mid_weight.shape[3]
    wide = clips * width
    depth = 3 * channels
    anywhere = pl.BlockSpec(memory_space=pl.ANY)
    whole = pl.BlockSpec(memory_space=pltpu.VMEM)
    turned = jnp.swapaxes(latents, 2, 3)

    inside_rim, across_rim, latent, in_rows = call(
        functools.partial(fetch_kernel, bands=bands),
        "fetch",
        [
            ((clips, channels, width), BF16),
            ((clips, channels, width), BF16),
            (turned.shape, BF16),
            ((3 * depth, channels), BF16),
        ],
        1,
        [pltpu.SemaphoreType.DMA((4,))],
        inputs=[anywhere, anywhere],
    )(in_hbm(turned), in_hbm(in_weight.reshape(3 * depth, channels)))
    inside_row = lax.ppermute(inside_rim, "frames", inside)
    across_row = lax.ppermute(across_rim, "frames", across)
    in_turned, field = call(
        prepare_kernel,
        "prepare",
        [((channels, 3 * depth), BF16), ((rows * depth, wide), BF16)],
        8,
        flops=2 * rows * wide * channels * wide,
        inputs=[whole] * 2,
    )(*in_vmem(latent, in_rows))
    (first,) = call(
        functools.partial(first_kernel, bands=bands),
        "first",
        [((rows, channels, wide), BF16)],
        8,
        [pltpu.VMEM((2 * depth, wide), BF16)],
        flops=2 * rows * wide * channels * 3 * depth,
        inputs=[whole] * 4,
    )(*in_vmem(inside_row, across_row, in_turned, field))
    of_half = lambda pairs, upper: [pair for pair in pairs if (band_of(pair[0]) < offset) == upper]
    lower_outer = lax.ppermute(first, "frames", of_half(outer_frames, False))
    lower_middle = lax.ppermute(first, "frames", of_half(middle_frames, False) + hops)
    upper_middle = lax.ppermute(first, "frames", of_half(middle_frames, True))
    upper_outer = lax.ppermute(first, "frames", of_half(outer_frames, True))
    time_rows, mid_rows, up_rows, first = lax.optimization_barrier(
        (
            time_weight.reshape(depth, channels),
            mid_weight.reshape(3 * depth, inner),
            jnp.swapaxes(up_weight, 2, 3),
            first,
        )
    )
    time_turned, mid_turned, skip_weight, phase_weight = call(
        weights_kernel,
        "weights",
        [
            ((channels, depth), BF16),
            ((inner, 3 * depth), BF16),
            ((channels, 3 * depth), BF16),
            ((4, channels, 4 * inner), BF16),
        ],
        20,
        [
            pltpu.VMEM(time_rows.shape, BF16),
            pltpu.VMEM(mid_rows.shape, BF16),
            pltpu.VMEM(up_rows.shape, BF16),
            pltpu.SemaphoreType.DMA((2 + -(-3 * depth // 1024),)),
        ],
        flops=2 * 10**9,
        inputs=[anywhere] * 3,
    )(in_hbm(time_rows), in_hbm(mid_rows), in_hbm(up_rows))

    hopped, time_turned = lax.optimization_barrier((lower_middle, time_turned))
    relayed = lax.ppermute(hopped, "frames", relays)
    skip_shapes = [
        ((rows, channels, wide), BF16),
        ((2, channels, wide), BF16),
        ((2, channels, wide), BF16),
    ]
    skip, inside_rows, lower_rows = call(
        functools.partial(skip_lower_kernel, bands=bands),
        "skip_lower",
        skip_shapes,
        8,
        flops=2 * rows * wide * depth * channels,
        inputs=[whole] * 4,
    )(*in_vmem(first, lower_outer, lower_middle, time_turned))
    lower_across = lax.ppermute(lower_rows, "frames", of_half(across, False))
    skip, inside_rows, upper_rows = call(
        functools.partial(skip_upper_kernel, bands=bands),
        "skip_upper",
        skip_shapes,
        8,
        flops=2 * rows * wide * depth * channels,
        inputs=[whole] * 7,
        aliases={5: 0, 6: 1},
    )(*in_vmem(first, upper_middle, upper_outer, relayed, time_turned, skip, inside_rows))
    upper_across = lax.ppermute(upper_rows, "frames", of_half(across, True))
    from_inside = lax.ppermute(inside_rows, "frames", inside)

    mixed, middle = call(
        lambda *refs: own_kernel(*refs, half=width // 2),
        "own_rows",
        [((rows, channels, wide), F32), ((inner, 2 * wide), F32)],
        16,
        [pltpu.VMEM((rows * depth, wide), BF16), pltpu.VMEM((depth, wide), BF16)],
        flops=2 * wide * depth * (3 * inner + (3 * rows - 2) * channels),
        inputs=[whole] * 4,
    )(*in_vmem(skip, inside_rows, mid_turned, skip_weight))

    (out,) = call(
        functools.partial(last_kernel, bands=bands),
        "last",
        [(turned.shape, BF16)],
        20,
        [
            pltpu.VMEM((depth, wide), BF16),
            pltpu.VMEM((depth, wide), BF16),
            pltpu.VMEM((depth, wide), BF16),
            pltpu.VMEM((2 * depth, wide), BF16),
            pltpu.VMEM((4 * 3 * inner, wide // 2), BF16),
        ],
        flops=2 * wide * (3 * depth * inner + 2 * depth * channels + rows * 4 * inner * channels),
        kept=False,
        inputs=[whole] * 9,
    )(
        *in_vmem(
            mixed, middle, from_inside, lower_across, upper_across, mid_turned, skip_weight, phase_weight, field
        ),
    )
    return jnp.swapaxes(out, 2, 3)


def solution(mesh):
    in_specs = (P("groups", "frames", None, None), P(), P(), P(), P())
    out_specs = P("groups", "frames", None, None)
    return jax.shard_map(body, mesh=mesh, in_specs=in_specs, out_specs=out_specs, check_vma=False)
```

```python
import functools

import jax
import jax.numpy as jnp
from jax import lax
from jax.experimental import pallas as pl
from jax.experimental.pallas import tpu as pltpu
from jax.sharding import PartitionSpec as P


FRAMES = 4
BF16 = jnp.bfloat16
F32 = jnp.float32
MIB = 1024 * 1024


def place(bands):
    index = lax.axis_index("frames") + bands // 2
    return lax.rem(index, bands), lax.rem(lax.div(index, bands), FRAMES)


def dot(left, right):
    return jnp.dot(left, right, preferred_element_type=F32)


def silu(value):
    return value / (1.0 + jnp.exp(-value))


def sort_pick(width, clips):
    wide, half = width * clips, width // 2
    source = lax.broadcasted_iota(jnp.int32, (wide, wide), 0)
    lane = lax.broadcasted_iota(jnp.int32, (wide, wide), 1)
    parity, clip, j = lane // (wide // 2), lane // half % clips, lane % half
    return (source == clip * width + 2 * j + parity).astype(BF16)


def unsort_pick(width, clips):
    wide, half = width * clips, width // 2
    source = lax.broadcasted_iota(jnp.int32, (wide, wide), 0)
    lane = lax.broadcasted_iota(jnp.int32, (wide, wide), 1)
    clip, column = lane // width, lane % width
    return (source == column % 2 * (wide // 2) + clip * half + column // 2).astype(BF16)


def from_left(value, half):
    lane = lax.broadcasted_iota(jnp.int32, (1, value.shape[1]), 1)
    return jnp.where(lane % half == 0, 0.0, pltpu.roll(value, 1, 1))


def from_right(value, half):
    width = value.shape[1]
    lane = lax.broadcasted_iota(jnp.int32, (1, width), 1)
    return jnp.where(lane % half == half - 1, 0.0, pltpu.roll(value, width - 1, 1))


def store_taps(field, base, even, odd, half):
    channels, lanes = even.shape
    e, o = even.astype(BF16), odd.astype(BF16)
    blocks = ((from_left(odd, half).astype(BF16), e), (e, o), (o, from_right(even, half).astype(BF16)))
    for tap, pair in enumerate(blocks):
        rows = slice(base + tap * channels, base + (tap + 1) * channels)
        field[rows, :lanes] = pair[0]
        field[rows, lanes:] = pair[1]


def store_row_taps(field, base, lane_base, value, half):
    channels, lanes = value.shape
    blocks = (from_left(value, half).astype(BF16), value.astype(BF16), from_right(value, half).astype(BF16))
    for tap, block in enumerate(blocks):
        field[base + tap * channels : base + (tap + 1) * channels, lane_base : lane_base + lanes] = block


def fetch_kernel(
    latent_hbm, weight_hbm, inside_ref, across_ref, latent_ref, weight_ref, sems, *, bands
):
    last = latent_hbm.shape[1] - 1
    odd = lax.rem(place(bands)[0], 2)
    pieces = [
        (latent_hbm.at[:, last * odd], across_ref),
        (latent_hbm.at[:, last * (1 - odd)], inside_ref),
        (latent_hbm, latent_ref),
        (weight_hbm, weight_ref),
    ]
    gets = [
        pltpu.make_async_copy(source, target, sems.at[n])
        for n, (source, target) in enumerate(pieces)
    ]
    for get in gets:
        get.start()
    for get in gets:
        get.wait()


def prepare_kernel(latent_ref, weight_ref, turned_ref, field_ref):
    clips, rows, channels, width = latent_ref.shape
    pick = sort_pick(width, clips)
    for row in range(rows):
        value = dot(jnp.concatenate([latent_ref[clip, row] for clip in range(clips)], axis=1), pick)
        lanes = value.shape[1] // 2
        store_taps(field_ref, row * 3 * channels, value[:, :lanes], value[:, lanes:], width // 2)
    turned_ref[...] = weight_ref[...].T


def first_kernel(inside_ref, across_ref, turned_ref, field_ref, first_ref, rim, *, bands):
    clips, channels, width = inside_ref.shape
    depth = 3 * channels
    rows = first_ref.shape[0]
    pick = sort_pick(width, clips)
    odd = lax.rem(place(bands)[0], 2) == 1
    for at in range(2):
        one, other = (inside_ref, across_ref) if at == 0 else (across_ref, inside_ref)
        blocks = [jnp.where(odd, one[clip], other[clip]) for clip in range(clips)]
        value = dot(jnp.concatenate(blocks, axis=1), pick)
        lanes = value.shape[1] // 2
        store_taps(rim, at * depth, value[:, :lanes], value[:, lanes:], width // 2)
    for row in list(range(1, rows - 1)) + [0, rows - 1]:
        start, stop = max(row - 1, 0), min(row + 2, rows)
        total = dot(
            turned_ref[:, (start - row + 1) * depth : (stop - row + 1) * depth],
            field_ref[start * depth : stop * depth, :],
        )
        if row == 0:
            total += dot(turned_ref[:, :depth], rim[:depth, :])
        if row == rows - 1:
            total += dot(turned_ref[:, 2 * depth :], rim[depth:, :])
        first_ref[row] = silu(total).astype(BF16)


def weights_kernel(
    time_hbm, mid_hbm, up_hbm, time_out, part_out, rest_out, outer_out, mid_out, skip_out, phase_out,
    time_rows, mid_rows, up_rows, sems, *, bands
):
    taps, inner = mid_rows.shape
    channels = up_rows.shape[2]
    cuts = list(range(0, taps, 1024)) + [taps]
    pieces = [(time_hbm, time_rows)]
    pieces += [(mid_hbm.at[a:b], mid_rows.at[a:b]) for a, b in zip(cuts, cuts[1:])]
    pieces += [(up_hbm, up_rows)]
    gets = [
        pltpu.make_async_copy(source, target, sems.at[n])
        for n, (source, target) in enumerate(pieces)
    ]
    for get in gets:
        get.start()
    gets[0].wait()
    time_out[...] = time_rows[...].T
    odd_frame = lax.rem(place(bands)[1], 2) == 1
    size = time_rows.shape[1]
    before, centre, after = [time_rows[at * size : (at + 1) * size, :] for at in range(3)]
    outer = jnp.where(odd_frame, before, after)
    part_out[...] = jnp.concatenate([centre, outer], axis=0).T
    rest_out[...] = jnp.where(odd_frame, after, before).T
    outer_out[...] = outer.T
    for get, a, b in zip(gets[1:-1], cuts, cuts[1:]):
        get.wait()
        mid_out[:, a:b] = mid_rows[a:b, :].T
    gets[-1].wait()
    skip_out[...] = jnp.concatenate(
        [up_rows[dr, dc, :, :channels] for dr in range(3) for dc in range(3)], axis=1
    )
    taps = [[up_rows[dr, dc, :, channels:].astype(F32) for dc in range(3)] for dr in range(3)]
    groups = ((lambda t: t[0], lambda t: t[1] + t[2]), (lambda t: t[0] + t[1], lambda t: t[2]))
    for row_phase in range(2):
        for row_tap in range(2):
            merged = [groups[row_phase][row_tap]([taps[dr][dc] for dr in range(3)]) for dc in range(3)]
            for column_phase in range(2):
                for column_tap in range(2):
                    value = groups[column_phase][column_tap](merged)
                    start = (2 * row_tap + column_tap) * inner
                    phase_out[2 * row_phase + column_phase, :, start : start + inner] = value.astype(
                        BF16
                    )


def share_skip(skips, skip_ref, inside_ref, across_ref, odd_band):
    lanes = skip_ref.shape[2] // 2
    for row, skip in enumerate(skips):
        skip_ref[row] = skip
    inside_ref[0] = jnp.where(odd_band, skips[0], skips[-1])
    across_ref[0] = jnp.where(odd_band, skips[-1], skips[0])
    for pooled_row in range(len(skips) // 2):
        sums = skips[2 * pooled_row].astype(F32) + skips[2 * pooled_row + 1].astype(F32)
        pooled = ((sums[:, :lanes] + sums[:, lanes:]) * 0.25).astype(BF16)
        span = slice(pooled_row * lanes, (pooled_row + 1) * lanes)
        inside_ref[1, :, span] = pooled
        across_ref[1, :, span] = pooled


def skip_lower_kernel(
    first_ref, outer_ref, middle_ref, weight_ref, skip_ref, inside_ref, across_ref, *, bands
):
    band, frame = place(bands)
    odd_frame = lax.rem(frame, 2) == 1
    is_host = jnp.logical_or(frame == 0, frame == FRAMES - 1)

    def middle(row):
        return jnp.where(is_host, jnp.zeros((), BF16), middle_ref[row])

    @pl.when(band >= bands // 2)
    def _():
        skips = []
        for row in range(first_ref.shape[0]):
            centre, outer, inner = first_ref[row], outer_ref[row], middle(row)
            before = jnp.where(odd_frame, outer, inner)
            after = jnp.where(odd_frame, inner, outer)
            stacked = jnp.concatenate([before, centre, after], axis=0)
            skips.append((centre.astype(F32) + dot(weight_ref[...], stacked)).astype(BF16))
        share_skip(skips, skip_ref, inside_ref, across_ref, lax.rem(band, 2) == 1)


def skip_part_kernel(first_ref, outer_ref, weight_ref, partial_ref, *, bands):
    @pl.when(place(bands)[0] < bands // 2)
    def _():
        for row in range(first_ref.shape[0]):
            centre = first_ref[row]
            stacked = jnp.concatenate([centre, outer_ref[row]], axis=0)
            partial_ref[row] = centre.astype(F32) + dot(weight_ref[...], stacked)


def skip_upper_kernel(
    partial_ref, middle_ref, relayed_ref, weight_ref, outer_weight, old_skip, old_inside,
    skip_ref, inside_ref, across_ref, *, bands
):
    band, frame = place(bands)
    upper = band < bands // 2
    is_relayed = jnp.logical_and(frame < 2, lax.rem(band, 2) == 0)

    def add(with_relayed):
        skips = []
        for row in range(partial_ref.shape[0]):
            total = partial_ref[row] + dot(weight_ref[...], middle_ref[row])
            if with_relayed:
                total += dot(outer_weight[...], relayed_ref[row])
            skips.append(total.astype(BF16))
        share_skip(skips, skip_ref, inside_ref, across_ref, lax.rem(band, 2) == 1)

    pl.when(jnp.logical_and(upper, is_relayed))(lambda: add(True))
    pl.when(jnp.logical_and(upper, jnp.logical_not(is_relayed)))(lambda: add(False))


def own_kernel(skip_ref, pair_ref, mid_ref, skip_weight, mixed_ref, middle_ref, field, pooled, *, half):
    rows, channels, wide = skip_ref.shape
    lanes = wide // 2
    depth = 3 * channels
    for at in range(2):
        row = pair_ref[1, :, at * lanes : (at + 1) * lanes].astype(F32)
        store_row_taps(pooled, 0, at * lanes, row, half)
    for row in range(rows):
        value = skip_ref[row].astype(F32)
        store_taps(field, row * depth, value[:, :lanes], value[:, lanes:], half)
    parts = [dot(mid_ref[:, dr * depth : (dr + 1) * depth], pooled[...]) for dr in range(3)]
    middle_ref[:, :lanes] = parts[2][:, :lanes]
    middle_ref[:, lanes : 2 * lanes] = parts[2][:, lanes:] + parts[1][:, :lanes]
    middle_ref[:, 2 * lanes : 3 * lanes] = parts[1][:, lanes:] + parts[0][:, :lanes]
    middle_ref[:, 3 * lanes :] = parts[0][:, lanes:]
    for row in range(rows):
        first, last = max(row - 1, 0), min(row + 2, rows)
        mixed_ref[row] = dot(
            skip_weight[:, (first - row + 1) * depth : (last - row + 1) * depth],
            field[first * depth : last * depth, :],
        )


def last_kernel(
    mixed_ref, middle_ref, upper_ref, lower_ref, inside_ref, mid_ref, skip_weight, phase_weight,
    field_ref, out_ref, low_field, high_field, cross_field, rims, middle_field, *, bands
):
    rows, channels, wide = mixed_ref.shape
    clips, _, _, width = out_ref.shape
    half, lanes = width // 2, wide // 2
    inner = mid_ref.shape[0]
    depth = 3 * channels

    band = place(bands)[0]
    odd = lax.rem(band, 2) == 1
    across = [lower_ref[at] + upper_ref[at] for at in range(2)]
    lows = [jnp.where(odd, inside_ref[at], across[at]) for at in range(2)]
    highs = [jnp.where(odd, across[at], inside_ref[at]) for at in range(2)]
    for target, pair, inward in ((low_field, lows[1], 1), (high_field, highs[1], 0)):
        for at in range(2):
            row = pair[:, at * lanes : (at + 1) * lanes].astype(F32)
            store_row_taps(target, 0, at * lanes, row, half)
        cross_field[:, (1 - inward) * lanes : (2 - inward) * lanes] = target[
            :, inward * lanes : (inward + 1) * lanes
        ]
    above = dot(mid_ref[:, :depth], low_field[...])
    cross = dot(mid_ref[:, depth : 2 * depth], cross_field[...])
    below = dot(mid_ref[:, 2 * depth :], high_field[...])
    middles = [
        middle_ref[:, :lanes] + above[:, :lanes] + cross[:, :lanes],
        middle_ref[:, lanes : 2 * lanes] + above[:, lanes:],
        middle_ref[:, 2 * lanes : 3 * lanes] + below[:, :lanes],
        middle_ref[:, 3 * lanes :] + below[:, lanes:] + cross[:, lanes:],
    ]
    kept = (band != 0, None, None, band != bands - 1)
    for at, (value, keep) in enumerate(zip(middles, kept)):
        value = silu(value)
        if keep is not None:
            value = jnp.where(keep, value, 0.0)
        store_row_taps(middle_field, at * 3 * inner, 0, value.astype(BF16).astype(F32), half)

    for at, row in enumerate((lows[0], highs[0])):
        value = row.astype(F32)
        store_taps(rims, at * depth, value[:, :lanes], value[:, lanes:], half)
    from_rim = {
        0: dot(skip_weight[:, :depth], rims[:depth, :]),
        rows - 1: dot(skip_weight[:, 2 * depth :], rims[depth:, :]),
    }
    unsort = unsort_pick(width, clips)
    block = 3 * inner
    for row_phase in range(2):
        phases = []
        for column_phase in range(2):
            start = column_phase * inner
            taps = [
                jnp.concatenate(
                    [
                        middle_field[
                            (row_phase + tap + at) * block + start : (row_phase + tap + at) * block
                            + start + 2 * inner,
                            :,
                        ]
                        for at in range(rows // 2)
                    ],
                    axis=1,
                )
                for tap in range(2)
            ]
            total = dot(phase_weight[2 * row_phase + column_phase], jnp.concatenate(taps, axis=0))
            phases.append(total)
        for at in range(rows // 2):
            row = 2 * at + row_phase
            latent = field_ref[row * depth + channels : row * depth + 2 * channels, :].astype(F32)
            upper = jnp.concatenate([phase[:, at * lanes : (at + 1) * lanes] for phase in phases], axis=1)
            total = latent + mixed_ref[row] + upper
            if row in from_rim:
                total += from_rim[row]
            natural = dot(total.astype(BF16), unsort).astype(BF16)
            for clip in range(clips):
                out_ref[clip, row] = natural[:, clip * width : (clip + 1) * width]


def call(kernel, name, outputs, limit, scratch=(), flops=0, kept=True, inputs=None, aliases=None):
    shapes = [
        pltpu.VMEM(shape, dtype) if kept else jax.ShapeDtypeStruct(shape, dtype)
        for shape, dtype in outputs
    ]
    specs = {} if inputs is None else {"in_specs": inputs}
    return pl.pallas_call(
        kernel,
        out_shape=shapes,
        scratch_shapes=list(scratch),
        compiler_params=pltpu.CompilerParams(vmem_limit_bytes=limit * MIB),
        cost_estimate=pl.CostEstimate(
            flops=flops or 0, bytes_accessed=0 if flops is None else 1 << 20, transcendentals=0
        ),
        name=name,
        input_output_aliases=aliases or {},
        **specs,
    )


def in_hbm(value):
    return pltpu.with_memory_space_constraint(value, pltpu.HBM)


def in_vmem(*values):
    return [pltpu.with_memory_space_constraint(value, pltpu.VMEM) for value in values]


def body(latents, in_weight, time_weight, mid_weight, up_weight):
    device_count = lax.axis_size("frames")
    bands = device_count // FRAMES
    offset = bands // 2
    band_of = lambda index: (index + offset) % bands
    frame_of = lambda index: (index + offset) // bands % FRAMES
    swap = lambda step, group, lowest: [
        pair
        for i in range(device_count)
        if group(i) % 2 == lowest and group(i) + 1 < (FRAMES if step == bands else bands)
        for j in [(i + step) % device_count]
        for pair in ((i, j), (j, i))
    ]
    inside, across = swap(1, band_of, 0), swap(1, band_of, 1)
    outer_frames, middle_frames = swap(bands, frame_of, 0), swap(bands, frame_of, 1)
    relayed_pairs = [(i, j) for i, j in outer_frames if abs(i - j) != bands and band_of(i) % 2 == 0]
    hops = [(i, i - offset + 1) for i, _ in relayed_pairs]
    relays = [(i - offset + 1, j) for i, j in relayed_pairs]
    outer_frames = [pair for pair in outer_frames if pair not in relayed_pairs]
    clips, rows, width, channels = latents.shape
    inner = mid_weight.shape[3]
    wide = clips * width
    depth = 3 * channels
    anywhere = pl.BlockSpec(memory_space=pl.ANY)
    whole = pl.BlockSpec(memory_space=pltpu.VMEM)
    turned = jnp.swapaxes(latents, 2, 3)

    inside_rim, across_rim, latent, in_rows = call(
        functools.partial(fetch_kernel, bands=bands),
        "fetch",
        [
            ((clips, channels, width), BF16),
            ((clips, channels, width), BF16),
            (turned.shape, BF16),
            ((3 * depth, channels), BF16),
        ],
        1,
        [pltpu.SemaphoreType.DMA((4,))],
        inputs=[anywhere, anywhere],
    )(in_hbm(turned), in_hbm(in_weight.reshape(3 * depth, channels)))
    inside_row = lax.ppermute(inside_rim, "frames", inside)
    across_row = lax.ppermute(across_rim, "frames", across)
    in_turned, field = call(
        prepare_kernel,
        "prepare",
        [((channels, 3 * depth), BF16), ((rows * depth, wide), BF16)],
        8,
        flops=2 * rows * wide * channels * wide,
        inputs=[whole] * 2,
    )(*in_vmem(latent, in_rows))
    (first,) = call(
        functools.partial(first_kernel, bands=bands),
        "first",
        [((rows, channels, wide), BF16)],
        8,
        [pltpu.VMEM((2 * depth, wide), BF16)],
        flops=2 * rows * wide * channels * 3 * depth,
        inputs=[whole] * 4,
    )(*in_vmem(inside_row, across_row, in_turned, field))
    of_half = lambda pairs, upper: [pair for pair in pairs if (band_of(pair[0]) < offset) == upper]
    lower_outer = lax.ppermute(first, "frames", of_half(outer_frames, False))
    lower_middle = lax.ppermute(first, "frames", of_half(middle_frames, False) + hops)
    upper_middle = lax.ppermute(first, "frames", of_half(middle_frames, True))
    upper_outer = lax.ppermute(first, "frames", of_half(outer_frames, True))
    time_rows, mid_rows, up_rows, first = lax.optimization_barrier(
        (
            time_weight.reshape(depth, channels),
            mid_weight.reshape(3 * depth, inner),
            jnp.swapaxes(up_weight, 2, 3),
            first,
        )
    )
    time_turned, part_turned, rest_turned, outer_turned, mid_turned, skip_weight, phase_weight = call(
        functools.partial(weights_kernel, bands=bands),
        "weights",
        [
            ((channels, depth), BF16),
            ((channels, 2 * channels), BF16),
            ((channels, channels), BF16),
            ((channels, channels), BF16),
            ((inner, 3 * depth), BF16),
            ((channels, 3 * depth), BF16),
            ((4, channels, 4 * inner), BF16),
        ],
        20,
        [
            pltpu.VMEM(time_rows.shape, BF16),
            pltpu.VMEM(mid_rows.shape, BF16),
            pltpu.VMEM(up_rows.shape, BF16),
            pltpu.SemaphoreType.DMA((2 + -(-3 * depth // 1024),)),
        ],
        flops=2 * 10**9,
        inputs=[anywhere] * 3,
    )(in_hbm(time_rows), in_hbm(mid_rows), in_hbm(up_rows))

    hopped, time_turned = lax.optimization_barrier((lower_middle, time_turned))
    relayed = lax.ppermute(hopped, "frames", relays)
    skip_shapes = [
        ((rows, channels, wide), BF16),
        ((2, channels, wide), BF16),
        ((2, channels, wide), BF16),
    ]
    skip, inside_rows, lower_rows = call(
        functools.partial(skip_lower_kernel, bands=bands),
        "skip_lower",
        skip_shapes,
        8,
        flops=2 * rows * wide * depth * channels,
        inputs=[whole] * 4,
    )(*in_vmem(first, lower_outer, lower_middle, time_turned))
    lower_across = lax.ppermute(lower_rows, "frames", of_half(across, False))
    (partial,) = call(
        functools.partial(skip_part_kernel, bands=bands),
        "skip_part",
        [((rows, channels, wide), F32)],
        8,
        flops=None,
        inputs=[whole] * 3,
    )(*in_vmem(first, upper_outer, part_turned))
    skip, inside_rows, upper_rows = call(
        functools.partial(skip_upper_kernel, bands=bands),
        "skip_upper",
        skip_shapes,
        8,
        flops=2 * rows * wide * channels * channels,
        inputs=[whole] * 7,
        aliases={5: 0, 6: 1},
    )(
        *in_vmem(
            partial, upper_middle, relayed, rest_turned, outer_turned, skip, inside_rows
        )
    )
    upper_across = lax.ppermute(upper_rows, "frames", of_half(across, True))
    from_inside = lax.ppermute(inside_rows, "frames", inside)

    mixed, middle = call(
        lambda *refs: own_kernel(*refs, half=width // 2),
        "own_rows",
        [((rows, channels, wide), F32), ((inner, 2 * wide), F32)],
        16,
        [pltpu.VMEM((rows * depth, wide), BF16), pltpu.VMEM((depth, wide), BF16)],
        flops=2 * wide * depth * (3 * inner + (3 * rows - 2) * channels),
        inputs=[whole] * 4,
    )(*in_vmem(skip, inside_rows, mid_turned, skip_weight))

    (out,) = call(
        functools.partial(last_kernel, bands=bands),
        "last",
        [(turned.shape, BF16)],
        20,
        [
            pltpu.VMEM((depth, wide), BF16),
            pltpu.VMEM((depth, wide), BF16),
            pltpu.VMEM((depth, wide), BF16),
            pltpu.VMEM((2 * depth, wide), BF16),
            pltpu.VMEM((4 * 3 * inner, wide // 2), BF16),
        ],
        flops=2 * wide * (3 * depth * inner + 2 * depth * channels + rows * 4 * inner * channels),
        kept=False,
        inputs=[whole] * 9,
    )(
        *in_vmem(
            mixed, middle, upper_across, lower_across, from_inside, mid_turned, skip_weight, phase_weight, field
        ),
    )
    return jnp.swapaxes(out, 2, 3)


def solution(mesh):
    in_specs = (P("groups", "frames", None, None), P(), P(), P(), P())
    out_specs = P("groups", "frames", None, None)
    return jax.shard_map(body, mesh=mesh, in_specs=in_specs, out_specs=out_specs, check_vma=False)
```

```python
import functools

import jax
import jax.numpy as jnp
from jax import lax
from jax.experimental import pallas as pl
from jax.experimental.pallas import tpu as pltpu
from jax.sharding import PartitionSpec as P


FRAMES = 4
BF16 = jnp.bfloat16
F32 = jnp.float32
MIB = 1024 * 1024


def place(bands):
    index = lax.axis_index("frames") + bands // 2
    return lax.rem(index, bands), lax.rem(lax.div(index, bands), FRAMES)


def dot(left, right):
    return jnp.dot(left, right, preferred_element_type=F32)


def silu(value):
    return value / (1.0 + jnp.exp(-value))


def sort_pick(width, clips):
    wide, half = width * clips, width // 2
    source = lax.broadcasted_iota(jnp.int32, (wide, wide), 0)
    lane = lax.broadcasted_iota(jnp.int32, (wide, wide), 1)
    parity, clip, j = lane // (wide // 2), lane // half % clips, lane % half
    return (source == clip * width + 2 * j + parity).astype(BF16)


def unsort_pick(width, clips):
    wide, half = width * clips, width // 2
    source = lax.broadcasted_iota(jnp.int32, (wide, wide), 0)
    lane = lax.broadcasted_iota(jnp.int32, (wide, wide), 1)
    clip, column = lane // width, lane % width
    return (source == column % 2 * (wide // 2) + clip * half + column // 2).astype(BF16)


def from_left(value, half):
    lane = lax.broadcasted_iota(jnp.int32, (1, value.shape[1]), 1)
    return jnp.where(lane % half == 0, 0.0, pltpu.roll(value, 1, 1))


def from_right(value, half):
    width = value.shape[1]
    lane = lax.broadcasted_iota(jnp.int32, (1, width), 1)
    return jnp.where(lane % half == half - 1, 0.0, pltpu.roll(value, width - 1, 1))


def store_taps(field, base, even, odd, half):
    channels, lanes = even.shape
    e, o = even.astype(BF16), odd.astype(BF16)
    blocks = ((from_left(odd, half).astype(BF16), e), (e, o), (o, from_right(even, half).astype(BF16)))
    for tap, pair in enumerate(blocks):
        rows = slice(base + tap * channels, base + (tap + 1) * channels)
        field[rows, :lanes] = pair[0]
        field[rows, lanes:] = pair[1]


def store_row_taps(field, base, lane_base, value, half):
    channels, lanes = value.shape
    blocks = (from_left(value, half).astype(BF16), value.astype(BF16), from_right(value, half).astype(BF16))
    for tap, block in enumerate(blocks):
        field[base + tap * channels : base + (tap + 1) * channels, lane_base : lane_base + lanes] = block


def fetch_kernel(
    latent_hbm, weight_hbm, inside_ref, across_ref, weight_ref, field_ref, latent, sems, *, bands
):
    clips, rows, channels, width = latent.shape
    odd = lax.rem(place(bands)[0], 2)
    pieces = [
        (latent_hbm, latent),
        (latent_hbm.at[:, (rows - 1) * odd], across_ref),
        (latent_hbm.at[:, (rows - 1) * (1 - odd)], inside_ref),
        (weight_hbm, weight_ref),
    ]
    gets = [
        pltpu.make_async_copy(source, target, sems.at[n])
        for n, (source, target) in enumerate(pieces)
    ]
    for get in gets:
        get.start()
    pick = sort_pick(width, clips)
    gets[0].wait()
    for row in range(rows):
        value = dot(jnp.concatenate([latent[clip, row] for clip in range(clips)], axis=1), pick)
        lanes = value.shape[1] // 2
        store_taps(field_ref, row * 3 * channels, value[:, :lanes], value[:, lanes:], width // 2)
    for get in gets[1:]:
        get.wait()


def prepare_kernel(weight_ref, turned_ref):
    turned_ref[...] = weight_ref[...].T


def first_kernel(inside_ref, across_ref, turned_ref, field_ref, first_ref, rim, *, bands):
    clips, channels, width = inside_ref.shape
    depth = 3 * channels
    rows = first_ref.shape[0]
    pick = sort_pick(width, clips)
    odd = lax.rem(place(bands)[0], 2) == 1
    for at in range(2):
        one, other = (inside_ref, across_ref) if at == 0 else (across_ref, inside_ref)
        blocks = [jnp.where(odd, one[clip], other[clip]) for clip in range(clips)]
        value = dot(jnp.concatenate(blocks, axis=1), pick)
        lanes = value.shape[1] // 2
        store_taps(rim, at * depth, value[:, :lanes], value[:, lanes:], width // 2)
    for row in list(range(1, rows - 1)) + [0, rows - 1]:
        start, stop = max(row - 1, 0), min(row + 2, rows)
        total = dot(
            turned_ref[:, (start - row + 1) * depth : (stop - row + 1) * depth],
            field_ref[start * depth : stop * depth, :],
        )
        if row == 0:
            total += dot(turned_ref[:, :depth], rim[:depth, :])
        if row == rows - 1:
            total += dot(turned_ref[:, 2 * depth :], rim[depth:, :])
        first_ref[row] = silu(total).astype(BF16)


def weights_kernel(
    time_hbm, mid_hbm, up_hbm, time_out, part_out, rest_out, outer_out, mid_out, skip_out, phase_out,
    time_rows, mid_rows, up_rows, sems, *, bands
):
    taps, inner = mid_rows.shape
    channels = up_rows.shape[2]
    cuts = list(range(0, taps, 1024)) + [taps]
    pieces = [(time_hbm, time_rows)]
    pieces += [(mid_hbm.at[a:b], mid_rows.at[a:b]) for a, b in zip(cuts, cuts[1:])]
    pieces += [(up_hbm, up_rows)]
    gets = [
        pltpu.make_async_copy(source, target, sems.at[n])
        for n, (source, target) in enumerate(pieces)
    ]
    for get in gets:
        get.start()
    gets[0].wait()
    time_out[...] = time_rows[...].T
    odd_frame = lax.rem(place(bands)[1], 2) == 1
    size = time_rows.shape[1]
    before, centre, after = [time_rows[at * size : (at + 1) * size, :] for at in range(3)]
    outer = jnp.where(odd_frame, before, after)
    part_out[...] = jnp.concatenate([centre, outer], axis=0).T
    rest_out[...] = jnp.where(odd_frame, after, before).T
    outer_out[...] = outer.T
    for get, a, b in zip(gets[1:-1], cuts, cuts[1:]):
        get.wait()
        mid_out[:, a:b] = mid_rows[a:b, :].T
    gets[-1].wait()
    skip_out[...] = jnp.concatenate(
        [up_rows[dr, dc, :, :channels] for dr in range(3) for dc in range(3)], axis=1
    )
    taps = [[up_rows[dr, dc, :, channels:].astype(F32) for dc in range(3)] for dr in range(3)]
    groups = ((lambda t: t[0], lambda t: t[1] + t[2]), (lambda t: t[0] + t[1], lambda t: t[2]))
    for row_phase in range(2):
        for row_tap in range(2):
            merged = [groups[row_phase][row_tap]([taps[dr][dc] for dr in range(3)]) for dc in range(3)]
            for column_phase in range(2):
                for column_tap in range(2):
                    value = groups[column_phase][column_tap](merged)
                    start = (2 * row_tap + column_tap) * inner
                    phase_out[2 * row_phase + column_phase, :, start : start + inner] = value.astype(
                        BF16
                    )


def share_skip(skips, skip_ref, inside_ref, across_ref, odd_band):
    lanes = skip_ref.shape[2] // 2
    for row, skip in enumerate(skips):
        skip_ref[row] = skip
    inside_ref[0] = jnp.where(odd_band, skips[0], skips[-1])
    across_ref[0] = jnp.where(odd_band, skips[-1], skips[0])
    for pooled_row in range(len(skips) // 2):
        sums = skips[2 * pooled_row].astype(F32) + skips[2 * pooled_row + 1].astype(F32)
        pooled = ((sums[:, :lanes] + sums[:, lanes:]) * 0.25).astype(BF16)
        span = slice(pooled_row * lanes, (pooled_row + 1) * lanes)
        inside_ref[1, :, span] = pooled
        across_ref[1, :, span] = pooled


def skip_lower_kernel(
    first_ref, outer_ref, middle_ref, weight_ref, skip_ref, inside_ref, across_ref, *, bands
):
    band, frame = place(bands)
    odd_frame = lax.rem(frame, 2) == 1
    is_host = jnp.logical_or(frame == 0, frame == FRAMES - 1)

    def middle(row):
        return jnp.where(is_host, jnp.zeros((), BF16), middle_ref[row])

    @pl.when(band >= bands // 2)
    def _():
        skips = []
        for row in range(first_ref.shape[0]):
            centre, outer, inner = first_ref[row], outer_ref[row], middle(row)
            before = jnp.where(odd_frame, outer, inner)
            after = jnp.where(odd_frame, inner, outer)
            stacked = jnp.concatenate([before, centre, after], axis=0)
            skips.append((centre.astype(F32) + dot(weight_ref[...], stacked)).astype(BF16))
        share_skip(skips, skip_ref, inside_ref, across_ref, lax.rem(band, 2) == 1)


def skip_part_kernel(first_ref, outer_ref, weight_ref, partial_ref, *, bands):
    @pl.when(place(bands)[0] < bands // 2)
    def _():
        for row in range(first_ref.shape[0]):
            centre = first_ref[row]
            stacked = jnp.concatenate([centre, outer_ref[row]], axis=0)
            partial_ref[row] = centre.astype(F32) + dot(weight_ref[...], stacked)


def skip_upper_kernel(
    partial_ref, middle_ref, relayed_ref, weight_ref, outer_weight, old_skip, old_inside,
    skip_ref, inside_ref, across_ref, *, bands
):
    band, frame = place(bands)
    upper = band < bands // 2
    is_relayed = jnp.logical_and(frame < 2, lax.rem(band, 2) == 0)

    def add(with_relayed):
        skips = []
        for row in range(partial_ref.shape[0]):
            total = partial_ref[row] + dot(weight_ref[...], middle_ref[row])
            if with_relayed:
                total += dot(outer_weight[...], relayed_ref[row])
            skips.append(total.astype(BF16))
        share_skip(skips, skip_ref, inside_ref, across_ref, lax.rem(band, 2) == 1)

    pl.when(jnp.logical_and(upper, is_relayed))(lambda: add(True))
    pl.when(jnp.logical_and(upper, jnp.logical_not(is_relayed)))(lambda: add(False))


def own_kernel(skip_ref, pair_ref, mid_ref, skip_weight, mixed_ref, middle_ref, field, pooled, *, half):
    rows, channels, wide = skip_ref.shape
    lanes = wide // 2
    depth = 3 * channels
    for at in range(2):
        row = pair_ref[1, :, at * lanes : (at + 1) * lanes].astype(F32)
        store_row_taps(pooled, 0, at * lanes, row, half)
    for row in range(rows):
        value = skip_ref[row].astype(F32)
        store_taps(field, row * depth, value[:, :lanes], value[:, lanes:], half)
    parts = [dot(mid_ref[:, dr * depth : (dr + 1) * depth], pooled[...]) for dr in range(3)]
    middle_ref[:, :lanes] = parts[2][:, :lanes]
    middle_ref[:, lanes : 2 * lanes] = parts[2][:, lanes:] + parts[1][:, :lanes]
    middle_ref[:, 2 * lanes : 3 * lanes] = parts[1][:, lanes:] + parts[0][:, :lanes]
    middle_ref[:, 3 * lanes :] = parts[0][:, lanes:]
    for row in range(rows):
        first, last = max(row - 1, 0), min(row + 2, rows)
        mixed_ref[row] = dot(
            skip_weight[:, (first - row + 1) * depth : (last - row + 1) * depth],
            field[first * depth : last * depth, :],
        )


def last_kernel(
    mixed_ref, middle_ref, upper_ref, lower_ref, inside_ref, mid_ref, skip_weight, phase_weight,
    field_ref, out_ref, low_field, high_field, cross_field, rims, middle_field, *, bands
):
    rows, channels, wide = mixed_ref.shape
    clips, _, _, width = out_ref.shape
    half, lanes = width // 2, wide // 2
    inner = mid_ref.shape[0]
    depth = 3 * channels

    band = place(bands)[0]
    odd = lax.rem(band, 2) == 1
    across = [lower_ref[at] + upper_ref[at] for at in range(2)]
    lows = [jnp.where(odd, inside_ref[at], across[at]) for at in range(2)]
    highs = [jnp.where(odd, across[at], inside_ref[at]) for at in range(2)]
    for target, pair, inward in ((low_field, lows[1], 1), (high_field, highs[1], 0)):
        for at in range(2):
            row = pair[:, at * lanes : (at + 1) * lanes].astype(F32)
            store_row_taps(target, 0, at * lanes, row, half)
        cross_field[:, (1 - inward) * lanes : (2 - inward) * lanes] = target[
            :, inward * lanes : (inward + 1) * lanes
        ]
    above = dot(mid_ref[:, :depth], low_field[...])
    cross = dot(mid_ref[:, depth : 2 * depth], cross_field[...])
    below = dot(mid_ref[:, 2 * depth :], high_field[...])
    middles = [
        middle_ref[:, :lanes] + above[:, :lanes] + cross[:, :lanes],
        middle_ref[:, lanes : 2 * lanes] + above[:, lanes:],
        middle_ref[:, 2 * lanes : 3 * lanes] + below[:, :lanes],
        middle_ref[:, 3 * lanes :] + below[:, lanes:] + cross[:, lanes:],
    ]
    kept = (band != 0, None, None, band != bands - 1)
    for at, (value, keep) in enumerate(zip(middles, kept)):
        value = silu(value)
        if keep is not None:
            value = jnp.where(keep, value, 0.0)
        store_row_taps(middle_field, at * 3 * inner, 0, value.astype(BF16).astype(F32), half)

    for at, row in enumerate((lows[0], highs[0])):
        value = row.astype(F32)
        store_taps(rims, at * depth, value[:, :lanes], value[:, lanes:], half)
    from_rim = {
        0: dot(skip_weight[:, :depth], rims[:depth, :]),
        rows - 1: dot(skip_weight[:, 2 * depth :], rims[depth:, :]),
    }
    unsort = unsort_pick(width, clips)
    block = 3 * inner
    for row_phase in range(2):
        phases = []
        for column_phase in range(2):
            start = column_phase * inner
            taps = [
                jnp.concatenate(
                    [
                        middle_field[
                            (row_phase + tap + at) * block + start : (row_phase + tap + at) * block
                            + start + 2 * inner,
                            :,
                        ]
                        for at in range(rows // 2)
                    ],
                    axis=1,
                )
                for tap in range(2)
            ]
            total = dot(phase_weight[2 * row_phase + column_phase], jnp.concatenate(taps, axis=0))
            phases.append(total)
        for at in range(rows // 2):
            row = 2 * at + row_phase
            latent = field_ref[row * depth + channels : row * depth + 2 * channels, :].astype(F32)
            upper = jnp.concatenate([phase[:, at * lanes : (at + 1) * lanes] for phase in phases], axis=1)
            total = latent + mixed_ref[row] + upper
            if row in from_rim:
                total += from_rim[row]
            natural = dot(total.astype(BF16), unsort).astype(BF16)
            for clip in range(clips):
                out_ref[clip, row] = natural[:, clip * width : (clip + 1) * width]


def call(kernel, name, outputs, limit, scratch=(), flops=0, kept=True, inputs=None, aliases=None):
    shapes = [
        pltpu.VMEM(shape, dtype) if kept else jax.ShapeDtypeStruct(shape, dtype)
        for shape, dtype in outputs
    ]
    specs = {} if inputs is None else {"in_specs": inputs}
    return pl.pallas_call(
        kernel,
        out_shape=shapes,
        scratch_shapes=list(scratch),
        compiler_params=pltpu.CompilerParams(vmem_limit_bytes=limit * MIB),
        cost_estimate=pl.CostEstimate(
            flops=flops or 0, bytes_accessed=0 if flops is None else 1 << 20, transcendentals=0
        ),
        name=name,
        input_output_aliases=aliases or {},
        **specs,
    )


def in_hbm(value):
    return pltpu.with_memory_space_constraint(value, pltpu.HBM)


def in_vmem(*values):
    return [pltpu.with_memory_space_constraint(value, pltpu.VMEM) for value in values]


def body(latents, in_weight, time_weight, mid_weight, up_weight):
    device_count = lax.axis_size("frames")
    bands = device_count // FRAMES
    offset = bands // 2
    band_of = lambda index: (index + offset) % bands
    frame_of = lambda index: (index + offset) // bands % FRAMES
    swap = lambda step, group, lowest: [
        pair
        for i in range(device_count)
        if group(i) % 2 == lowest and group(i) + 1 < (FRAMES if step == bands else bands)
        for j in [(i + step) % device_count]
        for pair in ((i, j), (j, i))
    ]
    inside, across = swap(1, band_of, 0), swap(1, band_of, 1)
    outer_frames, middle_frames = swap(bands, frame_of, 0), swap(bands, frame_of, 1)
    relayed_pairs = [(i, j) for i, j in outer_frames if abs(i - j) != bands and band_of(i) % 2 == 0]
    hops = [(i, i - offset + 1) for i, _ in relayed_pairs]
    relays = [(i - offset + 1, j) for i, j in relayed_pairs]
    outer_frames = [pair for pair in outer_frames if pair not in relayed_pairs]
    clips, rows, width, channels = latents.shape
    inner = mid_weight.shape[3]
    wide = clips * width
    depth = 3 * channels
    anywhere = pl.BlockSpec(memory_space=pl.ANY)
    whole = pl.BlockSpec(memory_space=pltpu.VMEM)
    turned = jnp.swapaxes(latents, 2, 3)

    inside_rim, across_rim, in_rows, field = call(
        functools.partial(fetch_kernel, bands=bands),
        "fetch",
        [
            ((clips, channels, width), BF16),
            ((clips, channels, width), BF16),
            ((3 * depth, channels), BF16),
            ((rows * depth, wide), BF16),
        ],
        8,
        [pltpu.VMEM(turned.shape, BF16), pltpu.SemaphoreType.DMA((4,))],
        inputs=[anywhere, anywhere],
    )(in_hbm(turned), in_hbm(in_weight.reshape(3 * depth, channels)))
    inside_row = lax.ppermute(inside_rim, "frames", inside)
    across_row = lax.ppermute(across_rim, "frames", across)
    (in_turned,) = call(
        prepare_kernel,
        "prepare",
        [((channels, 3 * depth), BF16)],
        8,
        flops=2 * rows * wide * channels * wide,
        inputs=[whole],
    )(*in_vmem(in_rows))
    (first,) = call(
        functools.partial(first_kernel, bands=bands),
        "first",
        [((rows, channels, wide), BF16)],
        8,
        [pltpu.VMEM((2 * depth, wide), BF16)],
        flops=2 * rows * wide * channels * 3 * depth,
        inputs=[whole] * 4,
    )(*in_vmem(inside_row, across_row, in_turned, field))
    of_half = lambda pairs, upper: [pair for pair in pairs if (band_of(pair[0]) < offset) == upper]
    lower_outer = lax.ppermute(first, "frames", of_half(outer_frames, False))
    lower_middle = lax.ppermute(first, "frames", of_half(middle_frames, False) + hops)
    upper_middle = lax.ppermute(first, "frames", of_half(middle_frames, True))
    upper_outer = lax.ppermute(first, "frames", of_half(outer_frames, True))
    time_rows, mid_rows, up_rows, first = lax.optimization_barrier(
        (
            time_weight.reshape(depth, channels),
            mid_weight.reshape(3 * depth, inner),
            jnp.swapaxes(up_weight, 2, 3),
            first,
        )
    )
    time_turned, part_turned, rest_turned, outer_turned, mid_turned, skip_weight, phase_weight = call(
        functools.partial(weights_kernel, bands=bands),
        "weights",
        [
            ((channels, depth), BF16),
            ((channels, 2 * channels), BF16),
            ((channels, channels), BF16),
            ((channels, channels), BF16),
            ((inner, 3 * depth), BF16),
            ((channels, 3 * depth), BF16),
            ((4, channels, 4 * inner), BF16),
        ],
        20,
        [
            pltpu.VMEM(time_rows.shape, BF16),
            pltpu.VMEM(mid_rows.shape, BF16),
            pltpu.VMEM(up_rows.shape, BF16),
            pltpu.SemaphoreType.DMA((2 + -(-3 * depth // 1024),)),
        ],
        flops=2 * 10**9,
        inputs=[anywhere] * 3,
    )(in_hbm(time_rows), in_hbm(mid_rows), in_hbm(up_rows))

    hopped, time_turned = lax.optimization_barrier((lower_middle, time_turned))
    relayed = lax.ppermute(hopped, "frames", relays)
    skip_shapes = [
        ((rows, channels, wide), BF16),
        ((2, channels, wide), BF16),
        ((2, channels, wide), BF16),
    ]
    skip, inside_rows, lower_rows = call(
        functools.partial(skip_lower_kernel, bands=bands),
        "skip_lower",
        skip_shapes,
        8,
        flops=2 * rows * wide * depth * channels,
        inputs=[whole] * 4,
    )(*in_vmem(first, lower_outer, lower_middle, time_turned))
    lower_across = lax.ppermute(lower_rows, "frames", of_half(across, False))
    (partial,) = call(
        functools.partial(skip_part_kernel, bands=bands),
        "skip_part",
        [((rows, channels, wide), F32)],
        8,
        flops=None,
        inputs=[whole] * 3,
    )(*in_vmem(first, upper_outer, part_turned))
    skip, inside_rows, upper_rows = call(
        functools.partial(skip_upper_kernel, bands=bands),
        "skip_upper",
        skip_shapes,
        8,
        flops=2 * rows * wide * channels * channels,
        inputs=[whole] * 7,
        aliases={5: 0, 6: 1},
    )(
        *in_vmem(
            partial, upper_middle, relayed, rest_turned, outer_turned, skip, inside_rows
        )
    )
    upper_across = lax.ppermute(upper_rows, "frames", of_half(across, True))
    from_inside = lax.ppermute(inside_rows, "frames", inside)

    mixed, middle = call(
        lambda *refs: own_kernel(*refs, half=width // 2),
        "own_rows",
        [((rows, channels, wide), F32), ((inner, 2 * wide), F32)],
        16,
        [pltpu.VMEM((rows * depth, wide), BF16), pltpu.VMEM((depth, wide), BF16)],
        flops=2 * wide * depth * (3 * inner + (3 * rows - 2) * channels),
        inputs=[whole] * 4,
    )(*in_vmem(skip, inside_rows, mid_turned, skip_weight))

    (out,) = call(
        functools.partial(last_kernel, bands=bands),
        "last",
        [(turned.shape, BF16)],
        20,
        [
            pltpu.VMEM((depth, wide), BF16),
            pltpu.VMEM((depth, wide), BF16),
            pltpu.VMEM((depth, wide), BF16),
            pltpu.VMEM((2 * depth, wide), BF16),
            pltpu.VMEM((4 * 3 * inner, wide // 2), BF16),
        ],
        flops=2 * wide * (3 * depth * inner + 2 * depth * channels + rows * 4 * inner * channels),
        kept=False,
        inputs=[whole] * 9,
    )(
        *in_vmem(
            mixed, middle, upper_across, lower_across, from_inside, mid_turned, skip_weight, phase_weight, field
        ),
    )
    return jnp.swapaxes(out, 2, 3)


def solution(mesh):
    in_specs = (P("groups", "frames", None, None), P(), P(), P(), P())
    out_specs = P("groups", "frames", None, None)
    return jax.shard_map(body, mesh=mesh, in_specs=in_specs, out_specs=out_specs, check_vma=False)
```
